128 devices in a mesh: rep: 2 (over x_hi), ctx: 32 (over z, x_lo, y), head: 2 (over core).
Axes of the slice: x: 4 (x_hi: 2, x_lo: 2; x = x_hi * 2 + x_lo), y: 4, z: 4, core: 2. Of those that a mesh axis runs over, the one named last changes fastest.
Arguments:
- tokens: bfloat16 [2, 6144, 1024], P('rep', 'ctx'), may hold values from -6 to 6
- segments: int32 [2, 6144], P('rep', 'ctx'), may hold values from 0 to 2, as said below
- positions: int32 [2, 6144], P('rep', 'ctx'), may hold values from 0 to 5951, as said below
- cotangent: bfloat16 [2, 6144, 1024], P('rep', 'ctx'), may hold values from -6 to 6
- query_weight: bfloat16 [1024, 2048], P('ctx', 'head'), may hold values from -0.1875 to 0.1875
- key_weight: bfloat16 [1024, 1024], P('ctx', 'head'), may hold values from -0.1875 to 0.1875
- value_weight: bfloat16 [1024, 1024], P('ctx', 'head'), may hold values from -0.1875 to 0.1875
- out_weight: bfloat16 [2048, 1024], P('head', 'ctx'), may hold values from -4 to 4
- attn_gain: bfloat16 [1024], P('ctx'), may hold values from 0.5 to 1.5
- query_gain: bfloat16 [128], replicated, may hold values from 0.5 to 1.5
- key_gain: bfloat16 [128], replicated, may hold values from 0.5 to 1.5
- gate_weight: bfloat16 [1024, 3072], P('ctx', 'head'), may hold values from -0.1875 to 0.1875
- up_weight: bfloat16 [1024, 3072], P('ctx', 'head'), may hold values from -0.1875 to 0.1875
- down_weight: bfloat16 [3072, 1024], P('head', 'ctx'), may hold values from -0.109375 to 0.109375
- mlp_gain: bfloat16 [1024], P('ctx'), may hold values from 0.5 to 1.5
Outputs:
- result: bfloat16 [2, 6144, 1024], P('rep', 'ctx')
- input_grad: bfloat16 [2, 6144, 1024], P('rep', 'ctx')
- grad_query_weight: float32 [1024, 2048], P('ctx', 'head')
- grad_key_weight: float32 [1024, 1024], P('ctx', 'head')
- grad_value_weight: float32 [1024, 1024], P('ctx', 'head')
- grad_out_weight: float32 [2048, 1024], P('head', 'ctx')
- grad_attn_gain: float32 [1024], P('ctx')
- grad_query_gain: float32 [128], replicated
- grad_key_gain: float32 [128], replicated
- grad_gate_weight: float32 [1024, 3072], P('ctx', 'head')
- grad_up_weight: float32 [1024, 3072], P('ctx', 'head')
- grad_down_weight: float32 [3072, 1024], P('head', 'ctx')
- grad_mlp_gain: float32 [1024], P('ctx')
The draws below stay inside these ranges and needn't reach their ends.
Inputs may be any that keep to these rules, and one draw needn't show every extreme that they name: `segments`: segment numbers never fall along a sequence. Document 0 holds the first tokens, 1 to 191 of them; document 1 follows with exactly 5952 tokens; document 2 holds the rest, at least one token. `positions`: each token's position within its document: 0 at a document's first token, rising by one per token.
All inputs are finite; a program needn't handle non-finite values.
Results may differ from the reference program's by a relative error of at most 0.03.
Values may be sent and summed in bfloat16 or wider, within the bound.
A program may use at most 192 MiB of HBM per device.

```python
import math
import jax
import jax.numpy as jnp
from jax import lax

D = 1024
HEAD_DIM = 128
FF = 3072
TOK_DEV = 192
QDIM = 2048
KVDIM = 1024
LENGTH = 6144
SEQS = 2


def document_layout(key):
    starts = jax.random.randint(jax.random.fold_in(key, 101), (SEQS,), 1, TOK_DEV, dtype=jnp.int32)
    endings = starts + (LENGTH - TOK_DEV)
    index_row = jnp.arange(LENGTH, dtype=jnp.int32)[None, :]
    doc_ids = (index_row >= starts[:, None]).astype(jnp.int32) + (index_row >= endings[:, None]).astype(jnp.int32)
    doc_start = jnp.where(doc_ids == 0, 0, jnp.where(doc_ids == 1, starts[:, None], endings[:, None]))
    return (doc_ids, (index_row - doc_start).astype(jnp.int32))


def draw_segments(key, part):
    doc_ids, places = document_layout(key)
    return doc_ids


def draw_positions(key, part):
    doc_ids, places = document_layout(key)
    return places


def block_levels(own_key, extent, cuts, low, high):
    level = 1.0
    for dim, parts in cuts:
        heights = jax.random.uniform(jax.random.fold_in(jax.random.fold_in(own_key, 6), dim), (parts,), jnp.float32, low / len(cuts), high / len(cuts))
        level = level * jnp.repeat(jnp.exp(heights), extent[dim] // parts).reshape((-1,) + (1,) * (len(extent) - 1 - dim))
    return level


def gaussian(key, shape, deviation, limit, shards=(), kind=jnp.bfloat16):
    result = deviation * jax.random.normal(key, shape, jnp.float32)
    if shards:
        result = result * block_levels(key, shape, shards, -0.22, 0.18)
    return jnp.clip(result, -limit, limit).astype(kind)


def setup_inputs(seed: int = 0) -> dict:
    splits = jax.random.split(jax.random.key(seed), 16)
    tokens = gaussian(splits[0], (SEQS, LENGTH, D), 1.0, 6.0, ((0, 2), (1, 32)))
    segments = draw_segments(jax.random.fold_in(splits[15], 71), 0)
    positions = draw_positions(jax.random.fold_in(splits[15], 71), 0)
    cotangent = gaussian(splits[3], (SEQS, LENGTH, D), 1.0, 6.0, ((0, 2), (1, 32)))
    query_weight = gaussian(splits[4], (D, QDIM), D ** -0.5, 0.1875, ((0, 32), (1, 2)))
    key_weight = gaussian(splits[5], (D, KVDIM), D ** -0.5, 0.1875, ((0, 32), (1, 2)))
    value_weight = gaussian(splits[6], (D, KVDIM), D ** -0.5, 0.1875, ((0, 32), (1, 2)))
    out_weight = gaussian(splits[7], (QDIM, D), 2 ** -0.5, 4.0, ((0, 2), (1, 32)))
    attn_gain = jnp.clip(1.0 + 0.1 * jax.random.normal(splits[8], (D,), jnp.float32), 0.5, 1.5).astype(jnp.bfloat16)
    query_gain = jnp.clip(1.0 + 0.1 * jax.random.normal(splits[9], (HEAD_DIM,), jnp.float32), 0.5, 1.5).astype(jnp.bfloat16)
    key_gain = jnp.clip(1.0 + 0.1 * jax.random.normal(splits[10], (HEAD_DIM,), jnp.float32), 0.5, 1.5).astype(jnp.bfloat16)
    gate_weight = gaussian(splits[11], (D, FF), D ** -0.5, 0.1875, ((0, 32), (1, 2)))
    up_weight = gaussian(splits[12], (D, FF), D ** -0.5, 0.1875, ((0, 32), (1, 2)))
    down_weight = gaussian(splits[13], (FF, D), FF ** -0.5, 0.109375, ((0, 2), (1, 32)))
    mlp_gain = jnp.clip(1.0 + 0.1 * jax.random.normal(splits[14], (D,), jnp.float32), 0.5, 1.5).astype(jnp.bfloat16)
    return dict(tokens=tokens, segments=segments, positions=positions, cotangent=cotangent, query_weight=query_weight, key_weight=key_weight, value_weight=value_weight, out_weight=out_weight, attn_gain=attn_gain, query_gain=query_gain, key_gain=key_gain, gate_weight=gate_weight, up_weight=up_weight, down_weight=down_weight, mlp_gain=mlp_gain)


EPSILON = 1e-06
ROPE_BASE = 1000000.0
PRECISE = lax.Precision.HIGHEST
MASKED_SCORE = -1e+30

@jax.custom_vjp
def low(v):
    return lax.optimization_barrier(v.astype(jnp.bfloat16)).astype(jnp.float32)

@jax.custom_vjp
def low_back(v):
    return v

def low_keep(v):
    return (low(v), None)

def low_pass(kept, grad):
    return (grad,)

def back_keep(v):
    return (v, None)

def back_low(kept, grad):
    return (low(grad),)
low.defvjp(low_keep, low_pass)
low_back.defvjp(back_keep, back_low)

def rms_scale(values, gain):
    return values * lax.rsqrt(lax.optimization_barrier(jnp.mean(values * values, axis=-1, keepdims=True)) + EPSILON) * gain

def rotate(values, places):
    half_dim = values.shape[-1] // 2
    inverse = ROPE_BASE ** (-jnp.arange(half_dim, dtype=jnp.float32) / half_dim)
    angles = places.astype(jnp.float32)[:, None] * inverse[None, :]
    cosine = jnp.cos(angles)[:, None, :]
    sine_part = jnp.sin(angles)[:, None, :]
    first_half = values[..., :half_dim]
    second_half = values[..., half_dim:]
    return jnp.concatenate([first_half * cosine - second_half * sine_part, second_half * cosine + first_half * sine_part], axis=-1)

def dense(left, right):
    return jnp.dot(left, right, precision=PRECISE)

def attend(query_heads, key_heads, value_heads, doc_ids):
    seq_length, head_count, head_size = query_heads.shape
    key_groups = key_heads.shape[1]
    group_size = head_count // key_groups
    block_size = math.gcd(seq_length, 512)
    block_count = seq_length // block_size
    factor = 1.0 / math.sqrt(head_size)
    grouped = query_heads.reshape(block_count, block_size, key_groups, group_size, head_size)
    block_starts = jnp.arange(block_count, dtype=jnp.int32) * block_size
    doc_blocks = doc_ids.reshape(block_count, block_size)
    key_index = jnp.arange(seq_length, dtype=jnp.int32)

    def one_block(block_entry):
        query_block, block_start, doc_block = block_entry
        scores = jnp.einsum('qgrd,kgd->grqk', query_block, key_heads, precision=PRECISE) * factor
        scores = low_back(scores)
        query_index = block_start + jnp.arange(block_size, dtype=jnp.int32)
        allowed = (key_index[None, :] <= query_index[:, None]) & (doc_block[:, None] == doc_ids[None, :])
        scores = jnp.where(allowed, scores, MASKED_SCORE)
        weights = low(jax.nn.softmax(scores, axis=-1))
        return jnp.einsum('grqk,kgd->qgrd', weights, value_heads, precision=PRECISE)
    mixed_heads = lax.map(jax.checkpoint(one_block), (grouped, block_starts, doc_blocks))
    return mixed_heads.reshape(seq_length, head_count * head_size)

def layer(inputs, doc_ids, places, query_weight, key_weight, value_weight, out_weight, attn_gain, query_gain, key_gain, gate_weight, up_weight, down_weight, mlp_gain):
    seq_length = inputs.shape[0]
    head_size = query_gain.shape[0]
    normed = low(rms_scale(inputs, attn_gain))
    query_pre = low_back(dense(normed, query_weight)).reshape(seq_length, -1, head_size)
    key_pre = low_back(dense(normed, key_weight)).reshape(seq_length, -1, head_size)
    value_heads = low(low_back(dense(normed, value_weight))).reshape(seq_length, -1, head_size)
    query_heads = low(rotate(rms_scale(query_pre, query_gain), places))
    key_heads = low(rotate(rms_scale(key_pre, key_gain), places))
    attended = low(low_back(attend(query_heads, key_heads, value_heads, doc_ids)))
    hidden_in = inputs + low_back(dense(attended, out_weight))
    normed_two = low(rms_scale(hidden_in, mlp_gain))
    gate_pre = low_back(dense(normed_two, gate_weight))
    up_pre = low_back(dense(normed_two, up_weight))
    activated = low(jax.nn.silu(gate_pre) * up_pre)
    return hidden_in + low_back(dense(activated, down_weight))

def reference(tokens, segments, positions, cotangent, query_weight, key_weight, value_weight, out_weight, attn_gain, query_gain, key_gain, gate_weight, up_weight, down_weight, mlp_gain):
    params = tuple((weight.astype(jnp.float32) for weight in (query_weight, key_weight, value_weight, out_weight, attn_gain, query_gain, key_gain, gate_weight, up_weight, down_weight, mlp_gain)))

    def one_sequence(totals, element):
        sequence, doc_ids, places, grad_result = element

        def forward(token_rows, *weights):
            return layer(token_rows, doc_ids, places, *weights)
        output, pull_back = jax.vjp(forward, sequence.astype(jnp.float32), *params)
        gradients = pull_back(grad_result.astype(jnp.float32))
        totals = tuple((running + addend for running, addend in zip(totals, gradients[1:])))
        return (totals, (output.astype(jnp.bfloat16), gradients[0].astype(jnp.bfloat16)))
    initial = tuple((jnp.zeros_like(weight) for weight in params))
    totals, (outputs, input_grads) = lax.scan(one_sequence, initial, (tokens, segments, positions, cotangent))
    return (outputs, input_grads, totals[0], totals[1], totals[2], totals[3], totals[4], totals[5], totals[6], totals[7], totals[8], totals[9], totals[10])
```

```python
import math

import jax
import jax.numpy as jnp
from jax import lax
from jax.experimental import pallas as pl
from jax.experimental.pallas import tpu as pltpu
from jax.sharding import Mesh
from jax.sharding import PartitionSpec as P

MESH = pl.DeviceIdType.MESH
CTX = ("ctx_0", "ctx_1", "ctx_2")
EPSILON = 1e-06
ROPE_BASE = 1000000.0
BF = jnp.bfloat16
F32 = jnp.float32
HD = 128
D = 1024
CH = 192
HALF = 96
MIDDLE = 5952
W1C = 512
W2C = 1408
SCALE = 1.0 / math.sqrt(HD)
SCALE2 = SCALE / math.log(2.0)
VMEM_LIMIT = 56 * 1024 * 1024
PLANE = ((0, 1), (0, 3), (1, 0), (1, 1), (1, 3), (0, 2), (1, 2))
RING = (1, 3, 2)


def nn(a, b):
    return jnp.dot(a, b, preferred_element_type=F32)


def nt(a, b):
    return lax.dot_general(a, b, (((1,), (1,)), ((), ())), preferred_element_type=F32)


def tn(a, b):
    return lax.dot_general(a, b, (((0,), (0,)), ((), ())), preferred_element_type=F32)


def rcopy(src, dst, send, recv, device):
    return pltpu.make_async_remote_copy(
        src_ref=src, dst_ref=dst, send_sem=send, recv_sem=recv, device_id=device, device_id_type=MESH
    )


def place():
    return tuple(lax.axis_index(name) for name in ("ctx_0", "ctx_1", "ctx_2", "head"))


def ring_peer(z, k):
    return {"ctx_0": lax.rem(z + k, 4)}


def plane_peer(x, y, dx, dy):
    return {"ctx_1": lax.rem(x + dx, 2), "ctx_2": lax.rem(y + dy, 4)}


def greet(devices):
    barrier = pltpu.get_barrier_semaphore()
    for device in devices:
        pl.semaphore_signal(barrier, inc=1, device_id=device, device_id_type=MESH)
    pl.semaphore_wait(barrier, len(devices))


def group_devices(z, h):
    return [{"head": 1 - h}] + [ring_peer(z, k) for k in RING]


def plane_devices(x, y):
    return [plane_peer(x, y, dx, dy) for dx, dy in PLANE]


class Gather:
    def __init__(self, own, buf, z, h, sems):
        self.buf, self.z, self.h = buf, z, h
        self.sz, self.rz, self.ss, self.rs = sems
        self.sent = []
        self.from_core = {}
        self.ring = {}
        for k in RING:
            copy = rcopy(own, buf.at[z, h], self.sz.at[k], self.rz.at[k], ring_peer(z, k))
            copy.start()
            self.ring[k] = copy
            self.sent.append(copy)

    def to_core(self, k):
        source = lax.rem(self.z + 4 - k, 4)
        slot = self.buf.at[source, self.h]
        copy = rcopy(slot, slot, self.ss.at[k], self.rs.at[k], {"head": 1 - self.h})
        copy.start()
        self.from_core[k] = copy
        self.sent.append(copy)

    def forward(self, k):
        self.ring[k].wait_recv()
        self.to_core(k)

    def arrived(self, k):
        self.from_core[k].wait_recv()

    def finish(self):
        for copy in self.sent:
            copy.wait_send()


class Reduce:
    def __init__(self, parts, other, sums, inbox, z, h, sems):
        self.parts, self.other, self.sums, self.inbox, self.z, self.h = parts, other, sums, inbox, z, h
        self.ss, self.rs, self.sz, self.rz = sems
        self.sent = []
        self.core = {}
        self.ring = {}

    def give(self, k, value):
        chunk = lax.rem(self.z + k, 4)
        self.parts[chunk] = value.astype(BF).reshape(2, HALF, D)
        copy = rcopy(
            self.parts.at[chunk, 1 - self.h],
            self.other.at[chunk],
            self.ss.at[k],
            self.rs.at[k],
            {"head": 1 - self.h},
        )
        copy.start()
        self.core[k] = copy
        self.sent.append(copy)

    def pass_on(self, k):
        chunk = lax.rem(self.z + k, 4)
        self.core[k].wait_recv()
        both = self.parts[chunk, self.h].astype(F32) + self.other[chunk].astype(F32)
        self.sums[chunk] = both.astype(BF)
        copy = rcopy(
            self.sums.at[chunk],
            self.inbox.at[self.z],
            self.sz.at[k],
            self.rz.at[k],
            ring_peer(self.z, k),
        )
        copy.start()
        self.ring[k] = copy
        self.sent.append(copy)

    def total(self):
        self.core[0].wait_recv()
        result = self.parts[self.z, self.h].astype(F32) + self.other[self.z].astype(F32)
        for k in RING:
            self.ring[k].wait_recv()
            result += self.inbox[lax.rem(self.z + 4 - k, 4)].astype(F32)
        return result

    def finish(self):
        for copy in self.sent:
            copy.wait_send()


def reduce_scratch():
    return [
        pltpu.VMEM((4, 2, HALF, D), BF),
        pltpu.VMEM((4, HALF, D), BF),
        pltpu.VMEM((4, HALF, D), BF),
        pltpu.VMEM((4, HALF, D), BF),
    ] + [pltpu.SemaphoreType.DMA((4,))] * 4


def gather_scratch():
    return [pltpu.SemaphoreType.DMA((4,))] * 4


def spread_kernel(
    tok, cot, w1, w2, gains, tok_all, cot_all, w1_all, w2_ring, gains_all,
    w1_ring, gains_ring, local, ring_send, ring_recv, plane_send, plane_recv,
    ts0, ts1, ts2, ts3, cs0, cs1, cs2, cs3,
):
    z, x, y, h = place()
    t = x * 4 + y
    greet(group_devices(z, h) + plane_devices(x, y))
    locals_ = [
        pltpu.make_async_copy(w1.at[z], w1_ring.at[z], local.at[0]),
        pltpu.make_async_copy(gains, gains_ring.at[z], local.at[1]),
        pltpu.make_async_copy(w2.at[z], w2_ring.at[z], local.at[2]),
        pltpu.make_async_copy(tok, tok_all.at[z], local.at[3]),
        pltpu.make_async_copy(cot, cot_all.at[z], local.at[4]),
    ]
    for copy in locals_:
        copy.start()
    sent = []
    ring = []
    for k in RING:
        peer = lax.rem(z + k, 4)
        pair = [
            rcopy(w1.at[peer], w1_ring.at[z], ring_send.at[0, k], ring_recv.at[0, k], ring_peer(z, k)),
            rcopy(gains, gains_ring.at[z], ring_send.at[1, k], ring_recv.at[1, k], ring_peer(z, k)),
        ]
        for copy in pair:
            copy.start()
        ring += pair
    tokens_out = Gather(tok.at[h], tok_all, z, h, (ts0, ts1, ts2, ts3))
    locals_[0].wait()
    locals_[1].wait()
    for copy in ring:
        copy.wait_recv()
    plane = []
    for n, (dx, dy) in enumerate(PLANE):
        device = plane_peer(x, y, dx, dy)
        pair = [
            rcopy(w1_ring, w1_all.at[:, t], plane_send.at[0, n], plane_recv.at[0, n], device),
            rcopy(gains_ring, gains_all.at[:, t], plane_send.at[1, n], plane_recv.at[1, n], device),
        ]
        for copy in pair:
            copy.start()
        plane += pair
    keep = [
        pltpu.make_async_copy(w1_ring, w1_all.at[:, t], local.at[5]),
        pltpu.make_async_copy(gains_ring, gains_all.at[:, t], local.at[6]),
    ]
    for copy in keep:
        copy.start()
    second = []
    for k in RING:
        peer = lax.rem(z + k, 4)
        copy = rcopy(w2.at[peer], w2_ring.at[z], ring_send.at[2, k], ring_recv.at[2, k], ring_peer(z, k))
        copy.start()
        second.append(copy)
    cot_out = Gather(cot.at[h], cot_all, z, h, (cs0, cs1, cs2, cs3))
    for k in RING:
        tokens_out.forward(k)
    for k in RING:
        cot_out.forward(k)
    for k in RING:
        tokens_out.arrived(k)
        cot_out.arrived(k)
    for copy in ring + plane + second:
        copy.wait_send()
    for copy in plane + second:
        copy.wait_recv()
    tokens_out.finish()
    cot_out.finish()
    for copy in locals_[2:] + keep:
        copy.wait()


def spread(tok, cot, w1, w2, gains):
    any_ = pl.BlockSpec(memory_space=pl.ANY)
    return pl.pallas_call(
        spread_kernel,
        out_shape=(
            jax.ShapeDtypeStruct((4, 2, HALF, D), BF),
            jax.ShapeDtypeStruct((4, 2, HALF, D), BF),
            jax.ShapeDtypeStruct((4, 8, 32, W1C), BF),
            jax.ShapeDtypeStruct((4, 32, W2C), BF),
            jax.ShapeDtypeStruct((4, 8, 8, 128), F32),
        ),
        in_specs=[any_] * 5,
        out_specs=(any_,) * 5,
        scratch_shapes=[
            pltpu.VMEM((4, 32, W1C), BF),
            pltpu.VMEM((4, 8, 128), F32),
            pltpu.SemaphoreType.DMA((7,)),
            pltpu.SemaphoreType.DMA((3, 4)),
            pltpu.SemaphoreType.DMA((3, 4)),
            pltpu.SemaphoreType.DMA((2, 7)),
            pltpu.SemaphoreType.DMA((2, 7)),
        ]
        + gather_scratch()
        + gather_scratch(),
        compiler_params=pltpu.CompilerParams(
            collective_id=0, has_side_effects=True, vmem_limit_bytes=VMEM_LIMIT
        ),
        name="spread",
    )(tok, cot, w1, w2, gains)


def turn(u, cosine, sine):
    return u * cosine + pltpu.roll(u, HD // 2, 1) * sine


def rms_rate(v):
    return lax.rsqrt(jnp.mean(v * v, axis=-1, keepdims=True) + EPSILON)


def heads_kernel(tok, w1, gain, qgain, kgain, cosine, sine, q, kv, pre, normed):
    v = tok[...].astype(F32)
    n = (v * rms_rate(v) * gain[...]).astype(BF)
    normed[...] = n
    out = nn(n, w1[...])
    pre[...] = out[:, :384]
    c, s = cosine[...], sine[...]
    for i in range(3):
        u = out[:, i * HD : (i + 1) * HD]
        u = turn(u * rms_rate(u) * (qgain if i < 2 else kgain)[...], c, s).astype(BF)
        if i < 2:
            q[0, i * CH : (i + 1) * CH, :] = u
        else:
            kv[0, :, :HD] = u
    kv[0, :, HD:] = out[:, 384:].astype(BF)


def make_heads(tok_all, w1, gain, qgain, kgain, cosine, sine):
    def whole(*shape):
        return pl.BlockSpec(shape, lambda i: (0,) * len(shape))

    return pl.pallas_call(
        heads_kernel,
        grid=(4,),
        out_shape=(
            jax.ShapeDtypeStruct((4, 2 * CH, HD), BF),
            jax.ShapeDtypeStruct((4, CH, 2 * HD), BF),
            jax.ShapeDtypeStruct((4 * CH, 384), F32),
            jax.ShapeDtypeStruct((4 * CH, D), BF),
        ),
        in_specs=[
            pl.BlockSpec((CH, D), lambda i: (i, 0)),
            whole(D, W1C),
            whole(1, D),
            whole(1, HD),
            whole(1, HD),
            pl.BlockSpec((CH, HD), lambda i: (i, 0)),
            pl.BlockSpec((CH, HD), lambda i: (i, 0)),
        ],
        out_specs=(
            pl.BlockSpec((1, 2 * CH, HD), lambda i: (i, 0, 0)),
            pl.BlockSpec((1, CH, 2 * HD), lambda i: (i, 0, 0)),
            pl.BlockSpec((CH, 384), lambda i: (i, 0)),
            pl.BlockSpec((CH, D), lambda i: (i, 0)),
        ),
        compiler_params=pltpu.CompilerParams(vmem_limit_bytes=VMEM_LIMIT),
        name="make_heads",
    )(tok_all, w1, gain, qgain, kgain, cosine, sine)


def query_index(chunk):
    lane = lax.broadcasted_iota(jnp.int32, (1, 2 * CH), 1)
    return chunk * CH + jnp.where(lane < CH, lane, lane - CH)


def first_allowed(index, start):
    return jnp.where(index < start, 0, jnp.where(index < start + MIDDLE, start, start + MIDDLE))


def key_index(chunk):
    return chunk * CH + lax.broadcasted_iota(jnp.int32, (CH, 1), 0)


def row_sums(p):
    return jnp.sum(p.reshape(CH // 8, 8, 2 * CH), axis=0)


def attend_kernel(
    q, kv, w2_ring, start_ref, att, out_t, logs, kv_all, w2_all, acc, den,
    local, kv_send, kv_recv, w_send, w_recv,
):
    z, x, y, h = place()
    t = x * 4 + y
    greet(plane_devices(x, y))
    copies = []
    weights = []
    for n, (dx, dy) in enumerate(PLANE):
        copy = rcopy(kv, kv_all.at[:, t], kv_send.at[n], kv_recv.at[n], plane_peer(x, y, dx, dy))
        copy.start()
        copies.append(copy)
    for n, (dx, dy) in enumerate(PLANE):
        copy = rcopy(w2_ring, w2_all.at[:, t], w_send.at[n], w_recv.at[n], plane_peer(x, y, dx, dy))
        copy.start()
        weights.append(copy)
    keep = pltpu.make_async_copy(w2_ring, w2_all.at[:, t], local.at[0])
    keep.start()
    kv_all[:, t] = kv[...]
    start = start_ref[0, 0]
    for copy in copies:
        copy.wait_recv()

    def block(j, qc):
        k, v = kv_all[j // 8, lax.rem(j, 8), :, :HD], kv_all[j // 8, lax.rem(j, 8), :, HD:]
        return jnp.exp2(nt(k, qc) * SCALE2), v

    for c in range(4):
        qc = q[c]
        mine = c * 8 + t
        index = query_index(mine)
        lowest = first_allowed(index, start)
        acc[...] = jnp.zeros_like(acc)
        den[...] = jnp.zeros_like(den)

        def several(first, count):
            a, d = None, None
            for u in range(count):
                p, v = block(first + u, qc)
                dd = row_sums(p)
                aa = tn(v, p.astype(BF))
                a = aa if a is None else a + aa
                d = dd if d is None else d + dd
            acc[...] += a
            den[...] += d

        plain = lax.max(mine - 1, 0)
        fours = plain // 4

        @pl.loop(0, fours)
        def _(i):
            several(1 + 4 * i, 4)

        @pl.loop(1 + 4 * fours, 1 + plain)
        def _(j):
            several(j, 1)

        inside = (index < start + MIDDLE).astype(F32)
        total = acc[...] * inside
        denominator = jnp.sum(den[...], axis=0, keepdims=True) * inside
        last = key_index(mine)
        p, v = block(mine, qc)
        p = jnp.where((last <= index) & (last >= lowest), p, 0.0)
        total += tn(v, p.astype(BF))
        denominator += jnp.sum(p, axis=0, keepdims=True)
        p, v = block(0, qc)
        low = key_index(0)
        p = jnp.where(low >= jnp.where(mine > 0, lowest, 1 << 30), p, 0.0)
        total += tn(v, p.astype(BF))
        denominator += jnp.sum(p, axis=0, keepdims=True)
        total = total / denominator
        out_t[c] = total
        logs[c] = jnp.log2(denominator)
        rows = total.T.astype(BF)
        att[c, :, :HD] = rows[:CH]
        att[c, :, HD:] = rows[CH:]
    for copy in copies + weights:
        copy.wait_send()
    for copy in weights:
        copy.wait_recv()
    keep.wait()


def attend(q, kv, w2_ring, start):
    any_ = pl.BlockSpec(memory_space=pl.ANY)
    vmem = pl.BlockSpec(memory_space=pltpu.VMEM)
    smem = pl.BlockSpec(memory_space=pltpu.SMEM)
    return pl.pallas_call(
        attend_kernel,
        out_shape=(
            jax.ShapeDtypeStruct((4, CH, 2 * HD), BF),
            jax.ShapeDtypeStruct((4, HD, 2 * CH), F32),
            jax.ShapeDtypeStruct((4, 1, 2 * CH), F32),
            jax.ShapeDtypeStruct((4, 8, CH, 2 * HD), BF),
            jax.ShapeDtypeStruct((4, 8, 32, W2C), BF),
        ),
        in_specs=[vmem, vmem, any_, smem],
        out_specs=(vmem, vmem, vmem, vmem, any_),
        scratch_shapes=[
            pltpu.VMEM((HD, 2 * CH), F32),
            pltpu.VMEM((8, 2 * CH), F32),
            pltpu.SemaphoreType.DMA((1,)),
            pltpu.SemaphoreType.DMA((7,)),
            pltpu.SemaphoreType.DMA((7,)),
            pltpu.SemaphoreType.DMA((7,)),
            pltpu.SemaphoreType.DMA((7,)),
        ],
        compiler_params=pltpu.CompilerParams(
            collective_id=1, has_side_effects=True, vmem_limit_bytes=VMEM_LIMIT
        ),
        name="attend",
    )(q, kv, w2_ring, start)


def middle_kernel(
    att, w2, gain, tok_all, cot_all, res, grad_hidden, grad_att, dw, gain_term,
    n2, gh, act, ggu, hidden, *scratch,
):
    first = scratch[0:8]
    down = scratch[8:16]
    back = scratch[16:24]
    fwd_sems = scratch[24:28]
    bwd_sems = scratch[28:32]
    res_send, res_recv = scratch[32:34]
    z, x, y, h = place()
    greet(group_devices(z, h))
    out_sum = Reduce(*first[:4], z, h, first[4:])
    for k in (1, 3, 2, 0):
        out_sum.give(k, nt(att[lax.rem(z + k, 4)], w2[:, 768:1024]))
    for k in RING:
        out_sum.pass_on(k)
    v = tok_all[z, h].astype(F32) + out_sum.total()
    hidden[...] = v
    g = gain[...]
    rate = rms_rate(v)
    n2[z, h] = (v * rate * g).astype(BF)
    n2_out = Gather(n2.at[z, h], n2, z, h, fwd_sems)
    n2_out.to_core(0)
    down_sum = Reduce(*down[:4], z, h, down[4:])
    back_sum = Reduce(*back[:4], z, h, back[4:])

    def feed(k):
        chunk = lax.rem(z + 4 - k, 4)
        back_k = (4 - k) % 4
        rows = n2[chunk].reshape(CH, D)
        gu = nn(rows, w2[:, :768])
        ga = nn(cot_all[chunk].reshape(CH, D), w2[:, 1024:])
        gate, up = gu[:, :384], gu[:, 384:]
        s = 1.0 / (1.0 + jnp.exp(-gate))
        silu = gate * s
        a = (silu * up).astype(BF)
        act[chunk] = a
        down_sum.give(back_k, nt(a, w2[:, 1024:]))
        gg = (ga * up * s * (1.0 + gate * (1.0 - s))).astype(BF)
        gp = (ga * silu).astype(BF)
        ggu[chunk, :, :384] = gg
        ggu[chunk, :, 384:] = gp
        back_sum.give(back_k, nt(ggu[chunk], w2[:, :768]))

    n2_out.arrived(0)
    feed(0)
    n2_out.forward(1)
    n2_out.forward(3)
    n2_out.arrived(1)
    feed(1)
    n2_out.forward(2)
    n2_out.arrived(3)
    back_sum.pass_on(3)
    feed(3)
    back_sum.pass_on(1)
    n2_out.arrived(2)
    feed(2)
    back_sum.pass_on(2)
    down_sum.pass_on(3)
    down_sum.pass_on(1)
    down_sum.pass_on(2)
    gy = back_sum.total()
    v = hidden[...]
    rate = rms_rate(v)
    vr = v * rate
    gain_term[...] = jnp.sum(gy * vr, axis=0, keepdims=True)
    gg = gy * g
    gv = rate * (gg - vr * jnp.mean(gg * vr, axis=-1, keepdims=True))
    grad = cot_all[z, h].astype(F32) + gv
    grad_hidden[...] = grad
    gh[z, h] = grad.astype(BF)
    gh_out = Gather(gh.at[z, h], gh, z, h, bwd_sems)
    gh_out.to_core(0)
    res[h] = (hidden[...] + down_sum.total()).astype(BF)
    res_out = rcopy(res.at[h], res.at[h], res_send.at[0], res_recv.at[0], {"head": 1 - h})
    res_out.start()
    dw[:, :768] = tn(n2[...].reshape(4 * CH, D), ggu[...].reshape(4 * CH, 768)).astype(BF)
    for k in RING:
        gh_out.forward(k)
    dw[:, 1024:] = tn(cot_all[...].reshape(4 * CH, D), act[...].reshape(4 * CH, 384)).astype(BF)
    for k in range(4):
        gh_out.arrived(k)
    full = gh[...].reshape(4 * CH, D)
    ga = nn(full, w2[:, 768:1024]).astype(BF)
    for c in range(4):
        for i in range(2):
            grad_att[c, i * CH : (i + 1) * CH, :] = ga[c * CH : (c + 1) * CH, i * HD : (i + 1) * HD]
    dw[:, 768:1024] = tn(full, att[...].reshape(4 * CH, 256)).astype(BF)
    res_out.wait()
    for item in (out_sum, down_sum, back_sum, n2_out, gh_out):
        item.finish()


def middle(att, w2, gain, tok_all, cot_all):
    vmem = pl.BlockSpec(memory_space=pltpu.VMEM)
    return pl.pallas_call(
        middle_kernel,
        out_shape=(
            jax.ShapeDtypeStruct((2, HALF, D), BF),
            jax.ShapeDtypeStruct((HALF, D), F32),
            jax.ShapeDtypeStruct((4, 2 * CH, HD), BF),
            jax.ShapeDtypeStruct((D, W2C), BF),
            jax.ShapeDtypeStruct((1, D), F32),
        ),
        in_specs=[vmem] * 5,
        out_specs=(vmem,) * 5,
        scratch_shapes=[
            pltpu.VMEM((4, 2, HALF, D), BF),
            pltpu.VMEM((4, 2, HALF, D), BF),
            pltpu.VMEM((4, CH, 384), BF),
            pltpu.VMEM((4, CH, 768), BF),
            pltpu.VMEM((HALF, D), F32),
        ]
        + reduce_scratch() * 3
        + gather_scratch() * 2
        + [pltpu.SemaphoreType.DMA((1,))] * 2,
        compiler_params=pltpu.CompilerParams(
            collective_id=2, has_side_effects=True, vmem_limit_bytes=VMEM_LIMIT
        ),
        name="middle",
    )(att, w2, gain, tok_all, cot_all)


def attend_back_kernel(
    q, kv_all, go, out_t, logs, dw, start_ref, dq, dkv, dw_sum,
    dq_t, delta, far, acc, give, take, dw_take, give_send, give_recv, dw_send, dw_recv,
):
    z, x, y, h = place()
    t = x * 4 + y
    greet(plane_devices(x, y))
    weights = []
    for n, (dx, dy) in enumerate(PLANE):
        peer = lax.rem(x + dx, 2) * 4 + lax.rem(y + dy, 4)
        copy = rcopy(dw.at[:, peer], dw_take.at[n], dw_send.at[n], dw_recv.at[n], plane_peer(x, y, dx, dy))
        copy.start()
        weights.append(copy)
    start = start_ref[0, 0]
    dq_t[...] = jnp.zeros_like(dq_t)
    for c in range(4):
        delta[c] = jnp.sum(out_t[c] * go[c].astype(F32).T, axis=0, keepdims=True)
        far[c] = jnp.where(query_index(c * 8 + t) < start + MIDDLE, logs[c], 1e30)

    def pair(c, k, v, log, keep):
        qc, g = q[c], go[c]
        p = jnp.exp2(nt(k, qc) * SCALE2 - log)
        if keep is not None:
            p = jnp.where(keep, p, 0.0)
        ds = (p * (nt(v, g) - delta[c])).astype(BF)
        dq_t[c] += tn(k, ds)
        return nn(ds, qc), nn(p.astype(BF), g)

    def keys_of(other, own):
        result = []
        for c in range(4):
            both = kv_all[c, other]
            k, v = both[:, :HD], both[:, HD:]
            index = key_index(c * 8 + other)
            late = index >= start if c == 0 else None
            if own:
                mine = query_index(c * 8 + t)
                keep = (index <= mine) & (index >= first_allowed(mine, start))
                dk, dv = pair(c, k, v, logs[c], keep)
                acc[:, :HD] = dk
                acc[:, HD:] = dv
            else:
                acc[...] = jnp.zeros_like(acc)

                @pl.when(other < t)
                def _():
                    dk, dv = pair(c, k, v, far[c], late)
                    acc[:, :HD] = dk
                    acc[:, HD:] = dv

            dk, dv = acc[:, :HD], acc[:, HD:]
            for later in range(c + 1, 4):
                a, b = pair(later, k, v, far[later], late)
                dk += a
                dv += b
            result.append((dk * SCALE, dv))
        return result

    sent = []
    for n, (dx, dy) in enumerate(PLANE):
        other = lax.rem(x + dx, 2) * 4 + lax.rem(y + dy, 4)
        for c, (dk, dv) in enumerate(keys_of(other, False)):
            give[n, c, :, :HD] = dk.astype(BF)
            give[n, c, :, HD:] = dv.astype(BF)
        copy = rcopy(give.at[n], take.at[n], give_send.at[n], give_recv.at[n], plane_peer(x, y, dx, dy))
        copy.start()
        sent.append(copy)
    for c, (dk, dv) in enumerate(keys_of(t, True)):
        dkv[c, :, :HD] = dk
        dkv[c, :, HD:] = dv
    for c in range(4):
        dq[c] = (dq_t[c] * SCALE).T
    for copy in weights:
        copy.wait()
    for c in range(4):
        part = dw[c, t].astype(F32)
        for n in range(7):
            part += dw_take[n, c].astype(F32)
        dw_sum[c] = part.astype(BF)
    for copy in sent:
        copy.wait()
    for c in range(4):
        part = dkv[c]
        for n in range(7):
            part += take[n, c].astype(F32)
        dkv[c] = part


def attend_back(q, kv_all, go, out_t, logs, dw, start):
    vmem = pl.BlockSpec(memory_space=pltpu.VMEM)
    smem = pl.BlockSpec(memory_space=pltpu.SMEM)
    return pl.pallas_call(
        attend_back_kernel,
        out_shape=(
            jax.ShapeDtypeStruct((4, 2 * CH, HD), F32),
            jax.ShapeDtypeStruct((4, CH, 2 * HD), F32),
            jax.ShapeDtypeStruct((4, 32, W2C), BF),
        ),
        in_specs=[vmem] * 6 + [smem],
        out_specs=(vmem,) * 3,
        scratch_shapes=[
            pltpu.VMEM((4, HD, 2 * CH), F32),
            pltpu.VMEM((4, 1, 2 * CH), F32),
            pltpu.VMEM((4, 1, 2 * CH), F32),
            pltpu.VMEM((CH, 2 * HD), F32),
            pltpu.VMEM((7, 4, CH, 2 * HD), BF),
            pltpu.VMEM((7, 4, CH, 2 * HD), BF),
            pltpu.VMEM((7, 4, 32, W2C), BF),
            pltpu.SemaphoreType.DMA((7,)),
            pltpu.SemaphoreType.DMA((7,)),
            pltpu.SemaphoreType.DMA((7,)),
            pltpu.SemaphoreType.DMA((7,)),
        ],
        compiler_params=pltpu.CompilerParams(
            collective_id=3, has_side_effects=True, vmem_limit_bytes=VMEM_LIMIT
        ),
        name="attend_back",
    )(q, kv_all, go, out_t, logs, dw, start)


def finish_kernel(
    dq, dkv, pre, normed, w1, gain, qgain, kgain, cosine, sine, tok_all, grad_hidden, dw2, gain_two,
    ig, g1, g2, terms_out,
    dpre, dw1, take, ring1, ring2, twin1, twin2, dw1_sum, term, term_core, term_plane, term_ring, term_twin, *scratch,
):
    sums = scratch[0:8]
    plane_send, plane_recv, ring_send, ring_recv, twin_send, twin_recv, ig_send, ig_recv, term_send, term_recv = scratch[8:]
    z, x, y, h = place()
    t = x * 4 + y
    twin = {"rep": 1 - lax.axis_index("rep")}
    greet(group_devices(z, h) + plane_devices(x, y) + [twin])

    def around(source, ring, which):
        copies = []
        for k in RING:
            copy = rcopy(
                source.at[lax.rem(z + k, 4)],
                ring.at[z],
                ring_send.at[which, k],
                ring_recv.at[which, k],
                ring_peer(z, k),
            )
            copy.start()
            copies.append(copy)
        ring[z] = source[z]
        return copies

    copies2 = around(dw2, ring2, 1)
    c_, s_ = cosine[...], sine[...]
    heads = []
    for i in range(2):
        heads.append(jnp.concatenate([dq[c, i * CH : (i + 1) * CH, :] for c in range(4)], axis=0))
    heads.append(dkv[...].reshape(4 * CH, 2 * HD)[:, :HD])
    terms = []
    for i, dy in enumerate(heads):
        gy = turn(dy, c_, -s_)
        v = pre[:, i * HD : (i + 1) * HD]
        rate = rms_rate(v)
        vr = v * rate
        terms.append(jnp.sum(gy * vr, axis=0, keepdims=True))
        gg = gy * (qgain if i < 2 else kgain)[...]
        out = rate * (gg - vr * jnp.mean(gg * vr, axis=-1, keepdims=True))
        dpre[:, i * HD : (i + 1) * HD] = out.astype(BF)
    dpre[:, 3 * HD :] = dkv[...].reshape(4 * CH, 2 * HD)[:, HD:].astype(BF)
    term[...] = jnp.zeros_like(term)
    term[16:17] = terms[0] + terms[1]
    term[17:18] = terms[2]
    dw1[...] = tn(normed[...], dpre[...]).astype(BF).reshape(4, 8, 32, W1C)
    plane = []
    for n, (dx, dy) in enumerate(PLANE):
        peer = lax.rem(x + dx, 2) * 4 + lax.rem(y + dy, 4)
        copy = rcopy(
            dw1.at[:, peer], take.at[n], plane_send.at[n], plane_recv.at[n], plane_peer(x, y, dx, dy)
        )
        copy.start()
        plane.append(copy)
    norm_sum = Reduce(*sums[:4], z, h, sums[4:])
    for k in (1, 3, 2, 0):
        chunk = lax.rem(z + k, 4)
        norm_sum.give(k, nt(dpre[pl.ds(pl.multiple_of(chunk * CH, CH), CH), :], w1[...]))
    for k in RING:
        norm_sum.pass_on(k)
    for copy in copies2:
        copy.wait()
    twin_copy2 = rcopy(ring2, twin2, twin_send.at[1], twin_recv.at[1], twin)
    twin_copy2.start()
    gy = norm_sum.total()
    v = tok_all[z, h].astype(F32)
    rate = rms_rate(v)
    vr = v * rate
    own_term = jnp.sum(gy * vr, axis=0, keepdims=True)
    for i in range(8):
        term[i : i + 1] = own_term[:, i * HD : (i + 1) * HD]
        term[8 + i : 9 + i] = gain_two[:, i * HD : (i + 1) * HD]
    term_copy = rcopy(term, term_core, term_send.at[0], term_recv.at[0], {"head": 1 - h})
    term_copy.start()
    gg = gy * gain[...]
    gv = rate * (gg - vr * jnp.mean(gg * vr, axis=-1, keepdims=True))
    ig[h] = (grad_hidden[...] + gv).astype(BF)
    ig_out = rcopy(ig.at[h], ig.at[h], ig_send.at[0], ig_recv.at[0], {"head": 1 - h})
    ig_out.start()
    term_copy.wait()
    term[...] += term_core[...]
    term_copies = []
    for n, (dx, dy) in enumerate(PLANE):
        copy = rcopy(term, term_plane.at[n], term_send.at[1 + n], term_recv.at[1 + n], plane_peer(x, y, dx, dy))
        copy.start()
        term_copies.append(copy)
    for copy in plane:
        copy.wait()
    part = dw1[:, t].astype(F32)
    for n in range(7):
        part += take[n].astype(F32)
    dw1_sum[...] = part.astype(BF)
    copies1 = around(dw1_sum, ring1, 0)
    for copy in term_copies:
        copy.wait()
    for n in range(7):
        term[...] += term_plane[n]
    term_copies = []
    for k in RING:
        copy = rcopy(term, term_ring.at[k - 1], term_send.at[7 + k], term_recv.at[7 + k], ring_peer(z, k))
        copy.start()
        term_copies.append(copy)
    for copy in copies1:
        copy.wait()
    twin_copy1 = rcopy(ring1, twin1, twin_send.at[0], twin_recv.at[0], twin)
    twin_copy1.start()
    for copy in term_copies:
        copy.wait()
    for k in range(3):
        term[...] += term_ring[k]
    term_copy = rcopy(term, term_twin, term_send.at[11], term_recv.at[11], twin)
    term_copy.start()
    twin_copy2.wait()
    g2[...] = ring2[...].astype(F32) + twin2[...].astype(F32)
    twin_copy1.wait()
    g1[...] = ring1[...].astype(F32) + twin1[...].astype(F32)
    ig_out.wait()
    term_copy.wait()
    terms_out[...] = term[...] + term_twin[...]
    norm_sum.finish()


def finish(dq, dkv, pre, normed, w1, gain, qgain, kgain, cosine, sine, tok_all, grad_hidden, dw2, gain_two):
    vmem = pl.BlockSpec(memory_space=pltpu.VMEM)
    return pl.pallas_call(
        finish_kernel,
        out_shape=(
            jax.ShapeDtypeStruct((2, HALF, D), BF),
            jax.ShapeDtypeStruct((4, 32, W1C), F32),
            jax.ShapeDtypeStruct((4, 32, W2C), F32),
            jax.ShapeDtypeStruct((24, HD), F32),
        ),
        in_specs=[vmem] * 14,
        out_specs=(vmem,) * 4,
        scratch_shapes=[
            pltpu.VMEM((4 * CH, W1C), BF),
            pltpu.VMEM((4, 8, 32, W1C), BF),
            pltpu.VMEM((7, 4, 32, W1C), BF),
            pltpu.VMEM((4, 32, W1C), BF),
            pltpu.VMEM((4, 32, W2C), BF),
            pltpu.VMEM((4, 32, W1C), BF),
            pltpu.VMEM((4, 32, W2C), BF),
            pltpu.VMEM((4, 32, W1C), BF),
            pltpu.VMEM((24, HD), F32),
            pltpu.VMEM((24, HD), F32),
            pltpu.VMEM((7, 24, HD), F32),
            pltpu.VMEM((3, 24, HD), F32),
            pltpu.VMEM((24, HD), F32),
        ]
        + reduce_scratch()
        + [
            pltpu.SemaphoreType.DMA((7,)),
            pltpu.SemaphoreType.DMA((7,)),
            pltpu.SemaphoreType.DMA((2, 4)),
            pltpu.SemaphoreType.DMA((2, 4)),
            pltpu.SemaphoreType.DMA((2,)),
            pltpu.SemaphoreType.DMA((2,)),
            pltpu.SemaphoreType.DMA((1,)),
            pltpu.SemaphoreType.DMA((1,)),
            pltpu.SemaphoreType.DMA((12,)),
            pltpu.SemaphoreType.DMA((12,)),
        ],
        compiler_params=pltpu.CompilerParams(
            collective_id=4, has_side_effects=True, vmem_limit_bytes=VMEM_LIMIT
        ),
        name="finish",
    )(dq, dkv, pre, normed, w1, gain, qgain, kgain, cosine, sine, tok_all, grad_hidden, dw2, gain_two)


def on_device(
    tokens, segments, positions, cotangent, query_weight, key_weight, value_weight, out_weight,
    attn_gain, query_gain, key_gain, gate_weight, up_weight, down_weight, mlp_gain,
):
    t = lax.axis_index("ctx_1") * 4 + lax.axis_index("ctx_2")
    own_index = lax.axis_index(CTX) * CH + jnp.arange(CH, dtype=jnp.int32)
    start = jnp.max(jnp.where(segments[0] == 1, own_index - positions[0], 0))
    group = ((jnp.arange(4, dtype=jnp.int32) * 8 + t)[:, None] * CH + jnp.arange(CH, dtype=jnp.int32)).reshape(-1)
    begin = jnp.where(group < start, 0, jnp.where(group < start + MIDDLE, start, start + MIDDLE))
    inverse = ROPE_BASE ** (-jnp.arange(HD // 2, dtype=F32) / (HD // 2))
    angles = (group - begin).astype(F32)[:, None] * inverse[None, :]
    cosine, sine = jnp.cos(angles), jnp.sin(angles)
    cosine = jnp.concatenate([cosine, cosine], axis=1)
    sine = jnp.concatenate([-sine, sine], axis=1)

    def shards(w):
        return w.reshape(32, 4, -1)

    w1 = jnp.concatenate([shards(query_weight), shards(key_weight), shards(value_weight)], axis=2)
    w2 = jnp.concatenate(
        [shards(gate_weight), shards(up_weight), shards(out_weight.T), shards(down_weight.T)], axis=2
    )
    gains = jnp.concatenate([attn_gain, mlp_gain, jnp.zeros((64,), BF)]).astype(F32)
    gains = jnp.broadcast_to(gains[None], (8, 128))
    tok_all, cot_all, w1_all, w2_ring, gains_all = spread(
        tokens.reshape(2, HALF, D),
        cotangent.reshape(2, HALF, D),
        w1.transpose(1, 0, 2),
        w2.transpose(1, 0, 2),
        gains,
    )
    gain_one = gains_all[:, :, 0, :32].reshape(1, D)
    gain_two = gains_all[:, :, 0, 32:64].reshape(1, D)
    w1_all = w1_all.reshape(D, W1C)
    qgain, kgain = query_gain.astype(F32)[None], key_gain.astype(F32)[None]
    q, kv, pre, normed = make_heads(
        tok_all.reshape(4 * CH, D), w1_all, gain_one, qgain, kgain, cosine, sine
    )
    start = start.reshape(1, 1)
    att, out_t, logs, kv_all, w2_all = attend(q, kv, w2_ring, start)
    result, grad_hidden, grad_att, dw2, gain_two_term = middle(
        att, w2_all.reshape(D, W2C), gain_two, tok_all, cot_all
    )
    dq, dkv, dw2_sum = attend_back(q, kv_all, grad_att, out_t, logs, dw2.reshape(4, 8, 32, W2C), start)
    input_grad, g1, g2, terms = finish(
        dq, dkv, pre, normed, w1_all, gain_one, qgain, kgain, cosine, sine, tok_all, grad_hidden, dw2_sum,
        gain_two_term,
    )
    terms = terms.reshape(-1)
    own = lax.axis_index(CTX) * 32

    def joined(g, a, b):
        return g[:, :, a:b].transpose(1, 0, 2).reshape(32, -1)

    return (
        result.reshape(1, CH, D),
        input_grad.reshape(1, CH, D),
        joined(g1, 0, 256),
        joined(g1, 256, 384),
        joined(g1, 384, 512),
        joined(g2, 768, 1024).T,
        lax.dynamic_slice(terms, (own,), (32,)),
        terms[2 * D : 2 * D + HD],
        terms[2 * D + HD : 2 * D + 2 * HD],
        joined(g2, 0, 384),
        joined(g2, 384, 768),
        joined(g2, 1024, 1408).T,
        lax.dynamic_slice(terms, (D + own,), (32,)),
    )


def solution(mesh):
    torus = Mesh(
        mesh.devices.reshape(mesh.shape["rep"], 4, 2, 4, mesh.shape["head"]),
        ("rep", "ctx_0", "ctx_1", "ctx_2", "head"),
    )
    return jax.shard_map(
        on_device,
        mesh=torus,
        in_specs=(
            P("rep", CTX, None),
            P("rep", CTX),
            P("rep", CTX),
            P("rep", CTX, None),
            P(CTX, "head"),
            P(CTX, "head"),
            P(CTX, "head"),
            P("head", CTX),
            P(CTX),
            P(),
            P(),
            P(CTX, "head"),
            P(CTX, "head"),
            P("head", CTX),
            P(CTX),
        ),
        out_specs=(
            P("rep", CTX, None),
            P("rep", CTX, None),
            P(CTX, "head"),
            P(CTX, "head"),
            P(CTX, "head"),
            P("head", CTX),
            P(CTX),
            P(),
            P(),
            P(CTX, "head"),
            P(CTX, "head"),
            P("head", CTX),
            P(CTX),
        ),
        check_vma=False,
    )
```

```python
import math

import jax
import jax.numpy as jnp
from jax import lax
from jax.experimental import pallas as pl
from jax.experimental.pallas import tpu as pltpu
from jax.sharding import Mesh
from jax.sharding import PartitionSpec as P

MESH = pl.DeviceIdType.MESH
CTX = ("ctx_0", "ctx_1", "ctx_2")
EPSILON = 1e-06
ROPE_BASE = 1000000.0
BF = jnp.bfloat16
F32 = jnp.float32
HD = 128
D = 1024
CH = 192
HALF = 96
MIDDLE = 5952
W1C = 512
SCALE = 1.0 / math.sqrt(HD)
SCALE2 = SCALE / math.log(2.0)
VMEM_LIMIT = 56 * 1024 * 1024
PLANE = ((0, 1), (0, 3), (1, 0), (1, 1), (1, 3), (0, 2), (1, 2))
RING = (1, 3, 2)


def nn(a, b):
    return jnp.dot(a, b, preferred_element_type=F32)


def nt(a, b):
    return lax.dot_general(a, b, (((1,), (1,)), ((), ())), preferred_element_type=F32)


def tn(a, b):
    return lax.dot_general(a, b, (((0,), (0,)), ((), ())), preferred_element_type=F32)


def rcopy(src, dst, send, recv, device):
    return pltpu.make_async_remote_copy(
        src_ref=src, dst_ref=dst, send_sem=send, recv_sem=recv, device_id=device, device_id_type=MESH
    )


def place():
    return tuple(lax.axis_index(name) for name in ("ctx_0", "ctx_1", "ctx_2", "head"))


def ring_peer(z, k):
    return {"ctx_0": lax.rem(z + k, 4)}


def plane_peer(x, y, dx, dy):
    return {"ctx_1": lax.rem(x + dx, 2), "ctx_2": lax.rem(y + dy, 4)}


def greet(devices):
    barrier = pltpu.get_barrier_semaphore()
    for device in devices:
        pl.semaphore_signal(barrier, inc=1, device_id=device, device_id_type=MESH)
    pl.semaphore_wait(barrier, len(devices))


def group_devices(z, h):
    return [{"head": 1 - h}] + [ring_peer(z, k) for k in RING]


def plane_devices(x, y):
    return [plane_peer(x, y, dx, dy) for dx, dy in PLANE]


class Gather:
    def __init__(self, own, buf, z, h, sems):
        self.buf, self.z, self.h = buf, z, h
        self.sz, self.rz, self.ss, self.rs = sems
        self.sent = []
        self.from_core = {}
        self.ring = {}
        for k in RING:
            copy = rcopy(own, buf.at[z, h], self.sz.at[k], self.rz.at[k], ring_peer(z, k))
            copy.start()
            self.ring[k] = copy
            self.sent.append(copy)

    def to_core(self, k):
        source = lax.rem(self.z + 4 - k, 4)
        slot = self.buf.at[source, self.h]
        copy = rcopy(slot, slot, self.ss.at[k], self.rs.at[k], {"head": 1 - self.h})
        copy.start()
        self.from_core[k] = copy
        self.sent.append(copy)

    def forward(self, k):
        self.ring[k].wait_recv()
        self.to_core(k)

    def arrived(self, k):
        self.from_core[k].wait_recv()

    def finish(self):
        for copy in self.sent:
            copy.wait_send()


class Reduce:
    def __init__(self, parts, other, sums, inbox, z, h, sems):
        self.parts, self.other, self.sums, self.inbox, self.z, self.h = parts, other, sums, inbox, z, h
        self.ss, self.rs, self.sz, self.rz = sems
        self.sent = []
        self.core = {}
        self.ring = {}

    def give(self, k, value):
        chunk = lax.rem(self.z + k, 4)
        self.parts[chunk] = value.astype(BF).reshape(2, HALF, D)
        self.offer(k)

    def offer(self, k):
        chunk = lax.rem(self.z + k, 4)
        copy = rcopy(
            self.parts.at[chunk, 1 - self.h],
            self.other.at[chunk],
            self.ss.at[k],
            self.rs.at[k],
            {"head": 1 - self.h},
        )
        copy.start()
        self.core[k] = copy
        self.sent.append(copy)

    def pass_on(self, k):
        chunk = lax.rem(self.z + k, 4)
        self.core[k].wait_recv()
        both = self.parts[chunk, self.h].astype(F32) + self.other[chunk].astype(F32)
        self.sums[chunk] = both.astype(BF)
        copy = rcopy(
            self.sums.at[chunk],
            self.inbox.at[self.z],
            self.sz.at[k],
            self.rz.at[k],
            ring_peer(self.z, k),
        )
        copy.start()
        self.ring[k] = copy
        self.sent.append(copy)

    def total(self):
        self.core[0].wait_recv()
        result = self.parts[self.z, self.h].astype(F32) + self.other[self.z].astype(F32)
        for k in RING:
            self.ring[k].wait_recv()
            result += self.inbox[lax.rem(self.z + 4 - k, 4)].astype(F32)
        return result

    def finish(self):
        for copy in self.sent:
            copy.wait_send()


def reduce_scratch(parts=True):
    return [pltpu.VMEM((4, 2, HALF, D), BF)] * parts + [
        pltpu.VMEM((4, HALF, D), BF),
        pltpu.VMEM((4, HALF, D), BF),
        pltpu.VMEM((4, HALF, D), BF),
    ] + [pltpu.SemaphoreType.DMA((4,))] * 4


def gather_scratch():
    return [pltpu.SemaphoreType.DMA((4,))] * 4


def spread_kernel(
    tok, w1, gains, tok_all, w1_all, gains_all,
    w1_ring, gains_ring, local, ring_send, ring_recv, plane_send, plane_recv, *sems
):
    z, x, y, h = place()
    t = x * 4 + y
    greet(group_devices(z, h) + plane_neighbours(x, y))
    keep = [
        pltpu.make_async_copy(w1.at[z], w1_ring.at[z], local.at[0]),
        pltpu.make_async_copy(gains, gains_ring.at[z], local.at[1]),
        pltpu.make_async_copy(tok, tok_all.at[z], local.at[2]),
    ]
    for copy in keep:
        copy.start()
    ring = []
    for k in RING:
        peer = lax.rem(z + k, 4)
        pair = [
            rcopy(w1.at[peer], w1_ring.at[z], ring_send.at[0, k], ring_recv.at[0, k], ring_peer(z, k)),
            rcopy(gains, gains_ring.at[z], ring_send.at[1, k], ring_recv.at[1, k], ring_peer(z, k)),
        ]
        for copy in pair:
            copy.start()
        ring += pair
    tokens_out = Gather(tok.at[h], tok_all, z, h, sems)
    for copy in keep:
        copy.wait()
    for copy in ring:
        copy.wait_recv()
    plane = [
        PlaneGather(w1_ring, w1_all, x, y, plane_send.at[0], plane_recv.at[0]),
        PlaneGather(gains_ring, gains_all, x, y, plane_send.at[1], plane_recv.at[1]),
    ]
    keep = [
        pltpu.make_async_copy(w1_ring, w1_all.at[:, t], local.at[3]),
        pltpu.make_async_copy(gains_ring, gains_all.at[:, t], local.at[4]),
    ]
    for copy in keep:
        copy.start()
    for item in plane:
        item.relay()
    for k in RING:
        tokens_out.forward(k)
    for k in RING:
        tokens_out.arrived(k)
    for copy in ring:
        copy.wait_send()
    for item in plane:
        item.arrived()
        item.finish()
    tokens_out.finish()
    for copy in keep:
        copy.wait()


def spread(tok, w1, gains):
    any_ = pl.BlockSpec(memory_space=pl.ANY)
    return pl.pallas_call(
        spread_kernel,
        out_shape=(
            jax.ShapeDtypeStruct((4, 2, HALF, D), BF),
            jax.ShapeDtypeStruct((4, 8, 32, W1C), BF),
            jax.ShapeDtypeStruct((4, 8, 8, 128), F32),
        ),
        in_specs=[any_] * 3,
        out_specs=(any_,) * 3,
        scratch_shapes=[
            pltpu.VMEM((4, 32, W1C), BF),
            pltpu.VMEM((4, 8, 128), F32),
            pltpu.SemaphoreType.DMA((5,)),
            pltpu.SemaphoreType.DMA((2, 4)),
            pltpu.SemaphoreType.DMA((2, 4)),
            pltpu.SemaphoreType.DMA((2, 11)),
            pltpu.SemaphoreType.DMA((2, 11)),
        ]
        + gather_scratch(),
        compiler_params=pltpu.CompilerParams(
            collective_id=0, has_side_effects=True, vmem_limit_bytes=VMEM_LIMIT
        ),
        name="spread",
    )(tok, w1, gains)


def swap_ring(source, ring, z, send, recv):
    copies = []
    for k in RING:
        copy = rcopy(source.at[lax.rem(z + k, 4)], ring.at[z], send.at[k], recv.at[k], ring_peer(z, k))
        copy.start()
        copies.append(copy)
    return copies


TURNS = (1, 3, 2)


def beside(x, y):
    along = [{"ctx_2": lax.rem(y + dy, 4)} for dy in TURNS]
    return along, {"ctx_1": 1 - x}, {"ctx_1": 1 - x, "rep": 1 - lax.axis_index("rep")}


def plane_neighbours(x, y):
    along, near, far = beside(x, y)
    return along + [near, far]


class PlaneGather:
    def __init__(self, source, buf, x, y, send, recv):
        self.buf, self.x, self.y, self.send, self.recv = buf, x, y, send, recv
        along, self.near, self.far = beside(x, y)
        self.down = []
        self.over = []
        slot = buf.at[:, x * 4 + y]
        for j in range(3):
            copy = rcopy(source, slot, send.at[j], recv.at[j], along[j])
            copy.start()
            self.down.append(copy)
        self.across(0, source, slot)

    def across(self, j, source, slot):
        for a, device in ((0, self.near), (1, self.far)):
            part = pl.ds(2 * a, 2)
            n = 3 + 2 * j + a
            copy = rcopy(source.at[part], slot.at[part], self.send.at[n], self.recv.at[n], device)
            copy.start()
            self.over.append(copy)

    def relay(self):
        for j, dy in enumerate(TURNS):
            self.down[j].wait_recv()
            slot = self.buf.at[:, self.x * 4 + lax.rem(self.y + 4 - dy, 4)]
            self.across(j + 1, slot, slot)

    def arrived(self):
        for copy in self.over:
            copy.wait_recv()

    def finish(self):
        for copy in self.down + self.over:
            copy.wait_send()


class PlaneReduce:
    def __init__(self, parts, inx, col, iny, x, y, send, recv):
        self.parts, self.inx, self.col, self.iny = parts, inx, col, iny
        self.x, self.y, self.send, self.recv = x, y, send, recv
        self.along, near, far = beside(x, y)
        self.over = []
        self.down = []
        for j, dy in enumerate(TURNS + (0,)):
            row = lax.rem(y + dy, 4)
            for a, device in ((0, near), (1, far)):
                part = pl.ds(2 * a, 2)
                copy = rcopy(
                    parts.at[part, (1 - x) * 4 + row],
                    inx.at[part, row],
                    send.at[2 * j + a],
                    recv.at[2 * j + a],
                    device,
                )
                copy.start()
                self.over.append(copy)

    def joined(self, j, row):
        self.over[2 * j].wait_recv()
        self.over[2 * j + 1].wait_recv()
        return self.parts[:, self.x * 4 + row].astype(F32) + self.inx[:, row].astype(F32)

    def relay(self):
        for j, dy in enumerate(TURNS):
            row = lax.rem(self.y + dy, 4)
            self.col[:, row] = self.joined(j, row).astype(BF)
            copy = rcopy(
                self.col.at[:, row], self.iny.at[j], self.send.at[8 + j], self.recv.at[8 + j], self.along[j]
            )
            copy.start()
            self.down.append(copy)

    def total(self):
        result = self.joined(3, self.y)
        for j in range(3):
            self.down[j].wait_recv()
            result += self.iny[j].astype(F32)
        return result

    def finish(self):
        for copy in self.down + self.over:
            copy.wait_send()


def plane_scratch(width):
    return [
        pltpu.VMEM((4, 4, 32, width), BF),
        pltpu.VMEM((4, 4, 32, width), BF),
        pltpu.VMEM((3, 4, 32, width), BF),
    ]


def turn(u, cosine, sine):
    return u * cosine + pltpu.roll(u, HD // 2, 1) * sine


def rms_rate(v):
    return lax.rsqrt(jnp.mean(v * v, axis=-1, keepdims=True) + EPSILON)


def heads_kernel(tok, w1, gain, qgain, kgain, cosine, sine, q, kv, pre, normed):
    v = tok[...].astype(F32)
    n = (v * rms_rate(v) * gain[...]).astype(BF)
    normed[...] = n
    out = nn(n, w1[...])
    pre[...] = out[:, :384]
    c, s = cosine[...], sine[...]
    for i in range(3):
        u = out[:, i * HD : (i + 1) * HD]
        u = turn(u * rms_rate(u) * (qgain if i < 2 else kgain)[...], c, s).astype(BF)
        if i < 2:
            q[0, i * CH : (i + 1) * CH, :] = u
        else:
            kv[0, :, :HD] = u
    kv[0, :, HD:] = out[:, 384:].astype(BF)


def make_heads(tok_all, w1, gain, qgain, kgain, cosine, sine):
    def whole(*shape):
        return pl.BlockSpec(shape, lambda i: (0,) * len(shape))

    return pl.pallas_call(
        heads_kernel,
        grid=(4,),
        out_shape=(
            jax.ShapeDtypeStruct((4, 2 * CH, HD), BF),
            jax.ShapeDtypeStruct((4, CH, 2 * HD), BF),
            jax.ShapeDtypeStruct((4 * CH, 384), F32),
            jax.ShapeDtypeStruct((4 * CH, D), BF),
        ),
        in_specs=[
            pl.BlockSpec((CH, D), lambda i: (i, 0)),
            whole(D, W1C),
            whole(1, D),
            whole(1, HD),
            whole(1, HD),
            pl.BlockSpec((CH, HD), lambda i: (i, 0)),
            pl.BlockSpec((CH, HD), lambda i: (i, 0)),
        ],
        out_specs=(
            pl.BlockSpec((1, 2 * CH, HD), lambda i: (i, 0, 0)),
            pl.BlockSpec((1, CH, 2 * HD), lambda i: (i, 0, 0)),
            pl.BlockSpec((CH, 384), lambda i: (i, 0)),
            pl.BlockSpec((CH, D), lambda i: (i, 0)),
        ),
        compiler_params=pltpu.CompilerParams(vmem_limit_bytes=VMEM_LIMIT),
        name="make_heads",
    )(tok_all, w1, gain, qgain, kgain, cosine, sine)


def query_index(chunk):
    lane = lax.broadcasted_iota(jnp.int32, (1, 2 * CH), 1)
    return chunk * CH + jnp.where(lane < CH, lane, lane - CH)


def first_allowed(index, start):
    return jnp.where(index < start, 0, jnp.where(index < start + MIDDLE, start, start + MIDDLE))


def key_index(chunk):
    return chunk * CH + lax.broadcasted_iota(jnp.int32, (CH, 1), 0)


def row_sums(p):
    return jnp.sum(p.reshape(CH // 8, 8, 2 * CH), axis=0)


def attend_kernel(
    q, kv, cot, wo, wg, wd, start_ref, att, out_t, logs, kv_all, cot_all, wo_ring, wg_ring, wd_ring,
    acc, den, own_acc, own_den, local, kv_send, kv_recv, ring_send, ring_recv, *sems
):
    z, x, y, h = place()
    t = x * 4 + y
    greet(group_devices(z, h) + plane_neighbours(x, y)[:4])
    along, near, _ = beside(x, y)

    def send(n, source, slot, device):
        copy = rcopy(source, slot, kv_send.at[n], kv_recv.at[n], device)
        copy.start()
        return copy

    copies = [send(n, kv, kv_all.at[:, t], device) for n, device in enumerate(along + [near])]
    cot_out = Gather(cot.at[h], cot_all, z, h, sems)
    weights = []
    keep = [pltpu.make_async_copy(cot, cot_all.at[z], local.at[3])]
    for i, (source, ring) in enumerate(((wo, wo_ring), (wg, wg_ring), (wd, wd_ring))):
        weights += swap_ring(source, ring, z, ring_send.at[i], ring_recv.at[i])
        keep.append(pltpu.make_async_copy(source.at[z], ring.at[z], local.at[i]))
    for copy in keep:
        copy.start()
    kv_all[:, t] = kv[...]
    start = start_ref[0, 0]
    acc[...] = jnp.zeros_like(acc)
    den[...] = jnp.zeros_like(den)

    def block(c, other, qc, late):
        p = jnp.exp2(nt(kv_all[c, other, :, :HD], qc) * SCALE2)
        if c == 0:
            p = jnp.where(late, p, 0.0)
        return tn(kv_all[c, other, :, HD:], p.astype(BF)), row_sums(p)

    def visit(other, own=False):
        late = key_index(other) >= start
        for c in range(4):
            if c > 0:
                a, d = block(0, other, q[c], late)
                for earlier in range(1, c):
                    aa, dd = block(earlier, other, q[c], late)
                    a += aa
                    d += dd
                acc[c] += a
                den[c] += d
            if not own:

                @pl.when(other < t)
                def _():
                    a, d = block(c, other, q[c], late)
                    acc[c] += a
                    den[c] += d

    for c in range(4):
        mine = c * 8 + t
        index = query_index(mine)
        last = key_index(mine)
        p = jnp.exp2(nt(kv[c, :, :HD], q[c]) * SCALE2)
        p = jnp.where((last <= index) & (last >= first_allowed(index, start)), p, 0.0)
        own_acc[c] = tn(kv[c, :, HD:], p.astype(BF))
        own_den[c] = row_sums(p)
    visit(t, True)
    rows = [lax.rem(y + 4 - dy, 4) for dy in TURNS]
    halves = (pl.ds(0, 2), pl.ds(2, 2))

    def over(j):
        copies[j].wait_recv()
        slot = kv_all.at[halves[0], x * 4 + rows[j]]
        copies.append(send(4 + j, slot, slot, near))

    over(0)
    over(1)
    copies[3].wait_recv()
    across = (1 - x) * 4 + y
    slot = kv_all.at[halves[1], across]
    for j in range(3):
        copies.append(send(7 + j, slot, slot, along[j]))
    visit(x * 4 + rows[0])
    visit(x * 4 + rows[1])
    over(2)
    visit(across)
    visit(x * 4 + rows[2])
    relayed = {0: (4, 6), 1: (5, 7), 2: (9, 8)}
    for k in RING:
        cot_out.forward(k)
    for j in range(3):
        for n in relayed[j]:
            copies[n].wait_recv()
        visit((1 - x) * 4 + rows[j])
    for c in range(4):
        inside = (query_index(c * 8 + t) < start + MIDDLE).astype(F32)
        denominator = jnp.sum(den[c] * inside + own_den[c], axis=0, keepdims=True)
        total = (acc[c] * inside + own_acc[c]) / denominator
        out_t[c] = total
        logs[c] = jnp.log2(denominator)
        full = total.T.astype(BF)
        att[c, :, :HD] = full[:CH]
        att[c, :, HD:] = full[CH:]
    for copy in copies:
        copy.wait_send()
    for k in RING:
        cot_out.arrived(k)
    cot_out.finish()
    for copy in weights + keep:
        copy.wait()


def attend(q, kv, cot, wo, wg, wd, start):
    any_ = pl.BlockSpec(memory_space=pl.ANY)
    vmem = pl.BlockSpec(memory_space=pltpu.VMEM)
    smem = pl.BlockSpec(memory_space=pltpu.SMEM)
    return pl.pallas_call(
        attend_kernel,
        out_shape=(
            jax.ShapeDtypeStruct((4, CH, 2 * HD), BF),
            jax.ShapeDtypeStruct((4, HD, 2 * CH), F32),
            jax.ShapeDtypeStruct((4, 1, 2 * CH), F32),
            jax.ShapeDtypeStruct((4, 8, CH, 2 * HD), BF),
            jax.ShapeDtypeStruct((4, 2, HALF, D), BF),
            jax.ShapeDtypeStruct((4, 32, 256), BF),
            jax.ShapeDtypeStruct((4, 32, 768), BF),
            jax.ShapeDtypeStruct((4, 32, 384), BF),
        ),
        in_specs=[vmem, vmem, any_, any_, any_, any_, smem],
        out_specs=(vmem, vmem, vmem, vmem, any_, any_, any_, any_),
        scratch_shapes=[
            pltpu.VMEM((4, HD, 2 * CH), F32),
            pltpu.VMEM((4, 8, 2 * CH), F32),
            pltpu.VMEM((4, HD, 2 * CH), F32),
            pltpu.VMEM((4, 8, 2 * CH), F32),
            pltpu.SemaphoreType.DMA((4,)),
            pltpu.SemaphoreType.DMA((10,)),
            pltpu.SemaphoreType.DMA((10,)),
            pltpu.SemaphoreType.DMA((3, 4)),
            pltpu.SemaphoreType.DMA((3, 4)),
        ]
        + gather_scratch(),
        compiler_params=pltpu.CompilerParams(
            collective_id=1, has_side_effects=True, vmem_limit_bytes=VMEM_LIMIT
        ),
        name="attend",
    )(q, kv, cot, wo, wg, wd, start)


def middle_kernel(
    att, wo_ring, wg_ring, wd_ring, gain, tok, cot_all,
    hidden, down_parts, grad_hidden, grad_att, dwo, dwg_sum, dwd_sum, gain_term,
    n2, gh, act, ggu, wo_all, wg_all, wd_all, dwg, dwd, *scratch,
):
    first = scratch[0:8]
    back = scratch[8:16]
    fwd_sems = scratch[16:20]
    bwd_sems = scratch[20:24]
    dwg_buf = scratch[24:27]
    dwd_buf = scratch[27:30]
    w_send, w_recv = scratch[30:32]
    z, x, y, h = place()
    t = x * 4 + y
    greet(group_devices(z, h) + plane_neighbours(x, y))
    wo_in = PlaneGather(wo_ring, wo_all, x, y, w_send.at[0], w_recv.at[0])
    wo_all[:, t] = wo_ring[...]
    wg_all[:, t] = wg_ring[...]
    wd_all[:, t] = wd_ring[...]
    wo_in.relay()
    wg_in = PlaneGather(wg_ring, wg_all, x, y, w_send.at[1], w_recv.at[1])
    wd_in = PlaneGather(wd_ring, wd_all, x, y, w_send.at[2], w_recv.at[2])
    wo_in.arrived()
    out_sum = Reduce(*first[:4], z, h, first[4:])
    for k in (1, 3, 2, 0):
        out_sum.give(k, nt(att[lax.rem(z + k, 4)], wo_all[...].reshape(D, 256)))
    for k in RING:
        out_sum.pass_on(k)
    wg_in.relay()
    v = tok[h].astype(F32) + out_sum.total()
    hidden[...] = v
    g = gain[...]
    rate = rms_rate(v)
    n2[z, h] = (v * rate * g).astype(BF)
    n2_out = Gather(n2.at[z, h], n2, z, h, fwd_sems)
    n2_out.to_core(0)
    wd_in.relay()
    back_sum = Reduce(*back[:4], z, h, back[4:])

    def feed(k):
        chunk = lax.rem(z + 4 - k, 4)
        back_k = (4 - k) % 4
        rows = n2[chunk].reshape(CH, D)
        gu = nn(rows, wg_all[...].reshape(D, 768))
        if k == 0:
            wd_in.arrived()
        ga = nn(cot_all[chunk].reshape(CH, D), wd_all[...].reshape(D, 384))
        gate, up = gu[:, :384], gu[:, 384:]
        s = 1.0 / (1.0 + jnp.exp(-gate))
        silu = gate * s
        a = (silu * up).astype(BF)
        act[chunk] = a
        gg = (ga * up * s * (1.0 + gate * (1.0 - s))).astype(BF)
        gp = (ga * silu).astype(BF)
        ggu[chunk, :, :384] = gg
        ggu[chunk, :, 384:] = gp
        back_sum.give(back_k, nt(ggu[chunk], wg_all[...].reshape(D, 768)))
        down_parts[chunk] = nt(a, wd_all[...].reshape(D, 384)).astype(BF).reshape(2, HALF, D)

    n2_out.arrived(0)
    wg_in.arrived()
    feed(0)
    n2_out.forward(1)
    n2_out.forward(3)
    n2_out.arrived(1)
    feed(1)
    n2_out.forward(2)
    n2_out.arrived(3)
    back_sum.pass_on(3)
    feed(3)
    back_sum.pass_on(1)
    n2_out.arrived(2)
    feed(2)
    back_sum.pass_on(2)
    dwg[...] = (
        tn(n2[...].reshape(4 * CH, D), ggu[...].reshape(4 * CH, 768)).astype(BF).reshape(4, 8, 32, 768)
    )
    dwg_out = PlaneReduce(dwg, *dwg_buf, x, y, w_send.at[3], w_recv.at[3])
    gy = back_sum.total()
    v = hidden[...]
    rate = rms_rate(v)
    vr = v * rate
    gain_term[...] = jnp.sum(gy * vr, axis=0, keepdims=True)
    gg = gy * g
    gv = rate * (gg - vr * jnp.mean(gg * vr, axis=-1, keepdims=True))
    grad = cot_all[z, h].astype(F32) + gv
    grad_hidden[...] = grad
    gh[z, h] = grad.astype(BF)
    gh_out = Gather(gh.at[z, h], gh, z, h, bwd_sems)
    gh_out.to_core(0)
    dwd[...] = (
        tn(cot_all[...].reshape(4 * CH, D), act[...].reshape(4 * CH, 384)).astype(BF).reshape(4, 8, 32, 384)
    )
    dwd_out = PlaneReduce(dwd, *dwd_buf, x, y, w_send.at[4], w_recv.at[4])
    for k in RING:
        gh_out.forward(k)
    dwg_out.relay()
    for k in range(4):
        gh_out.arrived(k)
    full = gh[...].reshape(4 * CH, D)
    ga = nn(full, wo_all[...].reshape(D, 256)).astype(BF)
    for c in range(4):
        for i in range(2):
            grad_att[c, i * CH : (i + 1) * CH, :] = ga[c * CH : (c + 1) * CH, i * HD : (i + 1) * HD]
    dwo[...] = tn(full, att[...].reshape(4 * CH, 256)).astype(BF)
    dwd_out.relay()
    dwg_sum[...] = dwg_out.total().astype(BF)
    dwd_sum[...] = dwd_out.total().astype(BF)
    for item in (out_sum, back_sum, n2_out, gh_out, wo_in, wg_in, wd_in, dwg_out, dwd_out):
        item.finish()


def middle(att, wo, wg, wd, gain, tok, cot_all):
    vmem = pl.BlockSpec(memory_space=pltpu.VMEM)
    return pl.pallas_call(
        middle_kernel,
        out_shape=(
            jax.ShapeDtypeStruct((HALF, D), F32),
            jax.ShapeDtypeStruct((4, 2, HALF, D), BF),
            jax.ShapeDtypeStruct((HALF, D), F32),
            jax.ShapeDtypeStruct((4, 2 * CH, HD), BF),
            jax.ShapeDtypeStruct((D, 256), BF),
            jax.ShapeDtypeStruct((4, 32, 768), BF),
            jax.ShapeDtypeStruct((4, 32, 384), BF),
            jax.ShapeDtypeStruct((1, D), F32),
        ),
        in_specs=[vmem] * 7,
        out_specs=(vmem,) * 8,
        scratch_shapes=[
            pltpu.VMEM((4, 2, HALF, D), BF),
            pltpu.VMEM((4, 2, HALF, D), BF),
            pltpu.VMEM((4, CH, 384), BF),
            pltpu.VMEM((4, CH, 768), BF),
            pltpu.VMEM((4, 8, 32, 256), BF),
            pltpu.VMEM((4, 8, 32, 768), BF),
            pltpu.VMEM((4, 8, 32, 384), BF),
            pltpu.VMEM((4, 8, 32, 768), BF),
            pltpu.VMEM((4, 8, 32, 384), BF),
        ]
        + reduce_scratch() * 2
        + gather_scratch() * 2
        + plane_scratch(768)
        + plane_scratch(384)
        + [pltpu.SemaphoreType.DMA((5, 11))] * 2,
        compiler_params=pltpu.CompilerParams(
            collective_id=2, has_side_effects=True, vmem_limit_bytes=VMEM_LIMIT
        ),
        name="middle",
    )(att, wo, wg, wd, gain, tok, cot_all)


def attend_back_kernel(
    q, kv_all, go, out_t, logs, dwo, dwg, dwd, hidden, down_parts, start_ref,
    dq, dkv, dwo_ring, dwg_ring, dwd_ring, res,
    dq_t, delta, far, acc, give_b, take_b, give_a, take_a, give_c, take_c, give_d, take_d, dwo_sum, *scratch,
):
    dwo_buf = scratch[:3]
    down = scratch[3:10]
    kv_send, kv_recv, w_send, w_recv, r_send, r_recv, res_send, res_recv = scratch[10:]
    z, x, y, h = place()
    t = x * 4 + y
    greet(group_devices(z, h) + plane_neighbours(x, y))
    along, near, _ = beside(x, y)
    down_sum = Reduce(down_parts, *down[:3], z, h, down[3:])
    for k in (1, 3, 2, 0):
        down_sum.offer(k)
    dwo_out = PlaneReduce(dwo, *dwo_buf, x, y, w_send, w_recv)
    rings = swap_ring(dwg, dwg_ring, z, r_send.at[1], r_recv.at[1])
    rings += swap_ring(dwd, dwd_ring, z, r_send.at[2], r_recv.at[2])
    dwg_ring[z] = dwg[z]
    dwd_ring[z] = dwd[z]
    start = start_ref[0, 0]
    dq_t[...] = jnp.zeros_like(dq_t)
    for c in range(4):
        delta[c] = jnp.sum(out_t[c] * go[c].astype(F32).T, axis=0, keepdims=True)
        far[c] = jnp.where(query_index(c * 8 + t) < start + MIDDLE, logs[c], 1e30)

    def pair(c, k, v, log, keep):
        qc, g = q[c], go[c]
        p = jnp.exp2(nt(k, qc) * SCALE2 - log)
        if keep is not None:
            p = jnp.where(keep, p, 0.0)
        ds = (p * (nt(v, g) - delta[c])).astype(BF)
        dq_t[c] += tn(k, ds)
        return nn(ds, qc), nn(p.astype(BF), g)

    def keys_of(other, chunks, own=False):
        result = []
        for c in chunks:
            both = kv_all[c, other]
            k, v = both[:, :HD], both[:, HD:]
            index = key_index(c * 8 + other)
            late = index >= start if c == 0 else None
            if own:
                mine = query_index(c * 8 + t)
                keep = (index <= mine) & (index >= first_allowed(mine, start))
                dk, dv = pair(c, k, v, logs[c], keep)
                acc[:, :HD] = dk
                acc[:, HD:] = dv
            else:
                acc[...] = jnp.zeros_like(acc)

                @pl.when(other < t)
                def _():
                    dk, dv = pair(c, k, v, far[c], late)
                    acc[:, :HD] = dk
                    acc[:, HD:] = dv

            dk, dv = acc[:, :HD], acc[:, HD:]
            for later in range(c + 1, 4):
                a, b = pair(later, k, v, far[later], late)
                dk += a
                dv += b
            result.append((dk * SCALE, dv))
        return result

    sent = []

    def send(n, source, slot, device):
        copy = rcopy(source, slot, kv_send.at[n], kv_recv.at[n], device)
        copy.start()
        sent.append(copy)

    def put(ref, values):
        for i, (dk, dv) in enumerate(values):
            ref[i, :, :HD] = dk.astype(BF)
            ref[i, :, HD:] = dv.astype(BF)

    rows = [lax.rem(y + dy, 4) for dy in TURNS]
    for j in range(3):
        for i, column in enumerate((x, 1 - x)):
            put(give_b.at[j, i], keys_of(column * 4 + rows[j], (2, 3)))
        send(j, give_b.at[j], take_b.at[j], along[j])
    for k in RING:
        down_sum.pass_on(k)
    for j, row in enumerate(rows + [y]):
        put(give_a.at[j], keys_of((1 - x) * 4 + row, (0, 1)))
        send(3 + j, give_a.at[j], take_a.at[j], near)
    dwo_out.relay()
    res[h] = (hidden[...] + down_sum.total()).astype(BF)
    res_out = rcopy(res.at[h], res.at[h], res_send.at[0], res_recv.at[0], {"head": 1 - h})
    res_out.start()
    dwo_sum[...] = dwo_out.total().astype(BF)
    rings += swap_ring(dwo_sum, dwo_ring, z, r_send.at[0], r_recv.at[0])
    dwo_ring[z] = dwo_sum[z]

    def add(values, *others):
        result = []
        for i, (dk, dv) in enumerate(values):
            for other in others:
                both = other[i].astype(F32)
                dk += both[:, :HD]
                dv += both[:, HD:]
            result.append((dk, dv))
        return result

    for j in range(3):
        values = keys_of(x * 4 + rows[j], (0, 1))
        sent[3 + j].wait_recv()
        put(give_c.at[j], add(values, take_a.at[j]))
        send(7 + j, give_c.at[j], take_c.at[j], along[j])
    values = keys_of((1 - x) * 4 + y, (2, 3))
    for j in range(3):
        sent[j].wait_recv()
    put(give_d, add(values, *(take_b.at[j, 1] for j in range(3))))
    send(10, give_d, take_d, near)
    low = keys_of(t, (0, 1), True)
    high = keys_of(t, (2, 3), True)
    for c in range(4):
        dq[c] = (dq_t[c] * SCALE).T
    sent[6].wait_recv()
    low = add(low, take_a.at[3])
    high = add(high, *(take_b.at[j, 0] for j in range(3)))
    for j in range(3):
        sent[7 + j].wait_recv()
    sent[10].wait_recv()
    low = add(low, *(take_c.at[j] for j in range(3)))
    high = add(high, take_d)
    for c, (dk, dv) in enumerate(low + high):
        dkv[c, :, :HD] = dk
        dkv[c, :, HD:] = dv
    for copy in rings:
        copy.wait()
    res_out.wait()
    for copy in sent:
        copy.wait_send()
    dwo_out.finish()
    down_sum.finish()


def attend_back(q, kv_all, go, out_t, logs, dwo, dwg, dwd, hidden, down_parts, start):
    vmem = pl.BlockSpec(memory_space=pltpu.VMEM)
    smem = pl.BlockSpec(memory_space=pltpu.SMEM)
    return pl.pallas_call(
        attend_back_kernel,
        out_shape=(
            jax.ShapeDtypeStruct((4, 2 * CH, HD), F32),
            jax.ShapeDtypeStruct((4, CH, 2 * HD), F32),
            jax.ShapeDtypeStruct((4, 32, 256), BF),
            jax.ShapeDtypeStruct((4, 32, 768), BF),
            jax.ShapeDtypeStruct((4, 32, 384), BF),
            jax.ShapeDtypeStruct((2, HALF, D), BF),
        ),
        in_specs=[vmem] * 10 + [smem],
        out_specs=(vmem,) * 6,
        scratch_shapes=[
            pltpu.VMEM((4, HD, 2 * CH), F32),
            pltpu.VMEM((4, 1, 2 * CH), F32),
            pltpu.VMEM((4, 1, 2 * CH), F32),
            pltpu.VMEM((CH, 2 * HD), F32),
            pltpu.VMEM((3, 2, 2, CH, 2 * HD), BF),
            pltpu.VMEM((3, 2, 2, CH, 2 * HD), BF),
            pltpu.VMEM((4, 2, CH, 2 * HD), BF),
            pltpu.VMEM((4, 2, CH, 2 * HD), BF),
            pltpu.VMEM((3, 2, CH, 2 * HD), BF),
            pltpu.VMEM((3, 2, CH, 2 * HD), BF),
            pltpu.VMEM((2, CH, 2 * HD), BF),
            pltpu.VMEM((2, CH, 2 * HD), BF),
            pltpu.VMEM((4, 32, 256), BF),
        ]
        + plane_scratch(256)
        + reduce_scratch(False)
        + [
            pltpu.SemaphoreType.DMA((11,)),
            pltpu.SemaphoreType.DMA((11,)),
            pltpu.SemaphoreType.DMA((11,)),
            pltpu.SemaphoreType.DMA((11,)),
            pltpu.SemaphoreType.DMA((3, 4)),
            pltpu.SemaphoreType.DMA((3, 4)),
            pltpu.SemaphoreType.DMA((1,)),
            pltpu.SemaphoreType.DMA((1,)),
        ],
        compiler_params=pltpu.CompilerParams(
            collective_id=3, has_side_effects=True, vmem_limit_bytes=VMEM_LIMIT
        ),
        name="attend_back",
    )(q, kv_all, go, out_t, logs, dwo, dwg, dwd, hidden, down_parts, start)


def finish_kernel(
    dq, dkv, pre, normed, w1, gain, qgain, kgain, cosine, sine, tok, grad_hidden, dwo, dwg, dwd,
    gain_two, ig, g1, go, gg_, gd, terms_out,
    dpre, dw1, ring1, twin1, dw1_sum, two, twg, twd, term, term_plane, term_ring, *scratch,
):
    sums = scratch[0:8]
    dw1_buf = scratch[8:11]
    plane_send, plane_recv, ring_send, ring_recv, twin_send, twin_recv, ig_send, ig_recv, term_send, term_recv = scratch[11:]
    z, x, y, h = place()
    t = x * 4 + y
    twin = {"rep": 1 - lax.axis_index("rep")}
    others = [{"head": h_, **device} for device in plane_devices(x, y) for h_ in (h, 1 - h)]
    rings = [{**ring_peer(z, k), **r} for k in RING for r in ({}, twin)]
    greet(group_devices(z, h)[:1] + others + rings + [twin, beside(x, y)[2]])

    twins = []
    for i, (source, other) in enumerate(((dwo, two), (dwg, twg), (dwd, twd))):
        copy = rcopy(source, other, twin_send.at[1 + i], twin_recv.at[1 + i], twin)
        copy.start()
        twins.append(copy)
    c_, s_ = cosine[...], sine[...]
    heads = []
    for i in range(2):
        heads.append(jnp.concatenate([dq[c, i * CH : (i + 1) * CH, :] for c in range(4)], axis=0))
    heads.append(dkv[...].reshape(4 * CH, 2 * HD)[:, :HD])
    terms = []
    for i, dy in enumerate(heads):
        gy = turn(dy, c_, -s_)
        v = pre[:, i * HD : (i + 1) * HD]
        rate = rms_rate(v)
        vr = v * rate
        terms.append(jnp.sum(gy * vr, axis=0, keepdims=True))
        gg = gy * (qgain if i < 2 else kgain)[...]
        out = rate * (gg - vr * jnp.mean(gg * vr, axis=-1, keepdims=True))
        dpre[:, i * HD : (i + 1) * HD] = out.astype(BF)
    dpre[:, 3 * HD :] = dkv[...].reshape(4 * CH, 2 * HD)[:, HD:].astype(BF)
    term[...] = jnp.zeros_like(term)
    term[16:17] = terms[0] + terms[1]
    term[17:18] = terms[2]
    dw1[...] = tn(normed[...], dpre[...]).astype(BF).reshape(4, 8, 32, W1C)
    dw1_out = PlaneReduce(dw1, *dw1_buf, x, y, plane_send, plane_recv)
    norm_sum = Reduce(*sums[:4], z, h, sums[4:])
    for k in (1, 3, 2, 0):
        chunk = lax.rem(z + k, 4)
        norm_sum.give(k, nt(dpre[pl.ds(pl.multiple_of(chunk * CH, CH), CH), :], w1[...]))
    for k in RING:
        norm_sum.pass_on(k)
    dw1_out.relay()
    gy = norm_sum.total()
    v = tok[h].astype(F32)
    rate = rms_rate(v)
    vr = v * rate
    own_term = jnp.sum(gy * vr, axis=0, keepdims=True)
    for i in range(8):
        term[i : i + 1] = own_term[:, i * HD : (i + 1) * HD]
        term[8 + i : 9 + i] = gain_two[:, i * HD : (i + 1) * HD]
    term_copies = []
    for n, device in enumerate(group_devices(z, h)[:1] + others):
        copy = rcopy(term, term_plane.at[n], term_send.at[n], term_recv.at[n], device)
        copy.start()
        term_copies.append(copy)
    gg = gy * gain[...]
    gv = rate * (gg - vr * jnp.mean(gg * vr, axis=-1, keepdims=True))
    ig[h] = (grad_hidden[...] + gv).astype(BF)
    ig_out = rcopy(ig.at[h], ig.at[h], ig_send.at[0], ig_recv.at[0], {"head": 1 - h})
    ig_out.start()
    dw1_sum[...] = dw1_out.total().astype(BF)
    copies1 = swap_ring(dw1_sum, ring1, z, ring_send, ring_recv)
    ring1[z] = dw1_sum[z]
    for copy in term_copies:
        copy.wait()
    for n in range(15):
        term[...] += term_plane[n]
    term_copies = []
    for n, device in enumerate(rings + [twin]):
        copy = rcopy(term, term_ring.at[n], term_send.at[15 + n], term_recv.at[15 + n], device)
        copy.start()
        term_copies.append(copy)
    for copy in copies1:
        copy.wait()
    twin_copy1 = rcopy(ring1, twin1, twin_send.at[0], twin_recv.at[0], twin)
    twin_copy1.start()
    for copy in twins:
        copy.wait()
    for out, a, b in ((go, dwo, two), (gg_, dwg, twg), (gd, dwd, twd)):
        out[...] = a[...].astype(F32) + b[...].astype(F32)
    for copy in term_copies:
        copy.wait()
    own_term = term[...]
    for n in range(7):
        own_term += term_ring[n]
    terms_out[...] = own_term
    twin_copy1.wait()
    g1[...] = ring1[...].astype(F32) + twin1[...].astype(F32)
    ig_out.wait()
    dw1_out.finish()
    norm_sum.finish()


def finish(dq, dkv, pre, normed, w1, gain, qgain, kgain, cosine, sine, tok, grad_hidden, dwo, dwg, dwd, gain_two):
    vmem = pl.BlockSpec(memory_space=pltpu.VMEM)
    return pl.pallas_call(
        finish_kernel,
        out_shape=(
            jax.ShapeDtypeStruct((2, HALF, D), BF),
            jax.ShapeDtypeStruct((4, 32, W1C), F32),
            jax.ShapeDtypeStruct((4, 32, 256), F32),
            jax.ShapeDtypeStruct((4, 32, 768), F32),
            jax.ShapeDtypeStruct((4, 32, 384), F32),
            jax.ShapeDtypeStruct((24, HD), F32),
        ),
        in_specs=[vmem] * 16,
        out_specs=(vmem,) * 6,
        scratch_shapes=[
            pltpu.VMEM((4 * CH, W1C), BF),
            pltpu.VMEM((4, 8, 32, W1C), BF),
            pltpu.VMEM((4, 32, W1C), BF),
            pltpu.VMEM((4, 32, W1C), BF),
            pltpu.VMEM((4, 32, W1C), BF),
            pltpu.VMEM((4, 32, 256), BF),
            pltpu.VMEM((4, 32, 768), BF),
            pltpu.VMEM((4, 32, 384), BF),
            pltpu.VMEM((24, HD), F32),
            pltpu.VMEM((15, 24, HD), F32),
            pltpu.VMEM((7, 24, HD), F32),
        ]
        + reduce_scratch()
        + plane_scratch(W1C)
        + [
            pltpu.SemaphoreType.DMA((11,)),
            pltpu.SemaphoreType.DMA((11,)),
            pltpu.SemaphoreType.DMA((4,)),
            pltpu.SemaphoreType.DMA((4,)),
            pltpu.SemaphoreType.DMA((4,)),
            pltpu.SemaphoreType.DMA((4,)),
            pltpu.SemaphoreType.DMA((1,)),
            pltpu.SemaphoreType.DMA((1,)),
            pltpu.SemaphoreType.DMA((22,)),
            pltpu.SemaphoreType.DMA((22,)),
        ],
        compiler_params=pltpu.CompilerParams(
            collective_id=4, has_side_effects=True, vmem_limit_bytes=VMEM_LIMIT
        ),
        name="finish",
    )(dq, dkv, pre, normed, w1, gain, qgain, kgain, cosine, sine, tok, grad_hidden, dwo, dwg, dwd, gain_two)


def on_device(
    tokens, segments, positions, cotangent, query_weight, key_weight, value_weight, out_weight,
    attn_gain, query_gain, key_gain, gate_weight, up_weight, down_weight, mlp_gain,
):
    t = lax.axis_index("ctx_1") * 4 + lax.axis_index("ctx_2")
    own_index = lax.axis_index(CTX) * CH + jnp.arange(CH, dtype=jnp.int32)
    start = jnp.max(jnp.where(segments[0] == 1, own_index - positions[0], 0))
    group = ((jnp.arange(4, dtype=jnp.int32) * 8 + t)[:, None] * CH + jnp.arange(CH, dtype=jnp.int32)).reshape(-1)
    begin = jnp.where(group < start, 0, jnp.where(group < start + MIDDLE, start, start + MIDDLE))
    inverse = ROPE_BASE ** (-jnp.arange(HD // 2, dtype=F32) / (HD // 2))
    angles = (group - begin).astype(F32)[:, None] * inverse[None, :]
    cosine, sine = jnp.cos(angles), jnp.sin(angles)
    cosine = jnp.concatenate([cosine, cosine], axis=1)
    sine = jnp.concatenate([-sine, sine], axis=1)

    def shards(w):
        return w.reshape(32, 4, -1)

    w1 = jnp.concatenate([shards(query_weight), shards(key_weight), shards(value_weight)], axis=2)
    wg = jnp.concatenate([shards(gate_weight), shards(up_weight)], axis=2)
    gains = jnp.concatenate([attn_gain, mlp_gain, jnp.zeros((64,), BF)]).astype(F32)
    gains = jnp.broadcast_to(gains[None], (8, 128))
    tok = tokens.reshape(2, HALF, D)
    tok_all, w1_all, gains_all = spread(tok, w1.transpose(1, 0, 2), gains)
    gain_one = gains_all[:, :, 0, :32].reshape(1, D)
    gain_two = gains_all[:, :, 0, 32:64].reshape(1, D)
    w1_all = w1_all.reshape(D, W1C)
    qgain, kgain = query_gain.astype(F32)[None], key_gain.astype(F32)[None]
    q, kv, pre, normed = make_heads(
        tok_all.reshape(4 * CH, D), w1_all, gain_one, qgain, kgain, cosine, sine
    )
    start = start.reshape(1, 1)
    att, out_t, logs, kv_all, cot_all, wo, wg, wd = attend(
        q,
        kv,
        cotangent.reshape(2, HALF, D),
        shards(out_weight.T).transpose(1, 0, 2),
        wg.transpose(1, 0, 2),
        shards(down_weight.T).transpose(1, 0, 2),
        start,
    )
    hidden, down_parts, grad_hidden, grad_att, dwo, dwg, dwd, gain_two_term = middle(
        att, wo, wg, wd, gain_two, tok, cot_all
    )
    dq, dkv, dwo, dwg, dwd, result = attend_back(
        q, kv_all, grad_att, out_t, logs, dwo.reshape(4, 8, 32, 256), dwg, dwd, hidden, down_parts, start
    )
    input_grad, g1, g_out, g_gu, g_down, terms = finish(
        dq, dkv, pre, normed, w1_all, gain_one, qgain, kgain, cosine, sine, tok, grad_hidden, dwo, dwg, dwd,
        gain_two_term,
    )
    terms = terms.reshape(-1)
    own = lax.axis_index(CTX) * 32

    def joined(g, a, b):
        return g[:, :, a:b].transpose(1, 0, 2).reshape(32, -1)

    return (
        result.reshape(1, CH, D),
        input_grad.reshape(1, CH, D),
        joined(g1, 0, 256),
        joined(g1, 256, 384),
        joined(g1, 384, 512),
        joined(g_out, 0, 256).T,
        lax.dynamic_slice(terms, (own,), (32,)),
        terms[2 * D : 2 * D + HD],
        terms[2 * D + HD : 2 * D + 2 * HD],
        joined(g_gu, 0, 384),
        joined(g_gu, 384, 768),
        joined(g_down, 0, 384).T,
        lax.dynamic_slice(terms, (D + own,), (32,)),
    )


def solution(mesh):
    torus = Mesh(
        mesh.devices.reshape(mesh.shape["rep"], 4, 2, 4, mesh.shape["head"]),
        ("rep", "ctx_0", "ctx_1", "ctx_2", "head"),
    )
    return jax.shard_map(
        on_device,
        mesh=torus,
        in_specs=(
            P("rep", CTX, None),
            P("rep", CTX),
            P("rep", CTX),
            P("rep", CTX, None),
            P(CTX, "head"),
            P(CTX, "head"),
            P(CTX, "head"),
            P("head", CTX),
            P(CTX),
            P(),
            P(),
            P(CTX, "head"),
            P(CTX, "head"),
            P("head", CTX),
            P(CTX),
        ),
        out_specs=(
            P("rep", CTX, None),
            P("rep", CTX, None),
            P(CTX, "head"),
            P(CTX, "head"),
            P(CTX, "head"),
            P("head", CTX),
            P(CTX),
            P(),
            P(),
            P(CTX, "head"),
            P(CTX, "head"),
            P("head", CTX),
            P(CTX),
        ),
        check_vma=False,
    )
```

```python
import math

import jax
import jax.numpy as jnp
from jax import lax
from jax.experimental import pallas as pl
from jax.experimental.pallas import tpu as pltpu
from jax.sharding import Mesh
from jax.sharding import PartitionSpec as P

MESH = pl.DeviceIdType.MESH
CTX = ("ctx_0", "ctx_1", "ctx_2")
EPSILON = 1e-06
ROPE_BASE = 1000000.0
BF = jnp.bfloat16
F32 = jnp.float32
HD = 128
D = 1024
CH = 192
HALF = 96
MIDDLE = 5952
W1C = 512
SCALE = 1.0 / math.sqrt(HD)
SCALE2 = SCALE / math.log(2.0)
VMEM_LIMIT = 56 * 1024 * 1024
PLANE = ((0, 1), (0, 3), (1, 0), (1, 1), (1, 3), (0, 2), (1, 2))
RING = (1, 3, 2)


def nn(a, b):
    return jnp.dot(a, b, preferred_element_type=F32)


def nt(a, b):
    return lax.dot_general(a, b, (((1,), (1,)), ((), ())), preferred_element_type=F32)


def tn(a, b):
    return lax.dot_general(a, b, (((0,), (0,)), ((), ())), preferred_element_type=F32)


def rcopy(src, dst, send, recv, device):
    return pltpu.make_async_remote_copy(
        src_ref=src, dst_ref=dst, send_sem=send, recv_sem=recv, device_id=device, device_id_type=MESH
    )


def place():
    return tuple(lax.axis_index(name) for name in ("ctx_0", "ctx_1", "ctx_2", "head"))


def ring_peer(z, k):
    return {"ctx_0": lax.rem(z + k, 4)}


def plane_peer(x, y, dx, dy):
    return {"ctx_1": lax.rem(x + dx, 2), "ctx_2": lax.rem(y + dy, 4)}


def greet(devices):
    barrier = pltpu.get_barrier_semaphore()
    for device in devices:
        pl.semaphore_signal(barrier, inc=1, device_id=device, device_id_type=MESH)
    pl.semaphore_wait(barrier, len(devices))


def group_devices(z, h):
    return [{"head": 1 - h}] + [ring_peer(z, k) for k in RING]


def plane_devices(x, y):
    return [plane_peer(x, y, dx, dy) for dx, dy in PLANE]


class Gather:
    def __init__(self, own, buf, z, h, sems):
        self.buf, self.z, self.h = buf, z, h
        self.sz, self.rz, self.ss, self.rs = sems
        self.sent = []
        self.from_core = {}
        self.ring = {}
        for k in RING:
            copy = rcopy(own, buf.at[z, h], self.sz.at[k], self.rz.at[k], ring_peer(z, k))
            copy.start()
            self.ring[k] = copy
            self.sent.append(copy)

    def to_core(self, k):
        source = lax.rem(self.z + 4 - k, 4)
        slot = self.buf.at[source, self.h]
        copy = rcopy(slot, slot, self.ss.at[k], self.rs.at[k], {"head": 1 - self.h})
        copy.start()
        self.from_core[k] = copy
        self.sent.append(copy)

    def forward(self, k):
        self.ring[k].wait_recv()
        self.to_core(k)

    def arrived(self, k):
        self.from_core[k].wait_recv()

    def finish(self):
        for copy in self.sent:
            copy.wait_send()


class Reduce:
    def __init__(self, parts, other, sums, inbox, z, h, sems):
        self.parts, self.other, self.sums, self.inbox, self.z, self.h = parts, other, sums, inbox, z, h
        self.ss, self.rs, self.sz, self.rz = sems
        self.sent = []
        self.core = {}
        self.ring = {}

    def give(self, k, value):
        chunk = lax.rem(self.z + k, 4)
        self.parts[chunk] = value.astype(BF).reshape(2, HALF, D)
        self.offer(k)

    def offer(self, k):
        chunk = lax.rem(self.z + k, 4)
        copy = rcopy(
            self.parts.at[chunk, 1 - self.h],
            self.other.at[chunk],
            self.ss.at[k],
            self.rs.at[k],
            {"head": 1 - self.h},
        )
        copy.start()
        self.core[k] = copy
        self.sent.append(copy)

    def pass_on(self, k):
        chunk = lax.rem(self.z + k, 4)
        self.core[k].wait_recv()
        both = self.parts[chunk, self.h].astype(F32) + self.other[chunk].astype(F32)
        self.sums[chunk] = both.astype(BF)
        copy = rcopy(
            self.sums.at[chunk],
            self.inbox.at[self.z],
            self.sz.at[k],
            self.rz.at[k],
            ring_peer(self.z, k),
        )
        copy.start()
        self.ring[k] = copy
        self.sent.append(copy)

    def total(self):
        self.core[0].wait_recv()
        result = self.parts[self.z, self.h].astype(F32) + self.other[self.z].astype(F32)
        for k in RING:
            self.ring[k].wait_recv()
            result += self.inbox[lax.rem(self.z + 4 - k, 4)].astype(F32)
        return result

    def finish(self):
        for copy in self.sent:
            copy.wait_send()


def reduce_scratch(parts=True):
    return [pltpu.VMEM((4, 2, HALF, D), BF)] * parts + [
        pltpu.VMEM((4, HALF, D), BF),
        pltpu.VMEM((4, HALF, D), BF),
        pltpu.VMEM((4, HALF, D), BF),
    ] + [pltpu.SemaphoreType.DMA((4,))] * 4


def gather_scratch():
    return [pltpu.SemaphoreType.DMA((4,))] * 4


def spread_kernel(
    tok, w1, gains, tok_all, w1_all, gains_all,
    w1_ring, gains_ring, local, ring_send, ring_recv, plane_send, plane_recv, *sems
):
    z, x, y, h = place()
    t = x * 4 + y
    greet(group_devices(z, h) + plane_neighbours(x, y))
    keep = [
        pltpu.make_async_copy(w1.at[z], w1_ring.at[z], local.at[0]),
        pltpu.make_async_copy(gains, gains_ring.at[z], local.at[1]),
        pltpu.make_async_copy(tok, tok_all.at[z], local.at[2]),
    ]
    for copy in keep:
        copy.start()
    ring = []
    for k in RING:
        peer = lax.rem(z + k, 4)
        pair = [
            rcopy(w1.at[peer], w1_ring.at[z], ring_send.at[0, k], ring_recv.at[0, k], ring_peer(z, k)),
            rcopy(gains, gains_ring.at[z], ring_send.at[1, k], ring_recv.at[1, k], ring_peer(z, k)),
        ]
        for copy in pair:
            copy.start()
        ring += pair
    tokens_out = Gather(tok.at[h], tok_all, z, h, sems)
    for copy in keep:
        copy.wait()
    for copy in ring:
        copy.wait_recv()
    plane = [
        PlaneGather(w1_ring, w1_all, x, y, plane_send.at[0], plane_recv.at[0]),
        PlaneGather(gains_ring, gains_all, x, y, plane_send.at[1], plane_recv.at[1]),
    ]
    keep = [
        pltpu.make_async_copy(w1_ring, w1_all.at[:, t], local.at[3]),
        pltpu.make_async_copy(gains_ring, gains_all.at[:, t], local.at[4]),
    ]
    for copy in keep:
        copy.start()
    for item in plane:
        item.relay()
    for k in RING:
        tokens_out.forward(k)
    for k in RING:
        tokens_out.arrived(k)
    for copy in ring:
        copy.wait_send()
    for item in plane:
        item.arrived()
        item.finish()
    tokens_out.finish()
    for copy in keep:
        copy.wait()


def spread(tok, w1, gains):
    any_ = pl.BlockSpec(memory_space=pl.ANY)
    return pl.pallas_call(
        spread_kernel,
        out_shape=(
            jax.ShapeDtypeStruct((4, 2, HALF, D), BF),
            jax.ShapeDtypeStruct((4, 8, 32, W1C), BF),
            jax.ShapeDtypeStruct((4, 8, 8, 128), F32),
        ),
        in_specs=[any_] * 3,
        out_specs=(any_,) * 3,
        scratch_shapes=[
            pltpu.VMEM((4, 32, W1C), BF),
            pltpu.VMEM((4, 8, 128), F32),
            pltpu.SemaphoreType.DMA((5,)),
            pltpu.SemaphoreType.DMA((2, 4)),
            pltpu.SemaphoreType.DMA((2, 4)),
            pltpu.SemaphoreType.DMA((2, 11)),
            pltpu.SemaphoreType.DMA((2, 11)),
        ]
        + gather_scratch(),
        compiler_params=pltpu.CompilerParams(
            collective_id=0, has_side_effects=True, vmem_limit_bytes=VMEM_LIMIT
        ),
        name="spread",
    )(tok, w1, gains)


def swap_ring(source, ring, z, send, recv):
    copies = []
    for k in RING:
        copy = rcopy(source.at[lax.rem(z + k, 4)], ring.at[z], send.at[k], recv.at[k], ring_peer(z, k))
        copy.start()
        copies.append(copy)
    return copies


TURNS = (1, 3, 2)


def beside(x, y):
    along = [{"ctx_2": lax.rem(y + dy, 4)} for dy in TURNS]
    return along, {"ctx_1": 1 - x}, {"ctx_1": 1 - x, "rep": 1 - lax.axis_index("rep")}


def plane_neighbours(x, y):
    along, near, far = beside(x, y)
    return along + [near, far]


class PlaneGather:
    def __init__(self, source, buf, x, y, send, recv):
        self.buf, self.x, self.y, self.send, self.recv = buf, x, y, send, recv
        along, self.near, self.far = beside(x, y)
        self.down = []
        self.over = []
        slot = buf.at[:, x * 4 + y]
        for j in range(3):
            copy = rcopy(source, slot, send.at[j], recv.at[j], along[j])
            copy.start()
            self.down.append(copy)
        self.across(0, source, slot)

    def across(self, j, source, slot):
        for a, device in ((0, self.near), (1, self.far)):
            part = pl.ds(2 * a, 2)
            n = 3 + 2 * j + a
            copy = rcopy(source.at[part], slot.at[part], self.send.at[n], self.recv.at[n], device)
            copy.start()
            self.over.append(copy)

    def relay(self):
        for j, dy in enumerate(TURNS):
            self.down[j].wait_recv()
            slot = self.buf.at[:, self.x * 4 + lax.rem(self.y + 4 - dy, 4)]
            self.across(j + 1, slot, slot)

    def arrived(self):
        for copy in self.over:
            copy.wait_recv()

    def finish(self):
        for copy in self.down + self.over:
            copy.wait_send()


class PlaneReduce:
    def __init__(self, parts, inx, col, iny, x, y, send, recv):
        self.parts, self.inx, self.col, self.iny = parts, inx, col, iny
        self.x, self.y, self.send, self.recv = x, y, send, recv
        self.along, near, far = beside(x, y)
        self.over = []
        self.down = []
        for j, dy in enumerate(TURNS + (0,)):
            row = lax.rem(y + dy, 4)
            for a, device in ((0, near), (1, far)):
                part = pl.ds(2 * a, 2)
                copy = rcopy(
                    parts.at[part, (1 - x) * 4 + row],
                    inx.at[part, row],
                    send.at[2 * j + a],
                    recv.at[2 * j + a],
                    device,
                )
                copy.start()
                self.over.append(copy)

    def joined(self, j, row):
        self.over[2 * j].wait_recv()
        self.over[2 * j + 1].wait_recv()
        return self.parts[:, self.x * 4 + row].astype(F32) + self.inx[:, row].astype(F32)

    def relay(self):
        for j, dy in enumerate(TURNS):
            row = lax.rem(self.y + dy, 4)
            self.col[:, row] = self.joined(j, row).astype(BF)
            copy = rcopy(
                self.col.at[:, row], self.iny.at[j], self.send.at[8 + j], self.recv.at[8 + j], self.along[j]
            )
            copy.start()
            self.down.append(copy)

    def total(self):
        result = self.joined(3, self.y)
        for j in range(3):
            self.down[j].wait_recv()
            result += self.iny[j].astype(F32)
        return result

    def finish(self):
        for copy in self.down + self.over:
            copy.wait_send()


def plane_scratch(width):
    return [
        pltpu.VMEM((4, 4, 32, width), BF),
        pltpu.VMEM((4, 4, 32, width), BF),
        pltpu.VMEM((3, 4, 32, width), BF),
    ]


def turn(u, cosine, sine):
    return u * cosine + pltpu.roll(u, HD // 2, 1) * sine


def joined_gain(gains, first):
    return jnp.concatenate(
        [gains[c // 8, c % 8, 0:1, first : first + 32] for c in range(32)], axis=1
    )


def rms_rate(v):
    return lax.rsqrt(jnp.mean(v * v, axis=-1, keepdims=True) + EPSILON)


def heads_kernel(tok, w1, gains, qgain, kgain, cosine, sine, q, kv, pre, normed):
    v = tok[...].astype(F32)
    n = (v * rms_rate(v) * joined_gain(gains, 0)).astype(BF)
    normed[...] = n
    out = nn(n, w1[...])
    pre[...] = out[:, :384]
    c, s = cosine[...], sine[...]
    for i in range(3):
        u = out[:, i * HD : (i + 1) * HD]
        u = turn(u * rms_rate(u) * (qgain if i < 2 else kgain)[...], c, s).astype(BF)
        if i < 2:
            q[0, i * CH : (i + 1) * CH, :] = u
        else:
            kv[0, :, :HD] = u
    kv[0, :, HD:] = out[:, 384:].astype(BF)


def make_heads(tok_all, w1, gains, qgain, kgain, cosine, sine):
    def whole(*shape):
        return pl.BlockSpec(shape, lambda i: (0,) * len(shape))

    return pl.pallas_call(
        heads_kernel,
        grid=(4,),
        out_shape=(
            jax.ShapeDtypeStruct((4, 2 * CH, HD), BF),
            jax.ShapeDtypeStruct((4, CH, 2 * HD), BF),
            jax.ShapeDtypeStruct((4 * CH, 384), F32),
            jax.ShapeDtypeStruct((4 * CH, D), BF),
        ),
        in_specs=[
            pl.BlockSpec((CH, D), lambda i: (i, 0)),
            whole(D, W1C),
            whole(4, 8, 8, HD),
            whole(1, HD),
            whole(1, HD),
            pl.BlockSpec((CH, HD), lambda i: (i, 0)),
            pl.BlockSpec((CH, HD), lambda i: (i, 0)),
        ],
        out_specs=(
            pl.BlockSpec((1, 2 * CH, HD), lambda i: (i, 0, 0)),
            pl.BlockSpec((1, CH, 2 * HD), lambda i: (i, 0, 0)),
            pl.BlockSpec((CH, 384), lambda i: (i, 0)),
            pl.BlockSpec((CH, D), lambda i: (i, 0)),
        ),
        compiler_params=pltpu.CompilerParams(vmem_limit_bytes=VMEM_LIMIT),
        name="make_heads",
    )(tok_all, w1, gains, qgain, kgain, cosine, sine)


def query_index(chunk):
    lane = lax.broadcasted_iota(jnp.int32, (1, 2 * CH), 1)
    return chunk * CH + jnp.where(lane < CH, lane, lane - CH)


def first_allowed(index, start):
    return jnp.where(index < start, 0, jnp.where(index < start + MIDDLE, start, start + MIDDLE))


def key_index(chunk):
    return chunk * CH + lax.broadcasted_iota(jnp.int32, (CH, 1), 0)


def row_sums(p):
    return jnp.sum(p.reshape(CH // 8, 8, 2 * CH), axis=0)


def attend_kernel(
    q, kv, cot, wo, wg, wd, start_ref, att, out_t, logs, kv_all, cot_all, wo_all, wg_ring, wd_ring,
    acc, den, own_acc, own_den, wo_ring, wo_send, wo_recv, local, kv_send, kv_recv, ring_send, ring_recv, *sems
):
    z, x, y, h = place()
    t = x * 4 + y
    greet(group_devices(z, h) + plane_neighbours(x, y))
    along, near, _ = beside(x, y)

    def send(n, source, slot, device):
        copy = rcopy(source, slot, kv_send.at[n], kv_recv.at[n], device)
        copy.start()
        return copy

    copies = [send(n, kv, kv_all.at[:, t], device) for n, device in enumerate(along + [near])]
    cot_out = Gather(cot.at[h], cot_all, z, h, sems)
    weights = []
    keep = [pltpu.make_async_copy(cot, cot_all.at[z], local.at[3])]
    for i, (source, ring) in enumerate(((wo, wo_ring), (wg, wg_ring), (wd, wd_ring))):
        weights += swap_ring(source, ring, z, ring_send.at[i], ring_recv.at[i])
        keep.append(pltpu.make_async_copy(source.at[z], ring.at[z], local.at[i]))
    for copy in keep:
        copy.start()
    kv_all[:, t] = kv[...]
    start = start_ref[0, 0]
    acc[...] = jnp.zeros_like(acc)
    den[...] = jnp.zeros_like(den)

    def block(c, other, qc, late):
        p = jnp.exp2(nt(kv_all[c, other, :, :HD], qc) * SCALE2)
        if c == 0:
            p = jnp.where(late, p, 0.0)
        return tn(kv_all[c, other, :, HD:], p.astype(BF)), row_sums(p)

    def visit(other, own=False):
        late = key_index(other) >= start
        for c in range(4):
            if c > 0:
                a, d = block(0, other, q[c], late)
                for earlier in range(1, c):
                    aa, dd = block(earlier, other, q[c], late)
                    a += aa
                    d += dd
                acc[c] += a
                den[c] += d
            if not own:

                @pl.when(other < t)
                def _():
                    a, d = block(c, other, q[c], late)
                    acc[c] += a
                    den[c] += d

    for c in range(4):
        mine = c * 8 + t
        index = query_index(mine)
        last = key_index(mine)
        p = jnp.exp2(nt(kv[c, :, :HD], q[c]) * SCALE2)
        p = jnp.where((last <= index) & (last >= first_allowed(index, start)), p, 0.0)
        own_acc[c] = tn(kv[c, :, HD:], p.astype(BF))
        own_den[c] = row_sums(p)
    visit(t, True)
    rows = [lax.rem(y + 4 - dy, 4) for dy in TURNS]
    halves = (pl.ds(0, 2), pl.ds(2, 2))

    def over(j):
        copies[j].wait_recv()
        slot = kv_all.at[halves[0], x * 4 + rows[j]]
        copies.append(send(4 + j, slot, slot, near))

    over(0)
    over(1)
    copies[3].wait_recv()
    across = (1 - x) * 4 + y
    slot = kv_all.at[halves[1], across]
    for j in range(3):
        copies.append(send(7 + j, slot, slot, along[j]))
    for copy in weights[:3]:
        copy.wait_recv()
    keep[1].wait()
    wo_in = PlaneGather(wo_ring, wo_all, x, y, wo_send, wo_recv)
    visit(x * 4 + rows[0])
    visit(x * 4 + rows[1])
    over(2)
    visit(across)
    visit(x * 4 + rows[2])
    wo_in.relay()
    wo_all[:, t] = wo_ring[...]
    relayed = {0: (4, 6), 1: (5, 7), 2: (9, 8)}
    for k in RING:
        cot_out.forward(k)
    for j in range(3):
        for n in relayed[j]:
            copies[n].wait_recv()
        visit((1 - x) * 4 + rows[j])
    for c in range(4):
        inside = (query_index(c * 8 + t) < start + MIDDLE).astype(F32)
        denominator = jnp.sum(den[c] * inside + own_den[c], axis=0, keepdims=True)
        total = (acc[c] * inside + own_acc[c]) / denominator
        out_t[c] = total
        logs[c] = jnp.log2(denominator)
        full = total.T.astype(BF)
        att[c, :, :HD] = full[:CH]
        att[c, :, HD:] = full[CH:]
    for copy in copies:
        copy.wait_send()
    for k in RING:
        cot_out.arrived(k)
    cot_out.finish()
    wo_in.arrived()
    wo_in.finish()
    for copy in weights[:3]:
        copy.wait_send()
    for copy in weights[3:] + keep[:1] + keep[2:]:
        copy.wait()


def attend(q, kv, cot, wo, wg, wd, start):
    any_ = pl.BlockSpec(memory_space=pl.ANY)
    vmem = pl.BlockSpec(memory_space=pltpu.VMEM)
    smem = pl.BlockSpec(memory_space=pltpu.SMEM)
    return pl.pallas_call(
        attend_kernel,
        out_shape=(
            jax.ShapeDtypeStruct((4, CH, 2 * HD), BF),
            jax.ShapeDtypeStruct((4, HD, 2 * CH), F32),
            jax.ShapeDtypeStruct((4, 1, 2 * CH), F32),
            jax.ShapeDtypeStruct((4, 8, CH, 2 * HD), BF),
            jax.ShapeDtypeStruct((4, 2, HALF, D), BF),
            jax.ShapeDtypeStruct((4, 8, 32, 256), BF),
            jax.ShapeDtypeStruct((4, 32, 768), BF),
            jax.ShapeDtypeStruct((4, 32, 384), BF),
        ),
        in_specs=[vmem, vmem, any_, any_, any_, any_, smem],
        out_specs=(vmem, vmem, vmem, vmem, any_, vmem, any_, any_),
        scratch_shapes=[
            pltpu.VMEM((4, HD, 2 * CH), F32),
            pltpu.VMEM((4, 8, 2 * CH), F32),
            pltpu.VMEM((4, HD, 2 * CH), F32),
            pltpu.VMEM((4, 8, 2 * CH), F32),
            pltpu.VMEM((4, 32, 256), BF),
            pltpu.SemaphoreType.DMA((11,)),
            pltpu.SemaphoreType.DMA((11,)),
            pltpu.SemaphoreType.DMA((4,)),
            pltpu.SemaphoreType.DMA((10,)),
            pltpu.SemaphoreType.DMA((10,)),
            pltpu.SemaphoreType.DMA((3, 4)),
            pltpu.SemaphoreType.DMA((3, 4)),
        ]
        + gather_scratch(),
        compiler_params=pltpu.CompilerParams(
            collective_id=1, has_side_effects=True, vmem_limit_bytes=VMEM_LIMIT
        ),
        name="attend",
    )(q, kv, cot, wo, wg, wd, start)


def middle_kernel(
    att, wo_all, wg_ring, wd_ring, gains, tok, cot_all,
    hidden, down_parts, grad_hidden, grad_att, dwo, dwg_sum, dwd, gain_term,
    n2, gh, act, ggu, wg_all, wd_all, dwg, *scratch,
):
    first = scratch[0:8]
    back = scratch[8:16]
    fwd_sems = scratch[16:20]
    bwd_sems = scratch[20:24]
    dwg_buf = scratch[24:27]
    w_send, w_recv = scratch[27:29]
    z, x, y, h = place()
    t = x * 4 + y
    greet(group_devices(z, h) + plane_neighbours(x, y))
    wg_all[:, t] = wg_ring[...]
    wd_all[:, t] = wd_ring[...]
    wg_in = PlaneGather(wg_ring, wg_all, x, y, w_send.at[1], w_recv.at[1])
    wd_in = PlaneGather(wd_ring, wd_all, x, y, w_send.at[2], w_recv.at[2])
    out_sum = Reduce(*first[:4], z, h, first[4:])
    for k in (1, 3, 2, 0):
        out_sum.give(k, nt(att[lax.rem(z + k, 4)], wo_all[...].reshape(D, 256)))
    for k in RING:
        out_sum.pass_on(k)
    wg_in.relay()
    v = tok[h].astype(F32) + out_sum.total()
    hidden[...] = v
    g = joined_gain(gains, 32)
    rate = rms_rate(v)
    n2[z, h] = (v * rate * g).astype(BF)
    n2_out = Gather(n2.at[z, h], n2, z, h, fwd_sems)
    n2_out.to_core(0)
    wd_in.relay()
    back_sum = Reduce(*back[:4], z, h, back[4:])

    def feed(k):
        chunk = lax.rem(z + 4 - k, 4)
        back_k = (4 - k) % 4
        rows = n2[chunk].reshape(CH, D)
        gu = nn(rows, wg_all[...].reshape(D, 768))
        if k == 0:
            wd_in.arrived()
        ga = nn(cot_all[chunk].reshape(CH, D), wd_all[...].reshape(D, 384))
        gate, up = gu[:, :384], gu[:, 384:]
        s = 1.0 / (1.0 + jnp.exp(-gate))
        silu = gate * s
        a = (silu * up).astype(BF)
        act[chunk] = a
        gg = (ga * up * s * (1.0 + gate * (1.0 - s))).astype(BF)
        gp = (ga * silu).astype(BF)
        ggu[chunk, :, :384] = gg
        ggu[chunk, :, 384:] = gp
        back_sum.give(back_k, nt(ggu[chunk], wg_all[...].reshape(D, 768)))
        down_parts[chunk] = nt(a, wd_all[...].reshape(D, 384)).astype(BF).reshape(2, HALF, D)

    n2_out.arrived(0)
    wg_in.arrived()
    feed(0)
    n2_out.forward(1)
    n2_out.forward(3)
    n2_out.arrived(1)
    feed(1)
    n2_out.forward(2)
    n2_out.arrived(3)
    back_sum.pass_on(3)
    feed(3)
    back_sum.pass_on(1)
    n2_out.arrived(2)
    feed(2)
    back_sum.pass_on(2)
    dwg[...] = (
        tn(n2[...].reshape(4 * CH, D), ggu[...].reshape(4 * CH, 768)).astype(BF).reshape(4, 8, 32, 768)
    )
    dwg_out = PlaneReduce(dwg, *dwg_buf, x, y, w_send.at[3], w_recv.at[3])
    gy = back_sum.total()
    v = hidden[...]
    rate = rms_rate(v)
    vr = v * rate
    gain_term[...] = jnp.sum(gy * vr, axis=0, keepdims=True)
    gg = gy * g
    gv = rate * (gg - vr * jnp.mean(gg * vr, axis=-1, keepdims=True))
    grad = cot_all[z, h].astype(F32) + gv
    grad_hidden[...] = grad
    gh[z, h] = grad.astype(BF)
    gh_out = Gather(gh.at[z, h], gh, z, h, bwd_sems)
    gh_out.to_core(0)
    dwd[...] = (
        tn(cot_all[...].reshape(4 * CH, D), act[...].reshape(4 * CH, 384)).astype(BF).reshape(4, 8, 32, 384)
    )
    for k in RING:
        gh_out.forward(k)
    dwg_out.relay()
    for k in range(4):
        gh_out.arrived(k)
    full = gh[...].reshape(4 * CH, D)
    ga = nn(full, wo_all[...].reshape(D, 256)).astype(BF)
    for c in range(4):
        for i in range(2):
            grad_att[c, i * CH : (i + 1) * CH, :] = ga[c * CH : (c + 1) * CH, i * HD : (i + 1) * HD]
    dwo[...] = tn(full, att[...].reshape(4 * CH, 256)).astype(BF)
    dwg_sum[...] = dwg_out.total().astype(BF)
    for item in (out_sum, back_sum, n2_out, gh_out, wg_in, wd_in, dwg_out):
        item.finish()


def middle(att, wo, wg, wd, gains, tok, cot_all):
    vmem = pl.BlockSpec(memory_space=pltpu.VMEM)
    return pl.pallas_call(
        middle_kernel,
        out_shape=(
            jax.ShapeDtypeStruct((HALF, D), F32),
            jax.ShapeDtypeStruct((4, 2, HALF, D), BF),
            jax.ShapeDtypeStruct((HALF, D), F32),
            jax.ShapeDtypeStruct((4, 2 * CH, HD), BF),
            jax.ShapeDtypeStruct((D, 256), BF),
            jax.ShapeDtypeStruct((4, 32, 768), BF),
            jax.ShapeDtypeStruct((4, 8, 32, 384), BF),
            jax.ShapeDtypeStruct((1, D), F32),
        ),
        in_specs=[vmem] * 7,
        out_specs=(vmem,) * 8,
        scratch_shapes=[
            pltpu.VMEM((4, 2, HALF, D), BF),
            pltpu.VMEM((4, 2, HALF, D), BF),
            pltpu.VMEM((4, CH, 384), BF),
            pltpu.VMEM((4, CH, 768), BF),
            pltpu.VMEM((4, 8, 32, 768), BF),
            pltpu.VMEM((4, 8, 32, 384), BF),
            pltpu.VMEM((4, 8, 32, 768), BF),
        ]
        + reduce_scratch() * 2
        + gather_scratch() * 2
        + plane_scratch(768)
        + [pltpu.SemaphoreType.DMA((4, 11))] * 2,
        compiler_params=pltpu.CompilerParams(
            collective_id=2, has_side_effects=True, vmem_limit_bytes=VMEM_LIMIT
        ),
        name="middle",
    )(att, wo, wg, wd, gains, tok, cot_all)


def attend_back_kernel(
    q, kv_all, go, out_t, logs, dwo, dwg, dwd, hidden, down_parts, start_ref,
    dq, dkv, dwo_ring, dwg_ring, dwd_ring, res,
    dq_t, delta, far, acc, give_b, take_b, give_a, take_a, give_c, take_c, give_d, take_d, dwo_sum, dwd_sum, *scratch,
):
    dwo_buf = scratch[:3]
    dwd_buf = scratch[3:6]
    down = scratch[6:13]
    kv_send, kv_recv, w_send, w_recv, r_send, r_recv, res_send, res_recv = scratch[13:]
    z, x, y, h = place()
    t = x * 4 + y
    greet(group_devices(z, h) + plane_neighbours(x, y))
    along, near, _ = beside(x, y)
    down_sum = Reduce(down_parts, *down[:3], z, h, down[3:])
    for k in (1, 3, 2, 0):
        down_sum.offer(k)
    dwo_out = PlaneReduce(dwo, *dwo_buf, x, y, w_send.at[0], w_recv.at[0])
    dwd_out = PlaneReduce(dwd, *dwd_buf, x, y, w_send.at[1], w_recv.at[1])
    rings = swap_ring(dwg, dwg_ring, z, r_send.at[1], r_recv.at[1])
    dwg_ring[z] = dwg[z]
    start = start_ref[0, 0]
    dq_t[...] = jnp.zeros_like(dq_t)
    for c in range(4):
        delta[c] = jnp.sum(out_t[c] * go[c].astype(F32).T, axis=0, keepdims=True)
        far[c] = jnp.where(query_index(c * 8 + t) < start + MIDDLE, logs[c], 1e30)

    def pair(c, k, v, log, keep):
        qc, g = q[c], go[c]
        p = jnp.exp2(nt(k, qc) * SCALE2 - log)
        if keep is not None:
            p = jnp.where(keep, p, 0.0)
        ds = (p * (nt(v, g) - delta[c])).astype(BF)
        dq_t[c] += tn(k, ds)
        return nn(ds, qc), nn(p.astype(BF), g)

    def keys_of(other, chunks, own=False):
        result = []
        for c in chunks:
            both = kv_all[c, other]
            k, v = both[:, :HD], both[:, HD:]
            index = key_index(c * 8 + other)
            late = index >= start if c == 0 else None
            if own:
                mine = query_index(c * 8 + t)
                keep = (index <= mine) & (index >= first_allowed(mine, start))
                dk, dv = pair(c, k, v, logs[c], keep)
                acc[:, :HD] = dk
                acc[:, HD:] = dv
            else:
                acc[...] = jnp.zeros_like(acc)

                @pl.when(other < t)
                def _():
                    dk, dv = pair(c, k, v, far[c], late)
                    acc[:, :HD] = dk
                    acc[:, HD:] = dv

            dk, dv = acc[:, :HD], acc[:, HD:]
            for later in range(c + 1, 4):
                a, b = pair(later, k, v, far[later], late)
                dk += a
                dv += b
            result.append((dk * SCALE, dv))
        return result

    sent = []

    def send(n, source, slot, device):
        copy = rcopy(source, slot, kv_send.at[n], kv_recv.at[n], device)
        copy.start()
        sent.append(copy)

    def put(ref, values):
        for i, (dk, dv) in enumerate(values):
            ref[i, :, :HD] = dk.astype(BF)
            ref[i, :, HD:] = dv.astype(BF)

    rows = [lax.rem(y + dy, 4) for dy in TURNS]
    for j in range(3):
        for i, column in enumerate((x, 1 - x)):
            put(give_b.at[j, i], keys_of(column * 4 + rows[j], (2, 3)))
        send(j, give_b.at[j], take_b.at[j], along[j])
    for k in RING:
        down_sum.pass_on(k)
    for j, row in enumerate(rows + [y]):
        put(give_a.at[j], keys_of((1 - x) * 4 + row, (0, 1)))
        send(3 + j, give_a.at[j], take_a.at[j], near)
    dwo_out.relay()
    dwd_out.relay()
    res[h] = (hidden[...] + down_sum.total()).astype(BF)
    res_out = rcopy(res.at[h], res.at[h], res_send.at[0], res_recv.at[0], {"head": 1 - h})
    res_out.start()
    dwo_sum[...] = dwo_out.total().astype(BF)
    rings += swap_ring(dwo_sum, dwo_ring, z, r_send.at[0], r_recv.at[0])
    dwo_ring[z] = dwo_sum[z]
    dwd_sum[...] = dwd_out.total().astype(BF)
    rings += swap_ring(dwd_sum, dwd_ring, z, r_send.at[2], r_recv.at[2])
    dwd_ring[z] = dwd_sum[z]

    def add(values, *others):
        result = []
        for i, (dk, dv) in enumerate(values):
            for other in others:
                both = other[i].astype(F32)
                dk += both[:, :HD]
                dv += both[:, HD:]
            result.append((dk, dv))
        return result

    for j in range(3):
        values = keys_of(x * 4 + rows[j], (0, 1))
        sent[3 + j].wait_recv()
        put(give_c.at[j], add(values, take_a.at[j]))
        send(7 + j, give_c.at[j], take_c.at[j], along[j])
    values = keys_of((1 - x) * 4 + y, (2, 3))
    for j in range(3):
        sent[j].wait_recv()
    put(give_d, add(values, *(take_b.at[j, 1] for j in range(3))))
    send(10, give_d, take_d, near)
    low = keys_of(t, (0, 1), True)
    high = keys_of(t, (2, 3), True)
    for c in range(4):
        dq[c] = (dq_t[c] * SCALE).T
    sent[6].wait_recv()
    low = add(low, take_a.at[3])
    high = add(high, *(take_b.at[j, 0] for j in range(3)))
    for j in range(3):
        sent[7 + j].wait_recv()
    sent[10].wait_recv()
    low = add(low, *(take_c.at[j] for j in range(3)))
    high = add(high, take_d)
    for c, (dk, dv) in enumerate(low + high):
        dkv[c, :, :HD] = dk
        dkv[c, :, HD:] = dv
    for copy in rings:
        copy.wait()
    res_out.wait()
    for copy in sent:
        copy.wait_send()
    dwo_out.finish()
    dwd_out.finish()
    down_sum.finish()


def attend_back(q, kv_all, go, out_t, logs, dwo, dwg, dwd, hidden, down_parts, start):
    vmem = pl.BlockSpec(memory_space=pltpu.VMEM)
    smem = pl.BlockSpec(memory_space=pltpu.SMEM)
    return pl.pallas_call(
        attend_back_kernel,
        out_shape=(
            jax.ShapeDtypeStruct((4, 2 * CH, HD), F32),
            jax.ShapeDtypeStruct((4, CH, 2 * HD), F32),
            jax.ShapeDtypeStruct((4, 32, 256), BF),
            jax.ShapeDtypeStruct((4, 32, 768), BF),
            jax.ShapeDtypeStruct((4, 32, 384), BF),
            jax.ShapeDtypeStruct((2, HALF, D), BF),
        ),
        in_specs=[vmem] * 10 + [smem],
        out_specs=(vmem,) * 6,
        scratch_shapes=[
            pltpu.VMEM((4, HD, 2 * CH), F32),
            pltpu.VMEM((4, 1, 2 * CH), F32),
            pltpu.VMEM((4, 1, 2 * CH), F32),
            pltpu.VMEM((CH, 2 * HD), F32),
            pltpu.VMEM((3, 2, 2, CH, 2 * HD), BF),
            pltpu.VMEM((3, 2, 2, CH, 2 * HD), BF),
            pltpu.VMEM((4, 2, CH, 2 * HD), BF),
            pltpu.VMEM((4, 2, CH, 2 * HD), BF),
            pltpu.VMEM((3, 2, CH, 2 * HD), BF),
            pltpu.VMEM((3, 2, CH, 2 * HD), BF),
            pltpu.VMEM((2, CH, 2 * HD), BF),
            pltpu.VMEM((2, CH, 2 * HD), BF),
            pltpu.VMEM((4, 32, 256), BF),
            pltpu.VMEM((4, 32, 384), BF),
        ]
        + plane_scratch(256)
        + plane_scratch(384)
        + reduce_scratch(False)
        + [
            pltpu.SemaphoreType.DMA((11,)),
            pltpu.SemaphoreType.DMA((11,)),
            pltpu.SemaphoreType.DMA((2, 11)),
            pltpu.SemaphoreType.DMA((2, 11)),
            pltpu.SemaphoreType.DMA((3, 4)),
            pltpu.SemaphoreType.DMA((3, 4)),
            pltpu.SemaphoreType.DMA((1,)),
            pltpu.SemaphoreType.DMA((1,)),
        ],
        compiler_params=pltpu.CompilerParams(
            collective_id=3, has_side_effects=True, vmem_limit_bytes=VMEM_LIMIT
        ),
        name="attend_back",
    )(q, kv_all, go, out_t, logs, dwo, dwg, dwd, hidden, down_parts, start)


def finish_kernel(
    dq, dkv, pre, normed, w1, gains, qgain, kgain, cosine, sine, tok, grad_hidden, dwo, dwg, dwd,
    gain_two, ig, ring1, twin1, two, twg, twd, terms_out,
    dpre, dw1, dw1_sum, term, term_plane, term_ring, *scratch,
):
    sums = scratch[0:8]
    dw1_buf = scratch[8:11]
    plane_send, plane_recv, ring_send, ring_recv, twin_send, twin_recv, ig_send, ig_recv, term_send, term_recv = scratch[11:]
    z, x, y, h = place()
    t = x * 4 + y
    twin = {"rep": 1 - lax.axis_index("rep")}
    others = [{"head": h_, **device} for device in plane_devices(x, y) for h_ in (h, 1 - h)]
    rings = [{**ring_peer(z, k), **r} for k in RING for r in ({}, twin)]
    greet(group_devices(z, h)[:1] + others + rings + [twin, beside(x, y)[2]])

    twins = []
    for i, (source, other) in enumerate(((dwo, two), (dwg, twg), (dwd, twd))):
        copy = rcopy(source, other, twin_send.at[i], twin_recv.at[i], twin)
        copy.start()
        twins.append(copy)
    c_, s_ = cosine[...], sine[...]
    heads = []
    for i in range(2):
        heads.append(jnp.concatenate([dq[c, i * CH : (i + 1) * CH, :] for c in range(4)], axis=0))
    heads.append(dkv[...].reshape(4 * CH, 2 * HD)[:, :HD])
    terms = []
    for i, dy in enumerate(heads):
        gy = turn(dy, c_, -s_)
        v = pre[:, i * HD : (i + 1) * HD]
        rate = rms_rate(v)
        vr = v * rate
        terms.append(jnp.sum(gy * vr, axis=0, keepdims=True))
        gg = gy * (qgain if i < 2 else kgain)[...]
        out = rate * (gg - vr * jnp.mean(gg * vr, axis=-1, keepdims=True))
        dpre[:, i * HD : (i + 1) * HD] = out.astype(BF)
    dpre[:, 3 * HD :] = dkv[...].reshape(4 * CH, 2 * HD)[:, HD:].astype(BF)
    term[...] = jnp.zeros_like(term)
    term[16:17] = terms[0] + terms[1]
    term[17:18] = terms[2]
    dw1[...] = tn(normed[...], dpre[...]).astype(BF).reshape(4, 8, 32, W1C)
    dw1_out = PlaneReduce(dw1, *dw1_buf, x, y, plane_send, plane_recv)
    norm_sum = Reduce(*sums[:4], z, h, sums[4:])
    for k in (1, 3, 2, 0):
        chunk = lax.rem(z + k, 4)
        norm_sum.give(k, nt(dpre[pl.ds(pl.multiple_of(chunk * CH, CH), CH), :], w1[...]))
    for k in RING:
        norm_sum.pass_on(k)
    dw1_out.relay()
    gy = norm_sum.total()
    v = tok[h].astype(F32)
    rate = rms_rate(v)
    vr = v * rate
    own_term = jnp.sum(gy * vr, axis=0, keepdims=True)
    for i in range(8):
        term[i : i + 1] = own_term[:, i * HD : (i + 1) * HD]
        term[8 + i : 9 + i] = gain_two[:, i * HD : (i + 1) * HD]
    term_copies = []
    for n, device in enumerate(group_devices(z, h)[:1] + others):
        copy = rcopy(term, term_plane.at[n], term_send.at[n], term_recv.at[n], device)
        copy.start()
        term_copies.append(copy)
    gg = gy * joined_gain(gains, 0)
    gv = rate * (gg - vr * jnp.mean(gg * vr, axis=-1, keepdims=True))
    ig[h] = (grad_hidden[...] + gv).astype(BF)
    ig_out = rcopy(ig.at[h], ig.at[h], ig_send.at[0], ig_recv.at[0], {"head": 1 - h})
    ig_out.start()
    dw1_sum[...] = dw1_out.total().astype(BF)
    copies1 = swap_ring(dw1_sum, ring1, z, ring_send, ring_recv)
    for k in range(4):
        copy = rcopy(
            dw1_sum.at[lax.rem(z + k, 4)],
            twin1.at[z],
            twin_send.at[3 + k],
            twin_recv.at[3 + k],
            {**ring_peer(z, k), **twin},
        )
        copy.start()
        copies1.append(copy)
    ring1[z] = dw1_sum[z]
    for copy in term_copies:
        copy.wait()
    for n in range(15):
        term[...] += term_plane[n]
    term_copies = []
    for n, device in enumerate(rings + [twin]):
        copy = rcopy(term, term_ring.at[n], term_send.at[15 + n], term_recv.at[15 + n], device)
        copy.start()
        term_copies.append(copy)
    for copy in twins:
        copy.wait()
    for copy in term_copies:
        copy.wait()
    own_term = term[...]
    for n in range(7):
        own_term += term_ring[n]
    terms_out[...] = own_term
    for copy in copies1:
        copy.wait()
    ig_out.wait()
    dw1_out.finish()
    norm_sum.finish()


def finish(dq, dkv, pre, normed, w1, gains, qgain, kgain, cosine, sine, tok, grad_hidden, dwo, dwg, dwd, gain_two):
    vmem = pl.BlockSpec(memory_space=pltpu.VMEM)
    return pl.pallas_call(
        finish_kernel,
        out_shape=(
            jax.ShapeDtypeStruct((2, HALF, D), BF),
            jax.ShapeDtypeStruct((4, 32, W1C), BF),
            jax.ShapeDtypeStruct((4, 32, W1C), BF),
            jax.ShapeDtypeStruct((4, 32, 256), BF),
            jax.ShapeDtypeStruct((4, 32, 768), BF),
            jax.ShapeDtypeStruct((4, 32, 384), BF),
            jax.ShapeDtypeStruct((24, HD), F32),
        ),
        in_specs=[vmem] * 16,
        out_specs=(vmem,) * 7,
        scratch_shapes=[
            pltpu.VMEM((4 * CH, W1C), BF),
            pltpu.VMEM((4, 8, 32, W1C), BF),
            pltpu.VMEM((4, 32, W1C), BF),
            pltpu.VMEM((24, HD), F32),
            pltpu.VMEM((15, 24, HD), F32),
            pltpu.VMEM((7, 24, HD), F32),
        ]
        + reduce_scratch()
        + plane_scratch(W1C)
        + [
            pltpu.SemaphoreType.DMA((11,)),
            pltpu.SemaphoreType.DMA((11,)),
            pltpu.SemaphoreType.DMA((4,)),
            pltpu.SemaphoreType.DMA((4,)),
            pltpu.SemaphoreType.DMA((7,)),
            pltpu.SemaphoreType.DMA((7,)),
            pltpu.SemaphoreType.DMA((1,)),
            pltpu.SemaphoreType.DMA((1,)),
            pltpu.SemaphoreType.DMA((22,)),
            pltpu.SemaphoreType.DMA((22,)),
        ],
        compiler_params=pltpu.CompilerParams(
            collective_id=4, has_side_effects=True, vmem_limit_bytes=VMEM_LIMIT
        ),
        name="finish",
    )(dq, dkv, pre, normed, w1, gains, qgain, kgain, cosine, sine, tok, grad_hidden, dwo, dwg, dwd, gain_two)


def prepare_kernel(
    seg, pos, wq, wk, wv, wout, wgate, wup, wdown, ga, gm, inverse,
    w1, wo, wg, wd, gains, start_out, cosine, sine,
):
    z, x, y, _ = place()
    t = x * 4 + y
    for i in range(4):
        w1[i, :, 0:256] = wq[:, i * 256 : (i + 1) * 256]
        w1[i, :, 256:384] = wk[:, i * 128 : (i + 1) * 128]
        w1[i, :, 384:512] = wv[:, i * 128 : (i + 1) * 128]
        wg[i, :, :384] = wgate[:, i * 384 : (i + 1) * 384]
        wg[i, :, 384:] = wup[:, i * 384 : (i + 1) * 384]
        wo[i] = wout[i * 256 : (i + 1) * 256, :].astype(F32).T.astype(BF)
        wd[i] = wdown[i * 384 : (i + 1) * 384, :].astype(F32).T.astype(BF)
    gains[...] = jnp.zeros_like(gains)
    gains[0:1, 0:32] = ga[...].astype(F32)
    gains[0:1, 32:64] = gm[...].astype(F32)
    own = (z * 8 + t) * CH + lax.broadcasted_iota(jnp.int32, (1, CH), 1)
    known = jnp.where(seg[...] == 1, own - pos[...], 0)
    start = jnp.max(known.astype(F32), axis=1, keepdims=True).astype(jnp.int32)
    start_out[...] = start
    for c in range(4):
        index = (c * 8 + t) * CH + lax.broadcasted_iota(jnp.int32, (CH, 1), 0)
        angle = (index - first_allowed(index, start)).astype(F32) * inverse[...]
        co, si = jnp.cos(angle), jnp.sin(angle)
        cosine[c * CH : (c + 1) * CH, :] = co
        sine[c * CH : (c + 1) * CH, :] = jnp.where(
            lax.broadcasted_iota(jnp.int32, (1, HD), 1) < HD // 2, -si, si
        )


def prepare(*arrays):
    vmem = pl.BlockSpec(memory_space=pltpu.VMEM)
    return pl.pallas_call(
        prepare_kernel,
        out_shape=(
            jax.ShapeDtypeStruct((4, 32, W1C), BF),
            jax.ShapeDtypeStruct((4, 32, 256), BF),
            jax.ShapeDtypeStruct((4, 32, 768), BF),
            jax.ShapeDtypeStruct((4, 32, 384), BF),
            jax.ShapeDtypeStruct((8, HD), F32),
            jax.ShapeDtypeStruct((1, 1), jnp.int32),
            jax.ShapeDtypeStruct((4 * CH, HD), F32),
            jax.ShapeDtypeStruct((4 * CH, HD), F32),
        ),
        in_specs=[vmem] * 12,
        out_specs=(vmem,) * 8,
        compiler_params=pltpu.CompilerParams(vmem_limit_bytes=VMEM_LIMIT),
        name="prepare",
    )(*arrays)


def arrange_kernel(
    res, ig, ring1, twin1, dwo, two, dwg, twg, dwd, twd, terms,
    res_out, ig_out, gq, gk, gv, g_out, g_gate, g_up, g_down, g_attn, g_mlp, g_qgain, g_kgain,
):
    z, x, y, _ = place()
    c = z * 8 + x * 4 + y
    res_out[...] = res[...]
    ig_out[...] = ig[...]
    for i in range(4):
        both = ring1[i].astype(F32) + twin1[i].astype(F32)
        gq[:, i * 256 : (i + 1) * 256] = both[:, :256]
        gk[:, i * 128 : (i + 1) * 128] = both[:, 256:384]
        gv[:, i * 128 : (i + 1) * 128] = both[:, 384:]
        both = dwg[i].astype(F32) + twg[i].astype(F32)
        g_gate[:, i * 384 : (i + 1) * 384] = both[:, :384]
        g_up[:, i * 384 : (i + 1) * 384] = both[:, 384:]
        g_out[i * 256 : (i + 1) * 256, :] = (dwo[i].astype(F32) + two[i].astype(F32)).T
        g_down[i * 384 : (i + 1) * 384, :] = (dwd[i].astype(F32) + twd[i].astype(F32)).T
    g_qgain[...] = terms[16:17]
    g_kgain[...] = terms[17:18]
    for out, first in ((g_attn, 0), (g_mlp, 8)):
        value = jnp.zeros((1, 32), F32)
        for n in range(32):
            piece = terms[first + n // 4 : first + n // 4 + 1, (n % 4) * 32 : (n % 4 + 1) * 32]
            value += jnp.where(c == n, piece, 0.0)
        out[...] = value


def arrange(*arrays):
    vmem = pl.BlockSpec(memory_space=pltpu.VMEM)
    return pl.pallas_call(
        arrange_kernel,
        out_shape=(
            jax.ShapeDtypeStruct((2, HALF, D), BF),
            jax.ShapeDtypeStruct((2, HALF, D), BF),
            jax.ShapeDtypeStruct((32, 1024), F32),
            jax.ShapeDtypeStruct((32, 512), F32),
            jax.ShapeDtypeStruct((32, 512), F32),
            jax.ShapeDtypeStruct((1024, 32), F32),
            jax.ShapeDtypeStruct((32, 1536), F32),
            jax.ShapeDtypeStruct((32, 1536), F32),
            jax.ShapeDtypeStruct((1536, 32), F32),
            jax.ShapeDtypeStruct((1, 32), F32),
            jax.ShapeDtypeStruct((1, 32), F32),
            jax.ShapeDtypeStruct((1, HD), F32),
            jax.ShapeDtypeStruct((1, HD), F32),
        ),
        in_specs=[vmem] * 11,
        out_specs=(vmem,) * 13,
        compiler_params=pltpu.CompilerParams(vmem_limit_bytes=VMEM_LIMIT),
        name="arrange",
    )(*arrays)


def on_device(
    tokens, segments, positions, cotangent, query_weight, key_weight, value_weight, out_weight,
    attn_gain, query_gain, key_gain, gate_weight, up_weight, down_weight, mlp_gain,
):
    half = HD // 2
    inverse = ROPE_BASE ** (-jnp.arange(half, dtype=F32) / half)
    inverse = jnp.concatenate([inverse, inverse])[None]
    w1, wo, wg, wd, gains, start, cosine, sine = prepare(
        segments, positions, query_weight, key_weight, value_weight, out_weight, gate_weight, up_weight,
        down_weight, attn_gain[None], mlp_gain[None], inverse,
    )
    tok = tokens.reshape(2, HALF, D)
    tok_all, w1_all, gains_all = spread(tok, w1, gains)
    w1_all = w1_all.reshape(D, W1C)
    qgain, kgain = query_gain.astype(F32)[None], key_gain.astype(F32)[None]
    q, kv, pre, normed = make_heads(
        tok_all.reshape(4 * CH, D), w1_all, gains_all, qgain, kgain, cosine, sine
    )
    att, out_t, logs, kv_all, cot_all, wo, wg, wd = attend(
        q, kv, cotangent.reshape(2, HALF, D), wo, wg, wd, start
    )
    hidden, down_parts, grad_hidden, grad_att, dwo, dwg, dwd, gain_two_term = middle(
        att, wo, wg, wd, gains_all, tok, cot_all
    )
    dq, dkv, dwo, dwg, dwd, result = attend_back(
        q, kv_all, grad_att, out_t, logs, dwo.reshape(4, 8, 32, 256), dwg, dwd, hidden, down_parts, start
    )
    input_grad, ring1, twin1, two, twg, twd, terms = finish(
        dq, dkv, pre, normed, w1_all, gains_all, qgain, kgain, cosine, sine, tok, grad_hidden, dwo, dwg, dwd,
        gain_two_term,
    )
    result, input_grad, gq, gk, gv, g_out, g_gate, g_up, g_down, g_attn, g_mlp, g_qgain, g_kgain = arrange(
        result, input_grad, ring1, twin1, dwo, two, dwg, twg, dwd, twd, terms
    )
    return (
        result.reshape(1, CH, D),
        input_grad.reshape(1, CH, D),
        gq,
        gk,
        gv,
        g_out,
        g_attn[0],
        g_qgain[0],
        g_kgain[0],
        g_gate,
        g_up,
        g_down,
        g_mlp[0],
    )


def solution(mesh):
    torus = Mesh(
        mesh.devices.reshape(mesh.shape["rep"], 4, 2, 4, mesh.shape["head"]),
        ("rep", "ctx_0", "ctx_1", "ctx_2", "head"),
    )
    return jax.shard_map(
        on_device,
        mesh=torus,
        in_specs=(
            P("rep", CTX, None),
            P("rep", CTX),
            P("rep", CTX),
            P("rep", CTX, None),
            P(CTX, "head"),
            P(CTX, "head"),
            P(CTX, "head"),
            P("head", CTX),
            P(CTX),
            P(),
            P(),
            P(CTX, "head"),
            P(CTX, "head"),
            P("head", CTX),
            P(CTX),
        ),
        out_specs=(
            P("rep", CTX, None),
            P("rep", CTX, None),
            P(CTX, "head"),
            P(CTX, "head"),
            P(CTX, "head"),
            P("head", CTX),
            P(CTX),
            P(),
            P(),
            P(CTX, "head"),
            P(CTX, "head"),
            P("head", CTX),
            P(CTX),
        ),
        check_vma=False,
    )
```

```python
import math

import jax
import jax.numpy as jnp
import numpy as np
from jax import lax
from jax.experimental import pallas as pl
from jax.experimental.pallas import tpu as pltpu
from jax.sharding import Mesh
from jax.sharding import PartitionSpec as P

MESH = pl.DeviceIdType.MESH
CTX = ("ctx_0", "ctx_1", "ctx_2")
EPSILON = 1e-06
ROPE_BASE = 1000000.0
BF = jnp.bfloat16
F32 = jnp.float32
HD = 128
D = 1024
CH = 192
HALF = 96
MIDDLE = 5952
W1C = 512
SCALE = 1.0 / math.sqrt(HD)
SCALE2 = SCALE / math.log(2.0)
VMEM_LIMIT = 56 * 1024 * 1024
PLANE = ((0, 1), (0, 3), (1, 0), (1, 1), (1, 3), (0, 2), (1, 2))
RING = (1, 3, 2)


def nn(a, b):
    return jnp.dot(a, b, preferred_element_type=F32)


def nt(a, b):
    return lax.dot_general(a, b, (((1,), (1,)), ((), ())), preferred_element_type=F32)


def tn(a, b):
    return lax.dot_general(a, b, (((0,), (0,)), ((), ())), preferred_element_type=F32)


def rcopy(src, dst, send, recv, device):
    return pltpu.make_async_remote_copy(
        src_ref=src, dst_ref=dst, send_sem=send, recv_sem=recv, device_id=device, device_id_type=MESH
    )


def place():
    return tuple(lax.axis_index(name) for name in ("ctx_0", "ctx_1", "ctx_2", "head"))


def ring_peer(z, k):
    return {"ctx_0": lax.rem(z + k, 4)}


def plane_peer(x, y, dx, dy):
    return {"ctx_1": lax.rem(x + dx, 2), "ctx_2": lax.rem(y + dy, 4)}


def greet(devices):
    barrier = pltpu.get_barrier_semaphore()
    for device in devices:
        pl.semaphore_signal(barrier, inc=1, device_id=device, device_id_type=MESH)
    pl.semaphore_wait(barrier, len(devices))


def group_devices(z, h):
    return [{"head": 1 - h}] + [ring_peer(z, k) for k in RING]


def plane_devices(x, y):
    return [plane_peer(x, y, dx, dy) for dx, dy in PLANE]


class Gather:
    def __init__(self, own, buf, z, h, sems):
        self.buf, self.z, self.h = buf, z, h
        self.sz, self.rz, self.ss, self.rs = sems
        self.sent = []
        self.from_core = {}
        self.ring = {}
        for k in RING:
            copy = rcopy(own, buf.at[z, h], self.sz.at[k], self.rz.at[k], ring_peer(z, k))
            copy.start()
            self.ring[k] = copy
            self.sent.append(copy)

    def to_core(self, k):
        source = lax.rem(self.z + 4 - k, 4)
        slot = self.buf.at[source, self.h]
        copy = rcopy(slot, slot, self.ss.at[k], self.rs.at[k], {"head": 1 - self.h})
        copy.start()
        self.from_core[k] = copy
        self.sent.append(copy)

    def forward(self, k):
        self.ring[k].wait_recv()
        self.to_core(k)

    def arrived(self, k):
        self.from_core[k].wait_recv()

    def finish(self):
        for copy in self.sent:
            copy.wait_send()


class Reduce:
    def __init__(self, parts, other, sums, inbox, z, h, sems):
        self.parts, self.other, self.sums, self.inbox, self.z, self.h = parts, other, sums, inbox, z, h
        self.ss, self.rs, self.sz, self.rz = sems
        self.sent = []
        self.core = {}
        self.ring = {}

    def give(self, k, value):
        chunk = lax.rem(self.z + k, 4)
        self.parts[chunk] = value.astype(BF).reshape(2, HALF, D)
        self.offer(k)

    def offer(self, k):
        chunk = lax.rem(self.z + k, 4)
        copy = rcopy(
            self.parts.at[chunk, 1 - self.h],
            self.other.at[chunk],
            self.ss.at[k],
            self.rs.at[k],
            {"head": 1 - self.h},
        )
        copy.start()
        self.core[k] = copy
        self.sent.append(copy)

    def pass_on(self, k):
        chunk = lax.rem(self.z + k, 4)
        self.core[k].wait_recv()
        both = self.parts[chunk, self.h].astype(F32) + self.other[chunk].astype(F32)
        self.sums[chunk] = both.astype(BF)
        copy = rcopy(
            self.sums.at[chunk],
            self.inbox.at[self.z],
            self.sz.at[k],
            self.rz.at[k],
            ring_peer(self.z, k),
        )
        copy.start()
        self.ring[k] = copy
        self.sent.append(copy)

    def total(self):
        self.core[0].wait_recv()
        result = self.parts[self.z, self.h].astype(F32) + self.other[self.z].astype(F32)
        for k in RING:
            self.ring[k].wait_recv()
            result += self.inbox[lax.rem(self.z + 4 - k, 4)].astype(F32)
        return result

    def finish(self):
        for copy in self.sent:
            copy.wait_send()


def reduce_scratch(parts=True):
    return [pltpu.VMEM((4, 2, HALF, D), BF)] * parts + [
        pltpu.VMEM((4, HALF, D), BF),
        pltpu.VMEM((4, HALF, D), BF),
        pltpu.VMEM((4, HALF, D), BF),
    ] + [pltpu.SemaphoreType.DMA((4,))] * 4


def gather_scratch():
    return [pltpu.SemaphoreType.DMA((4,))] * 4


def columns(source, width, peer):
    return source.at[:, pl.ds(pl.multiple_of(peer * width, 128), width)]


def swap_columns(source, width, ring, first, z, send, recv):
    slot = ring.at[z, :, pl.ds(first, width)]
    copies = []
    for k in RING:
        peer = lax.rem(z + k, 4)
        copy = rcopy(columns(source, width, peer), slot, send.at[k], recv.at[k], ring_peer(z, k))
        copy.start()
        copies.append(copy)
    keep = pltpu.make_async_copy(columns(source, width, z), slot, send.at[0])
    keep.start()
    return copies, keep


def spread_kernel(
    tok, wq, wk, wv, ga, gm, seg, pos, inverse, tok_all, w1_all, gains_all, start_out, cosine, sine,
    gains, w1_ring, gains_ring, local, ring_send, ring_recv, plane_send, plane_recv, *sems
):
    z, x, y, h = place()
    t = x * 4 + y
    gains[...] = jnp.zeros_like(gains)
    gains[0:1, 0:32] = ga[...].astype(F32)
    gains[0:1, 32:64] = gm[...].astype(F32)
    greet(group_devices(z, h) + plane_neighbours(x, y))
    keep = [
        pltpu.make_async_copy(gains, gains_ring.at[z], local.at[1]),
        pltpu.make_async_copy(tok, tok_all.at[z], local.at[2]),
    ]
    for copy in keep:
        copy.start()
    ring = []
    for n, (source, width, first) in enumerate(((wq, 256, 0), (wk, 128, 256), (wv, 128, 384))):
        copies, own = swap_columns(source, width, w1_ring, first, z, ring_send.at[n], ring_recv.at[n])
        ring += copies
        keep.append(own)
    for k in RING:
        copy = rcopy(gains, gains_ring.at[z], ring_send.at[3, k], ring_recv.at[3, k], ring_peer(z, k))
        copy.start()
        ring.append(copy)
    tokens_out = Gather(tok.at[h], tok_all, z, h, sems)
    for copy in keep:
        copy.wait()
    for copy in ring:
        copy.wait_recv()
    plane = [
        PlaneGather(w1_ring, w1_all, x, y, plane_send.at[0], plane_recv.at[0]),
        PlaneGather(gains_ring, gains_all, x, y, plane_send.at[1], plane_recv.at[1]),
    ]
    keep = [
        pltpu.make_async_copy(w1_ring, w1_all.at[:, t], local.at[3]),
        pltpu.make_async_copy(gains_ring, gains_all.at[:, t], local.at[4]),
    ]
    for copy in keep:
        copy.start()
    own_index = (z * 8 + t) * CH + lax.broadcasted_iota(jnp.int32, (1, CH), 1)
    known = jnp.where(seg[...] == 1, own_index - pos[...], 0)
    start = jnp.max(known.astype(F32), axis=1, keepdims=True).astype(jnp.int32)
    start_out[...] = start
    for c in range(4):
        index = (c * 8 + t) * CH + lax.broadcasted_iota(jnp.int32, (CH, 1), 0)
        angle = (index - first_allowed(index, start)).astype(F32) * inverse[...]
        co, si = jnp.cos(angle), jnp.sin(angle)
        cosine[c * CH : (c + 1) * CH, :] = co
        sine[c * CH : (c + 1) * CH, :] = jnp.where(
            lax.broadcasted_iota(jnp.int32, (1, HD), 1) < HD // 2, -si, si
        )
    for item in plane:
        item.relay()
    for k in RING:
        tokens_out.forward(k)
    for k in RING:
        tokens_out.arrived(k)
    for copy in ring:
        copy.wait_send()
    for item in plane:
        item.arrived()
        item.finish()
    tokens_out.finish()
    for copy in keep:
        copy.wait()


def spread(*arrays):
    any_ = pl.BlockSpec(memory_space=pl.ANY)
    vmem = pl.BlockSpec(memory_space=pltpu.VMEM)
    return pl.pallas_call(
        spread_kernel,
        out_shape=(
            jax.ShapeDtypeStruct((4, 2, HALF, D), BF),
            jax.ShapeDtypeStruct((4, 8, 32, W1C), BF),
            jax.ShapeDtypeStruct((4, 8, 8, 128), F32),
            jax.ShapeDtypeStruct((1, 1), jnp.int32),
            jax.ShapeDtypeStruct((4 * CH, HD), F32),
            jax.ShapeDtypeStruct((4 * CH, HD), F32),
        ),
        in_specs=[any_] * 4 + [vmem] * 5,
        out_specs=(any_,) * 3 + (vmem,) * 3,
        scratch_shapes=[
            pltpu.VMEM((8, 128), F32),
            pltpu.VMEM((4, 32, W1C), BF),
            pltpu.VMEM((4, 8, 128), F32),
            pltpu.SemaphoreType.DMA((5,)),
            pltpu.SemaphoreType.DMA((4, 4)),
            pltpu.SemaphoreType.DMA((4, 4)),
            pltpu.SemaphoreType.DMA((2, 11)),
            pltpu.SemaphoreType.DMA((2, 11)),
        ]
        + gather_scratch(),
        compiler_params=pltpu.CompilerParams(
            collective_id=0, has_side_effects=True, vmem_limit_bytes=VMEM_LIMIT
        ),
        name="spread",
    )(*arrays)


def swap_ring(source, ring, z, send, recv):
    copies = []
    for k in RING:
        copy = rcopy(source.at[lax.rem(z + k, 4)], ring.at[z], send.at[k], recv.at[k], ring_peer(z, k))
        copy.start()
        copies.append(copy)
    return copies


TURNS = (1, 3, 2)


def beside(x, y):
    along = [{"ctx_2": lax.rem(y + dy, 4)} for dy in TURNS]
    return along, {"ctx_1": 1 - x}, {"ctx_1": 1 - x, "rep": 1 - lax.axis_index("rep")}


def plane_neighbours(x, y):
    along, near, far = beside(x, y)
    return along + [near, far]


class PlaneGather:
    def __init__(self, source, buf, x, y, send, recv):
        self.buf, self.x, self.y, self.send, self.recv = buf, x, y, send, recv
        along, self.near, self.far = beside(x, y)
        self.down = []
        self.over = []
        slot = buf.at[:, x * 4 + y]
        for j in range(3):
            copy = rcopy(source, slot, send.at[j], recv.at[j], along[j])
            copy.start()
            self.down.append(copy)
        self.across(0, source, slot)

    def across(self, j, source, slot):
        for a, device in ((0, self.near), (1, self.far)):
            part = pl.ds(2 * a, 2)
            n = 3 + 2 * j + a
            copy = rcopy(source.at[part], slot.at[part], self.send.at[n], self.recv.at[n], device)
            copy.start()
            self.over.append(copy)

    def relay(self):
        for j, dy in enumerate(TURNS):
            self.down[j].wait_recv()
            slot = self.buf.at[:, self.x * 4 + lax.rem(self.y + 4 - dy, 4)]
            self.across(j + 1, slot, slot)

    def arrived(self):
        for copy in self.over:
            copy.wait_recv()

    def finish(self):
        for copy in self.down + self.over:
            copy.wait_send()


class PlaneReduce:
    def __init__(self, parts, inx, col, iny, x, y, send, recv):
        self.parts, self.inx, self.col, self.iny = parts, inx, col, iny
        self.x, self.y, self.send, self.recv = x, y, send, recv
        self.along, near, far = beside(x, y)
        self.over = []
        self.down = []
        for j, dy in enumerate(TURNS + (0,)):
            row = lax.rem(y + dy, 4)
            for a, device in ((0, near), (1, far)):
                part = pl.ds(2 * a, 2)
                copy = rcopy(
                    parts.at[part, (1 - x) * 4 + row],
                    inx.at[part, row],
                    send.at[2 * j + a],
                    recv.at[2 * j + a],
                    device,
                )
                copy.start()
                self.over.append(copy)

    def joined(self, j, row):
        self.over[2 * j].wait_recv()
        self.over[2 * j + 1].wait_recv()
        return self.parts[:, self.x * 4 + row].astype(F32) + self.inx[:, row].astype(F32)

    def relay(self):
        for j, dy in enumerate(TURNS):
            row = lax.rem(self.y + dy, 4)
            self.col[:, row] = self.joined(j, row).astype(BF)
            copy = rcopy(
                self.col.at[:, row], self.iny.at[j], self.send.at[8 + j], self.recv.at[8 + j], self.along[j]
            )
            copy.start()
            self.down.append(copy)

    def total(self):
        result = self.joined(3, self.y)
        for j in range(3):
            self.down[j].wait_recv()
            result += self.iny[j].astype(F32)
        return result

    def finish(self):
        for copy in self.down + self.over:
            copy.wait_send()


def plane_scratch(width):
    return [
        pltpu.VMEM((4, 4, 32, width), BF),
        pltpu.VMEM((4, 4, 32, width), BF),
        pltpu.VMEM((3, 4, 32, width), BF),
    ]


def turn(u, cosine, sine):
    return u * cosine + pltpu.roll(u, HD // 2, 1) * sine


def joined_gain(gains, first):
    return jnp.concatenate(
        [gains[c // 8, c % 8, 0:1, first : first + 32] for c in range(32)], axis=1
    )


def rms_rate(v):
    return lax.rsqrt(jnp.mean(v * v, axis=-1, keepdims=True) + EPSILON)


def make_heads(tok_all, w1, gain, qgain, kgain, cosine, sine, q, kv, pre, normed):
    for chunk in range(4):
        span = slice(chunk * CH, (chunk + 1) * CH)
        v = tok_all[chunk].reshape(CH, D).astype(F32)
        n = (v * rms_rate(v) * gain).astype(BF)
        normed[span] = n
        out = nn(n, w1[...])
        pre[span] = out[:, :384]
        c, s = cosine[span], sine[span]
        for i in range(3):
            u = out[:, i * HD : (i + 1) * HD]
            u = turn(u * rms_rate(u) * (qgain if i < 2 else kgain)[...], c, s).astype(BF)
            if i < 2:
                q[chunk, i * CH : (i + 1) * CH, :] = u
            else:
                kv[chunk, :, :HD] = u
        kv[chunk, :, HD:] = out[:, 384:].astype(BF)


def query_index(chunk):
    lane = lax.broadcasted_iota(jnp.int32, (1, 2 * CH), 1)
    return chunk * CH + jnp.where(lane < CH, lane, lane - CH)


def first_allowed(index, start):
    return jnp.where(index < start, 0, jnp.where(index < start + MIDDLE, start, start + MIDDLE))


def key_index(chunk):
    return chunk * CH + lax.broadcasted_iota(jnp.int32, (CH, 1), 0)


def row_sums(p):
    return jnp.sum(p.reshape(p.shape[0] // 8, 8, p.shape[1]), axis=0)


def attend_kernel(
    tok_all, w1, gains, qgain, kgain, cosine, sine, cot, wo, wgate, wup, wd, start_ref,
    q, pre, normed, att, out_t, logs, kv_all, cot_all, wo_all, wg_ring, wd_ring,
    kv, acc, den, own_acc, own_den, wo_ring, wo_send, wo_recv, local, kv_send, kv_recv, ring_send, ring_recv, *sems
):
    z, x, y, h = place()
    t = x * 4 + y
    greet(group_devices(z, h) + plane_neighbours(x, y))
    along, near, _ = beside(x, y)

    def send(n, source, slot, device):
        copy = rcopy(source, slot, kv_send.at[n], kv_recv.at[n], device)
        copy.start()
        return copy

    cot_out = Gather(cot.at[h], cot_all, z, h, sems)
    weights = []
    keep = [pltpu.make_async_copy(cot, cot_all.at[z], local.at[3])]
    keep[0].start()
    for n, (source, width, ring, first) in enumerate(
        ((wo, 256, wo_ring, 0), (wgate, 384, wg_ring, 0), (wup, 384, wg_ring, 384), (wd, 384, wd_ring, 0))
    ):
        moved, own = swap_columns(source, width, ring, first, z, ring_send.at[n], ring_recv.at[n])
        weights += moved
        keep.append(own)
    make_heads(tok_all, w1, joined_gain(gains, 0), qgain, kgain, cosine, sine, q, kv, pre, normed)
    copies = [send(n, kv, kv_all.at[t], device) for n, device in enumerate(along + [near])]
    kv_all[t] = kv[...]
    start = start_ref[0, 0]
    acc[...] = jnp.zeros_like(acc)
    den[...] = jnp.zeros_like(den)

    def block(other, first, keys, at, count):
        k = kv_all[other, first : first + keys, :, :HD].reshape(keys * CH, HD)
        v = kv_all[other, first : first + keys, :, HD:].reshape(keys * CH, HD)
        p = jnp.exp2(nt(k, q[at : at + count].reshape(count * 2 * CH, HD)) * SCALE2)
        if first == 0:
            row = lax.broadcasted_iota(jnp.int32, (keys * CH, 1), 0)
            p = jnp.where((row >= CH) | (row + other * CH >= start), p, 0.0)
        lanes = slice(at * 2 * CH, (at + count) * 2 * CH)
        den[:, lanes] += row_sums(p)
        acc[:, lanes] += tn(v, p.astype(BF))

    def visit(other, own=False):
        block(other, 0, 2, 2, 2)

        def later():
            block(other, 2, 1, 3, 1)
            block(other, 0, 1, 1, 1)

        def earlier():
            block(other, 2, 1, 2, 2)
            block(other, 3, 1, 3, 1)
            block(other, 0, 1, 0, 2)
            block(other, 1, 1, 1, 1)

        if own:
            later()
        else:
            pl.when(other < t)(earlier)
            pl.when(other > t)(later)

    for c in range(4):
        mine = c * 8 + t
        index = query_index(mine)
        last = key_index(mine)
        p = jnp.exp2(nt(kv[c, :, :HD], q[c]) * SCALE2)
        p = jnp.where((last <= index) & (last >= first_allowed(index, start)), p, 0.0)
        own_acc[:, c * 2 * CH : (c + 1) * 2 * CH] = tn(kv[c, :, HD:], p.astype(BF))
        own_den[:, c * 2 * CH : (c + 1) * 2 * CH] = row_sums(p)
    visit(t, True)
    rows = [lax.rem(y + 4 - dy, 4) for dy in TURNS]
    halves = (pl.ds(0, 2), pl.ds(2, 2))

    def over(j):
        copies[j].wait_recv()
        slot = kv_all.at[x * 4 + rows[j], halves[0]]
        copies.append(send(4 + j, slot, slot, near))

    over(0)
    over(1)
    copies[3].wait_recv()
    across = (1 - x) * 4 + y
    slot = kv_all.at[across, halves[1]]
    for j in range(3):
        copies.append(send(7 + j, slot, slot, along[j]))
    for copy in weights[:3]:
        copy.wait_recv()
    keep[1].wait()
    wo_in = PlaneGather(wo_ring, wo_all, x, y, wo_send, wo_recv)
    visit(x * 4 + rows[0])
    visit(x * 4 + rows[1])
    over(2)
    visit(across)
    visit(x * 4 + rows[2])
    wo_in.relay()
    wo_all[:, t] = wo_ring[...]
    relayed = {0: (4, 6), 1: (5, 7), 2: (9, 8)}
    for k in RING:
        cot_out.forward(k)
    for j in range(3):
        for n in relayed[j]:
            copies[n].wait_recv()
        visit((1 - x) * 4 + rows[j])
    for c in range(4):
        inside = (query_index(c * 8 + t) < start + MIDDLE).astype(F32)
        lanes = slice(c * 2 * CH, (c + 1) * 2 * CH)
        denominator = jnp.sum(den[:, lanes] * inside + own_den[:, lanes], axis=0, keepdims=True)
        total = (acc[:, lanes] * inside + own_acc[:, lanes]) / denominator
        out_t[c] = total
        logs[c] = jnp.log2(denominator)
        full = total.T.astype(BF)
        att[c, :, :HD] = full[:CH]
        att[c, :, HD:] = full[CH:]
    for copy in copies:
        copy.wait_send()
    for k in RING:
        cot_out.arrived(k)
    cot_out.finish()
    wo_in.arrived()
    wo_in.finish()
    for copy in weights[:3]:
        copy.wait_send()
    for copy in weights[3:] + keep[:1] + keep[2:]:
        copy.wait()


def attend(*arrays):
    any_ = pl.BlockSpec(memory_space=pl.ANY)
    vmem = pl.BlockSpec(memory_space=pltpu.VMEM)
    smem = pl.BlockSpec(memory_space=pltpu.SMEM)
    return pl.pallas_call(
        attend_kernel,
        out_shape=(
            jax.ShapeDtypeStruct((4, 2 * CH, HD), BF),
            jax.ShapeDtypeStruct((4 * CH, 384), F32),
            jax.ShapeDtypeStruct((4 * CH, D), BF),
            jax.ShapeDtypeStruct((4, CH, 2 * HD), BF),
            jax.ShapeDtypeStruct((4, HD, 2 * CH), F32),
            jax.ShapeDtypeStruct((4, 1, 2 * CH), F32),
            jax.ShapeDtypeStruct((8, 4, CH, 2 * HD), BF),
            jax.ShapeDtypeStruct((4, 2, HALF, D), BF),
            jax.ShapeDtypeStruct((4, 8, 32, 256), BF),
            jax.ShapeDtypeStruct((4, 32, 768), BF),
            jax.ShapeDtypeStruct((4, 32, 384), BF),
        ),
        in_specs=[vmem] * 7 + [any_] * 5 + [smem],
        out_specs=(vmem,) * 7 + (any_, vmem, any_, any_),
        scratch_shapes=[
            pltpu.VMEM((4, CH, 2 * HD), BF),
            pltpu.VMEM((HD, 8 * CH), F32),
            pltpu.VMEM((8, 8 * CH), F32),
            pltpu.VMEM((HD, 8 * CH), F32),
            pltpu.VMEM((8, 8 * CH), F32),
            pltpu.VMEM((4, 32, 256), BF),
            pltpu.SemaphoreType.DMA((11,)),
            pltpu.SemaphoreType.DMA((11,)),
            pltpu.SemaphoreType.DMA((4,)),
            pltpu.SemaphoreType.DMA((10,)),
            pltpu.SemaphoreType.DMA((10,)),
            pltpu.SemaphoreType.DMA((4, 4)),
            pltpu.SemaphoreType.DMA((4, 4)),
        ]
        + gather_scratch(),
        compiler_params=pltpu.CompilerParams(
            collective_id=1, has_side_effects=True, vmem_limit_bytes=VMEM_LIMIT
        ),
        name="attend",
    )(*arrays)


def middle_kernel(
    att, wo_all, wg_ring, wd_ring, gains, tok, cot_all,
    hidden, down_parts, grad_hidden, grad_att, dwo, dwg_sum, dwd, gain_term,
    n2, gh, act, ggu, wg_all, wd_all, dwg, *scratch,
):
    first = scratch[0:8]
    back = scratch[8:16]
    fwd_sems = scratch[16:20]
    bwd_sems = scratch[20:24]
    dwg_buf = scratch[24:27]
    w_send, w_recv = scratch[27:29]
    z, x, y, h = place()
    t = x * 4 + y
    greet(group_devices(z, h) + plane_neighbours(x, y))
    wg_all[:, t] = wg_ring[...]
    wd_all[:, t] = wd_ring[...]
    wg_in = PlaneGather(wg_ring, wg_all, x, y, w_send.at[1], w_recv.at[1])
    wd_in = PlaneGather(wd_ring, wd_all, x, y, w_send.at[2], w_recv.at[2])
    out_sum = Reduce(*first[:4], z, h, first[4:])
    for k in (1, 3, 2, 0):
        out_sum.give(k, nt(att[lax.rem(z + k, 4)], wo_all[...].reshape(D, 256)))
    for k in RING:
        out_sum.pass_on(k)
    wg_in.relay()
    v = tok[h].astype(F32) + out_sum.total()
    hidden[...] = v
    g = joined_gain(gains, 32)
    rate = rms_rate(v)
    n2[z, h] = (v * rate * g).astype(BF)
    n2_out = Gather(n2.at[z, h], n2, z, h, fwd_sems)
    n2_out.to_core(0)
    wd_in.relay()
    back_sum = Reduce(*back[:4], z, h, back[4:])

    def feed(k):
        chunk = lax.rem(z + 4 - k, 4)
        back_k = (4 - k) % 4
        rows = n2[chunk].reshape(CH, D)
        gu = nn(rows, wg_all[...].reshape(D, 768))
        if k == 0:
            wd_in.arrived()
        ga = nn(cot_all[chunk].reshape(CH, D), wd_all[...].reshape(D, 384))
        gate, up = gu[:, :384], gu[:, 384:]
        s = 1.0 / (1.0 + jnp.exp(-gate))
        silu = gate * s
        a = (silu * up).astype(BF)
        act[chunk] = a
        gg = (ga * up * s * (1.0 + gate * (1.0 - s))).astype(BF)
        gp = (ga * silu).astype(BF)
        ggu[chunk, :, :384] = gg
        ggu[chunk, :, 384:] = gp
        back_sum.give(back_k, nt(ggu[chunk], wg_all[...].reshape(D, 768)))
        down_parts[chunk] = nt(a, wd_all[...].reshape(D, 384)).astype(BF).reshape(2, HALF, D)

    n2_out.arrived(0)
    wg_in.arrived()
    feed(0)
    n2_out.forward(1)
    n2_out.forward(3)
    n2_out.arrived(1)
    feed(1)
    n2_out.forward(2)
    n2_out.arrived(3)
    back_sum.pass_on(3)
    feed(3)
    back_sum.pass_on(1)
    n2_out.arrived(2)
    feed(2)
    back_sum.pass_on(2)
    dwg[...] = (
        tn(n2[...].reshape(4 * CH, D), ggu[...].reshape(4 * CH, 768)).astype(BF).reshape(4, 8, 32, 768)
    )
    dwg_out = PlaneReduce(dwg, *dwg_buf, x, y, w_send.at[3], w_recv.at[3])
    gy = back_sum.total()
    v = hidden[...]
    rate = rms_rate(v)
    vr = v * rate
    gain_term[...] = jnp.sum(gy * vr, axis=0, keepdims=True)
    gg = gy * g
    gv = rate * (gg - vr * jnp.mean(gg * vr, axis=-1, keepdims=True))
    grad = cot_all[z, h].astype(F32) + gv
    grad_hidden[...] = grad
    gh[z, h] = grad.astype(BF)
    gh_out = Gather(gh.at[z, h], gh, z, h, bwd_sems)
    gh_out.to_core(0)
    dwd[...] = (
        tn(cot_all[...].reshape(4 * CH, D), act[...].reshape(4 * CH, 384)).astype(BF).reshape(4, 8, 32, 384)
    )
    for k in RING:
        gh_out.forward(k)
    dwg_out.relay()
    for k in range(4):
        gh_out.arrived(k)
    full = gh[...].reshape(4 * CH, D)
    ga = nn(full, wo_all[...].reshape(D, 256)).astype(BF)
    for c in range(4):
        for i in range(2):
            grad_att[c, i * CH : (i + 1) * CH, :] = ga[c * CH : (c + 1) * CH, i * HD : (i + 1) * HD]
    dwo[...] = tn(full, att[...].reshape(4 * CH, 256)).astype(BF)
    dwg_sum[...] = dwg_out.total().astype(BF)
    for item in (out_sum, back_sum, n2_out, gh_out, wg_in, wd_in, dwg_out):
        item.finish()


def middle(att, wo, wg, wd, gains, tok, cot_all):
    vmem = pl.BlockSpec(memory_space=pltpu.VMEM)
    return pl.pallas_call(
        middle_kernel,
        out_shape=(
            jax.ShapeDtypeStruct((HALF, D), F32),
            jax.ShapeDtypeStruct((4, 2, HALF, D), BF),
            jax.ShapeDtypeStruct((HALF, D), F32),
            jax.ShapeDtypeStruct((4, 2 * CH, HD), BF),
            jax.ShapeDtypeStruct((D, 256), BF),
            jax.ShapeDtypeStruct((4, 32, 768), BF),
            jax.ShapeDtypeStruct((4, 8, 32, 384), BF),
            jax.ShapeDtypeStruct((1, D), F32),
        ),
        in_specs=[vmem] * 7,
        out_specs=(vmem,) * 8,
        scratch_shapes=[
            pltpu.VMEM((4, 2, HALF, D), BF),
            pltpu.VMEM((4, 2, HALF, D), BF),
            pltpu.VMEM((4, CH, 384), BF),
            pltpu.VMEM((4, CH, 768), BF),
            pltpu.VMEM((4, 8, 32, 768), BF),
            pltpu.VMEM((4, 8, 32, 384), BF),
            pltpu.VMEM((4, 8, 32, 768), BF),
        ]
        + reduce_scratch() * 2
        + gather_scratch() * 2
        + plane_scratch(768)
        + [pltpu.SemaphoreType.DMA((4, 11))] * 2,
        compiler_params=pltpu.CompilerParams(
            collective_id=2, has_side_effects=True, vmem_limit_bytes=VMEM_LIMIT
        ),
        name="middle",
    )(att, wo, wg, wd, gains, tok, cot_all)


def attend_back_kernel(
    q, kv_all, go, out_t, logs, dwo, dwg, dwd, hidden, down_parts, start_ref,
    dq, dkv, dwo_ring, dwg_ring, dwd_ring, res,
    dq_t, delta, far, acc, give_b, take_b, give_a, take_a, give_c, take_c, give_d, take_d, dwo_sum, dwd_sum, *scratch,
):
    dwo_buf = scratch[:3]
    dwd_buf = scratch[3:6]
    down = scratch[6:13]
    kv_send, kv_recv, w_send, w_recv, r_send, r_recv, res_send, res_recv = scratch[13:]
    z, x, y, h = place()
    t = x * 4 + y
    greet(group_devices(z, h) + plane_neighbours(x, y))
    along, near, _ = beside(x, y)
    down_sum = Reduce(down_parts, *down[:3], z, h, down[3:])
    for k in (1, 3, 2, 0):
        down_sum.offer(k)
    dwo_out = PlaneReduce(dwo, *dwo_buf, x, y, w_send.at[0], w_recv.at[0])
    dwd_out = PlaneReduce(dwd, *dwd_buf, x, y, w_send.at[1], w_recv.at[1])
    rings = swap_ring(dwg, dwg_ring, z, r_send.at[1], r_recv.at[1])
    dwg_ring[z] = dwg[z]
    start = start_ref[0, 0]
    dq_t[...] = jnp.zeros_like(dq_t)
    for c in range(4):
        delta[c] = jnp.sum(out_t[c] * go[c].astype(F32).T, axis=0, keepdims=True)
        far[c] = jnp.where(query_index(c * 8 + t) < start + MIDDLE, logs[c], 1e30)

    def pair(c, k, v, log, keep):
        qc, g = q[c], go[c]
        p = jnp.exp2(nt(k, qc) * SCALE2 - log)
        if keep is not None:
            p = jnp.where(keep, p, 0.0)
        ds = (p * (nt(v, g) - delta[c])).astype(BF)
        dq_t[c] += tn(k, ds)
        return nn(ds, qc), nn(p.astype(BF), g)

    def keys_of(other, chunks, own=False):
        result = []
        for c in chunks:
            both = kv_all[other, c]
            k, v = both[:, :HD], both[:, HD:]
            index = key_index(c * 8 + other)
            late = index >= start if c == 0 else None
            if own:
                mine = query_index(c * 8 + t)
                keep = (index <= mine) & (index >= first_allowed(mine, start))
                dk, dv = pair(c, k, v, logs[c], keep)
                acc[:, :HD] = dk
                acc[:, HD:] = dv
            else:
                acc[...] = jnp.zeros_like(acc)

                @pl.when(other < t)
                def _():
                    dk, dv = pair(c, k, v, far[c], late)
                    acc[:, :HD] = dk
                    acc[:, HD:] = dv

            dk, dv = acc[:, :HD], acc[:, HD:]
            for later in range(c + 1, 4):
                a, b = pair(later, k, v, far[later], late)
                dk += a
                dv += b
            result.append((dk * SCALE, dv))
        return result

    sent = []

    def send(n, source, slot, device):
        copy = rcopy(source, slot, kv_send.at[n], kv_recv.at[n], device)
        copy.start()
        sent.append(copy)

    def put(ref, values):
        for i, (dk, dv) in enumerate(values):
            ref[i, :, :HD] = dk.astype(BF)
            ref[i, :, HD:] = dv.astype(BF)

    rows = [lax.rem(y + dy, 4) for dy in TURNS]
    for j in range(3):
        for i, column in enumerate((x, 1 - x)):
            put(give_b.at[j, i], keys_of(column * 4 + rows[j], (2, 3)))
        send(j, give_b.at[j], take_b.at[j], along[j])
    for k in RING:
        down_sum.pass_on(k)
    for j, row in enumerate(rows + [y]):
        put(give_a.at[j], keys_of((1 - x) * 4 + row, (0, 1)))
        send(3 + j, give_a.at[j], take_a.at[j], near)
    dwo_out.relay()
    dwd_out.relay()
    res[h] = (hidden[...] + down_sum.total()).astype(BF)
    res_out = rcopy(res.at[h], res.at[h], res_send.at[0], res_recv.at[0], {"head": 1 - h})
    res_out.start()
    dwo_sum[...] = dwo_out.total().astype(BF)
    rings += swap_ring(dwo_sum, dwo_ring, z, r_send.at[0], r_recv.at[0])
    dwo_ring[z] = dwo_sum[z]
    dwd_sum[...] = dwd_out.total().astype(BF)
    rings += swap_ring(dwd_sum, dwd_ring, z, r_send.at[2], r_recv.at[2])
    dwd_ring[z] = dwd_sum[z]

    def add(values, *others):
        result = []
        for i, (dk, dv) in enumerate(values):
            for other in others:
                both = other[i].astype(F32)
                dk += both[:, :HD]
                dv += both[:, HD:]
            result.append((dk, dv))
        return result

    for j in range(3):
        values = keys_of(x * 4 + rows[j], (0, 1))
        sent[3 + j].wait_recv()
        put(give_c.at[j], add(values, take_a.at[j]))
        send(7 + j, give_c.at[j], take_c.at[j], along[j])
    values = keys_of((1 - x) * 4 + y, (2, 3))
    for j in range(3):
        sent[j].wait_recv()
    put(give_d, add(values, *(take_b.at[j, 1] for j in range(3))))
    send(10, give_d, take_d, near)
    low = keys_of(t, (0, 1), True)
    high = keys_of(t, (2, 3), True)
    for c in range(4):
        dq[c] = (dq_t[c] * SCALE).T
    sent[6].wait_recv()
    low = add(low, take_a.at[3])
    high = add(high, *(take_b.at[j, 0] for j in range(3)))
    for j in range(3):
        sent[7 + j].wait_recv()
    sent[10].wait_recv()
    low = add(low, *(take_c.at[j] for j in range(3)))
    high = add(high, take_d)
    for c, (dk, dv) in enumerate(low + high):
        dkv[c, :, :HD] = dk
        dkv[c, :, HD:] = dv
    for copy in rings:
        copy.wait()
    res_out.wait()
    for copy in sent:
        copy.wait_send()
    dwo_out.finish()
    dwd_out.finish()
    down_sum.finish()


def attend_back(q, kv_all, go, out_t, logs, dwo, dwg, dwd, hidden, down_parts, start):
    vmem = pl.BlockSpec(memory_space=pltpu.VMEM)
    smem = pl.BlockSpec(memory_space=pltpu.SMEM)
    return pl.pallas_call(
        attend_back_kernel,
        out_shape=(
            jax.ShapeDtypeStruct((4, 2 * CH, HD), F32),
            jax.ShapeDtypeStruct((4, CH, 2 * HD), F32),
            jax.ShapeDtypeStruct((4, 32, 256), BF),
            jax.ShapeDtypeStruct((4, 32, 768), BF),
            jax.ShapeDtypeStruct((4, 32, 384), BF),
            jax.ShapeDtypeStruct((2, HALF, D), BF),
        ),
        in_specs=[vmem] * 10 + [smem],
        out_specs=(vmem,) * 6,
        scratch_shapes=[
            pltpu.VMEM((4, HD, 2 * CH), F32),
            pltpu.VMEM((4, 1, 2 * CH), F32),
            pltpu.VMEM((4, 1, 2 * CH), F32),
            pltpu.VMEM((CH, 2 * HD), F32),
            pltpu.VMEM((3, 2, 2, CH, 2 * HD), BF),
            pltpu.VMEM((3, 2, 2, CH, 2 * HD), BF),
            pltpu.VMEM((4, 2, CH, 2 * HD), BF),
            pltpu.VMEM((4, 2, CH, 2 * HD), BF),
            pltpu.VMEM((3, 2, CH, 2 * HD), BF),
            pltpu.VMEM((3, 2, CH, 2 * HD), BF),
            pltpu.VMEM((2, CH, 2 * HD), BF),
            pltpu.VMEM((2, CH, 2 * HD), BF),
            pltpu.VMEM((4, 32, 256), BF),
            pltpu.VMEM((4, 32, 384), BF),
        ]
        + plane_scratch(256)
        + plane_scratch(384)
        + reduce_scratch(False)
        + [
            pltpu.SemaphoreType.DMA((11,)),
            pltpu.SemaphoreType.DMA((11,)),
            pltpu.SemaphoreType.DMA((2, 11)),
            pltpu.SemaphoreType.DMA((2, 11)),
            pltpu.SemaphoreType.DMA((3, 4)),
            pltpu.SemaphoreType.DMA((3, 4)),
            pltpu.SemaphoreType.DMA((1,)),
            pltpu.SemaphoreType.DMA((1,)),
        ],
        compiler_params=pltpu.CompilerParams(
            collective_id=3, has_side_effects=True, vmem_limit_bytes=VMEM_LIMIT
        ),
        name="attend_back",
    )(q, kv_all, go, out_t, logs, dwo, dwg, dwd, hidden, down_parts, start)


def finish_kernel(
    dq, dkv, pre, normed, w1, gains, qgain, kgain, cosine, sine, tok, grad_hidden, dwo, dwg, dwd,
    gain_two, ig, ring1, twin1, two, twg, twd, terms_out,
    dpre, dw1, dw1_sum, term, term_plane, term_ring, *scratch,
):
    sums = scratch[0:8]
    dw1_buf = scratch[8:11]
    plane_send, plane_recv, ring_send, ring_recv, twin_send, twin_recv, ig_send, ig_recv, term_send, term_recv = scratch[11:]
    z, x, y, h = place()
    t = x * 4 + y
    twin = {"rep": 1 - lax.axis_index("rep")}
    others = [{"head": h_, **device} for device in plane_devices(x, y) for h_ in (h, 1 - h)]
    rings = [{**ring_peer(z, k), **r} for k in RING for r in ({}, twin)]
    greet(group_devices(z, h)[:1] + others + rings + [twin, beside(x, y)[2]])

    twins = []
    for i, (source, other) in enumerate(((dwo, two), (dwg, twg), (dwd, twd))):
        copy = rcopy(source, other, twin_send.at[i], twin_recv.at[i], twin)
        copy.start()
        twins.append(copy)
    c_, s_ = cosine[...], sine[...]
    heads = []
    for i in range(2):
        heads.append(jnp.concatenate([dq[c, i * CH : (i + 1) * CH, :] for c in range(4)], axis=0))
    heads.append(dkv[...].reshape(4 * CH, 2 * HD)[:, :HD])
    terms = []
    for i, dy in enumerate(heads):
        gy = turn(dy, c_, -s_)
        v = pre[:, i * HD : (i + 1) * HD]
        rate = rms_rate(v)
        vr = v * rate
        terms.append(jnp.sum(gy * vr, axis=0, keepdims=True))
        gg = gy * (qgain if i < 2 else kgain)[...]
        out = rate * (gg - vr * jnp.mean(gg * vr, axis=-1, keepdims=True))
        dpre[:, i * HD : (i + 1) * HD] = out.astype(BF)
    dpre[:, 3 * HD :] = dkv[...].reshape(4 * CH, 2 * HD)[:, HD:].astype(BF)
    term[...] = jnp.zeros_like(term)
    term[16:17] = terms[0] + terms[1]
    term[17:18] = terms[2]
    dw1[...] = tn(normed[...], dpre[...]).astype(BF).reshape(4, 8, 32, W1C)
    dw1_out = PlaneReduce(dw1, *dw1_buf, x, y, plane_send, plane_recv)
    norm_sum = Reduce(*sums[:4], z, h, sums[4:])
    for k in (1, 3, 2, 0):
        chunk = lax.rem(z + k, 4)
        norm_sum.give(k, nt(dpre[pl.ds(pl.multiple_of(chunk * CH, CH), CH), :], w1[...]))
    for k in RING:
        norm_sum.pass_on(k)
    dw1_out.relay()
    gy = norm_sum.total()
    v = tok[h].astype(F32)
    rate = rms_rate(v)
    vr = v * rate
    own_term = jnp.sum(gy * vr, axis=0, keepdims=True)
    for i in range(8):
        term[i : i + 1] = own_term[:, i * HD : (i + 1) * HD]
        term[8 + i : 9 + i] = gain_two[:, i * HD : (i + 1) * HD]
    term_copies = []
    for n, device in enumerate(group_devices(z, h)[:1] + others):
        copy = rcopy(term, term_plane.at[n], term_send.at[n], term_recv.at[n], device)
        copy.start()
        term_copies.append(copy)
    gg = gy * joined_gain(gains, 0)
    gv = rate * (gg - vr * jnp.mean(gg * vr, axis=-1, keepdims=True))
    ig[h] = (grad_hidden[...] + gv).astype(BF)
    ig_out = rcopy(ig.at[h], ig.at[h], ig_send.at[0], ig_recv.at[0], {"head": 1 - h})
    ig_out.start()
    dw1_sum[...] = dw1_out.total().astype(BF)
    copies1 = swap_ring(dw1_sum, ring1, z, ring_send, ring_recv)
    for k in range(4):
        copy = rcopy(
            dw1_sum.at[lax.rem(z + k, 4)],
            twin1.at[z],
            twin_send.at[3 + k],
            twin_recv.at[3 + k],
            {**ring_peer(z, k), **twin},
        )
        copy.start()
        copies1.append(copy)
    ring1[z] = dw1_sum[z]
    for copy in term_copies:
        copy.wait()
    for n in range(15):
        term[...] += term_plane[n]
    term_copies = []
    for n, device in enumerate(rings + [twin]):
        copy = rcopy(term, term_ring.at[n], term_send.at[15 + n], term_recv.at[15 + n], device)
        copy.start()
        term_copies.append(copy)
    for copy in twins:
        copy.wait()
    for copy in term_copies:
        copy.wait()
    own_term = term[...]
    for n in range(7):
        own_term += term_ring[n]
    terms_out[...] = own_term
    for copy in copies1:
        copy.wait()
    ig_out.wait()
    dw1_out.finish()
    norm_sum.finish()


def finish(dq, dkv, pre, normed, w1, gains, qgain, kgain, cosine, sine, tok, grad_hidden, dwo, dwg, dwd, gain_two):
    vmem = pl.BlockSpec(memory_space=pltpu.VMEM)
    return pl.pallas_call(
        finish_kernel,
        out_shape=(
            jax.ShapeDtypeStruct((2, HALF, D), BF),
            jax.ShapeDtypeStruct((4, 32, W1C), BF),
            jax.ShapeDtypeStruct((4, 32, W1C), BF),
            jax.ShapeDtypeStruct((4, 32, 256), BF),
            jax.ShapeDtypeStruct((4, 32, 768), BF),
            jax.ShapeDtypeStruct((4, 32, 384), BF),
            jax.ShapeDtypeStruct((24, HD), F32),
        ),
        in_specs=[vmem] * 16,
        out_specs=(vmem,) * 7,
        scratch_shapes=[
            pltpu.VMEM((4 * CH, W1C), BF),
            pltpu.VMEM((4, 8, 32, W1C), BF),
            pltpu.VMEM((4, 32, W1C), BF),
            pltpu.VMEM((24, HD), F32),
            pltpu.VMEM((15, 24, HD), F32),
            pltpu.VMEM((7, 24, HD), F32),
        ]
        + reduce_scratch()
        + plane_scratch(W1C)
        + [
            pltpu.SemaphoreType.DMA((11,)),
            pltpu.SemaphoreType.DMA((11,)),
            pltpu.SemaphoreType.DMA((4,)),
            pltpu.SemaphoreType.DMA((4,)),
            pltpu.SemaphoreType.DMA((7,)),
            pltpu.SemaphoreType.DMA((7,)),
            pltpu.SemaphoreType.DMA((1,)),
            pltpu.SemaphoreType.DMA((1,)),
            pltpu.SemaphoreType.DMA((22,)),
            pltpu.SemaphoreType.DMA((22,)),
        ],
        compiler_params=pltpu.CompilerParams(
            collective_id=4, has_side_effects=True, vmem_limit_bytes=VMEM_LIMIT
        ),
        name="finish",
    )(dq, dkv, pre, normed, w1, gains, qgain, kgain, cosine, sine, tok, grad_hidden, dwo, dwg, dwd, gain_two)


def arrange_kernel(
    res, ig, ring1, twin1, dwo, two, dwg, twg, dwd, twd, terms,
    res_out, ig_out, gq, gk, gv, g_out, g_gate, g_up, g_down, g_attn, g_mlp, g_qgain, g_kgain,
):
    z, x, y, _ = place()
    c = z * 8 + x * 4 + y
    res_out[...] = res[...]
    ig_out[...] = ig[...]
    for i in range(4):
        both = ring1[i].astype(F32) + twin1[i].astype(F32)
        gq[:, i * 256 : (i + 1) * 256] = both[:, :256]
        gk[:, i * 128 : (i + 1) * 128] = both[:, 256:384]
        gv[:, i * 128 : (i + 1) * 128] = both[:, 384:]
        both = dwg[i].astype(F32) + twg[i].astype(F32)
        g_gate[:, i * 384 : (i + 1) * 384] = both[:, :384]
        g_up[:, i * 384 : (i + 1) * 384] = both[:, 384:]
        g_out[:, i * 256 : (i + 1) * 256] = dwo[i].astype(F32) + two[i].astype(F32)
        g_down[:, i * 384 : (i + 1) * 384] = dwd[i].astype(F32) + twd[i].astype(F32)
    g_qgain[...] = terms[16:17]
    g_kgain[...] = terms[17:18]
    for out, first in ((g_attn, 0), (g_mlp, 8)):
        value = jnp.zeros((1, 32), F32)
        for n in range(32):
            piece = terms[first + n // 4 : first + n // 4 + 1, (n % 4) * 32 : (n % 4 + 1) * 32]
            value += jnp.where(c == n, piece, 0.0)
        out[...] = value


def arrange(*arrays):
    vmem = pl.BlockSpec(memory_space=pltpu.VMEM)
    return pl.pallas_call(
        arrange_kernel,
        out_shape=(
            jax.ShapeDtypeStruct((2, HALF, D), BF),
            jax.ShapeDtypeStruct((2, HALF, D), BF),
            jax.ShapeDtypeStruct((32, 1024), F32),
            jax.ShapeDtypeStruct((32, 512), F32),
            jax.ShapeDtypeStruct((32, 512), F32),
            jax.ShapeDtypeStruct((32, 1024), F32),
            jax.ShapeDtypeStruct((32, 1536), F32),
            jax.ShapeDtypeStruct((32, 1536), F32),
            jax.ShapeDtypeStruct((32, 1536), F32),
            jax.ShapeDtypeStruct((1, 32), F32),
            jax.ShapeDtypeStruct((1, 32), F32),
            jax.ShapeDtypeStruct((1, HD), F32),
            jax.ShapeDtypeStruct((1, HD), F32),
        ),
        in_specs=[vmem] * 11,
        out_specs=(vmem,) * 13,
        compiler_params=pltpu.CompilerParams(vmem_limit_bytes=VMEM_LIMIT),
        name="arrange",
    )(*arrays)


def on_device(
    tokens, segments, positions, cotangent, query_weight, key_weight, value_weight, out_weight,
    attn_gain, query_gain, key_gain, gate_weight, up_weight, down_weight, mlp_gain,
):
    half = HD // 2
    inverse = ROPE_BASE ** (-np.arange(half) / half)
    inverse = jnp.asarray(np.concatenate([inverse, inverse])[None], F32)
    tok = tokens.reshape(2, HALF, D)
    tok_all, w1_all, gains_all, start, cosine, sine = spread(
        tok, query_weight, key_weight, value_weight, attn_gain[None], mlp_gain[None], segments, positions, inverse
    )
    w1_all = w1_all.reshape(D, W1C)
    qgain, kgain = query_gain[None], key_gain[None]
    q, pre, normed, att, out_t, logs, kv_all, cot_all, wo, wg, wd = attend(
        tok_all, w1_all, gains_all, qgain, kgain, cosine, sine, cotangent.reshape(2, HALF, D), out_weight.T,
        gate_weight, up_weight, down_weight.T, start,
    )
    hidden, down_parts, grad_hidden, grad_att, dwo, dwg, dwd, gain_two_term = middle(
        att, wo, wg, wd, gains_all, tok, cot_all
    )
    dq, dkv, dwo, dwg, dwd, result = attend_back(
        q, kv_all, grad_att, out_t, logs, dwo.reshape(4, 8, 32, 256), dwg, dwd, hidden, down_parts, start
    )
    input_grad, ring1, twin1, two, twg, twd, terms = finish(
        dq, dkv, pre, normed, w1_all, gains_all, qgain, kgain, cosine, sine, tok, grad_hidden, dwo, dwg, dwd,
        gain_two_term,
    )
    result, input_grad, gq, gk, gv, g_out, g_gate, g_up, g_down, g_attn, g_mlp, g_qgain, g_kgain = arrange(
        result, input_grad, ring1, twin1, dwo, two, dwg, twg, dwd, twd, terms
    )
    return (
        result.reshape(1, CH, D),
        input_grad.reshape(1, CH, D),
        gq,
        gk,
        gv,
        g_out.T,
        g_attn[0],
        g_qgain[0],
        g_kgain[0],
        g_gate,
        g_up,
        g_down.T,
        g_mlp[0],
    )


def solution(mesh):
    torus = Mesh(
        mesh.devices.reshape(mesh.shape["rep"], 4, 2, 4, mesh.shape["head"]),
        ("rep", "ctx_0", "ctx_1", "ctx_2", "head"),
    )
    return jax.shard_map(
        on_device,
        mesh=torus,
        in_specs=(
            P("rep", CTX, None),
            P("rep", CTX),
            P("rep", CTX),
            P("rep", CTX, None),
            P(CTX, "head"),
            P(CTX, "head"),
            P(CTX, "head"),
            P("head", CTX),
            P(CTX),
            P(),
            P(),
            P(CTX, "head"),
            P(CTX, "head"),
            P("head", CTX),
            P(CTX),
        ),
        out_specs=(
            P("rep", CTX, None),
            P("rep", CTX, None),
            P(CTX, "head"),
            P(CTX, "head"),
            P(CTX, "head"),
            P("head", CTX),
            P(CTX),
            P(),
            P(),
            P(CTX, "head"),
            P(CTX, "head"),
            P("head", CTX),
            P(CTX),
        ),
        check_vma=False,
    )
```

```python
import math

import jax
import jax.numpy as jnp
import numpy as np
from jax import lax
from jax.experimental import pallas as pl
from jax.experimental.pallas import tpu as pltpu
from jax.sharding import Mesh
from jax.sharding import PartitionSpec as P

MESH = pl.DeviceIdType.MESH
CTX = ("ctx_0", "ctx_1", "ctx_2")
EPSILON = 1e-06
ROPE_BASE = 1000000.0
BF = jnp.bfloat16
F32 = jnp.float32
HD = 128
D = 1024
CH = 192
HALF = 96
MIDDLE = 5952
W1C = 512
SCALE = 1.0 / math.sqrt(HD)
SCALE2 = SCALE / math.log(2.0)
VMEM_LIMIT = 56 * 1024 * 1024
PLANE = ((0, 1), (0, 3), (1, 0), (1, 1), (1, 3), (0, 2), (1, 2))
RING = (1, 3, 2)


def nn(a, b):
    return jnp.dot(a, b, preferred_element_type=F32)


def nt(a, b):
    return lax.dot_general(a, b, (((1,), (1,)), ((), ())), preferred_element_type=F32)


def tn(a, b):
    return lax.dot_general(a, b, (((0,), (0,)), ((), ())), preferred_element_type=F32)


def rcopy(src, dst, send, recv, device):
    return pltpu.make_async_remote_copy(
        src_ref=src, dst_ref=dst, send_sem=send, recv_sem=recv, device_id=device, device_id_type=MESH
    )


def place():
    return tuple(lax.axis_index(name) for name in ("ctx_0", "ctx_1", "ctx_2", "head"))


def ring_peer(z, k):
    return {"ctx_0": lax.rem(z + k, 4)}


def plane_peer(x, y, dx, dy):
    return {"ctx_1": lax.rem(x + dx, 2), "ctx_2": lax.rem(y + dy, 4)}


def greet(devices):
    barrier = pltpu.get_barrier_semaphore()
    for device in devices:
        pl.semaphore_signal(barrier, inc=1, device_id=device, device_id_type=MESH)
    pl.semaphore_wait(barrier, len(devices))


def group_devices(z, h):
    return [{"head": 1 - h}] + [ring_peer(z, k) for k in RING]


def plane_devices(x, y):
    return [plane_peer(x, y, dx, dy) for dx, dy in PLANE]


class Gather:
    def __init__(self, own, buf, z, h, sems):
        self.buf, self.z, self.h = buf, z, h
        self.sz, self.rz, self.ss, self.rs = sems
        self.sent = []
        self.from_core = {}
        self.ring = {}
        for k in RING:
            copy = rcopy(own, buf.at[z, h], self.sz.at[k], self.rz.at[k], ring_peer(z, k))
            copy.start()
            self.ring[k] = copy
            self.sent.append(copy)

    def to_core(self, k):
        source = lax.rem(self.z + 4 - k, 4)
        slot = self.buf.at[source, self.h]
        copy = rcopy(slot, slot, self.ss.at[k], self.rs.at[k], {"head": 1 - self.h})
        copy.start()
        self.from_core[k] = copy
        self.sent.append(copy)

    def forward(self, k):
        self.ring[k].wait_recv()
        self.to_core(k)

    def arrived(self, k):
        self.from_core[k].wait_recv()

    def finish(self):
        for copy in self.sent:
            copy.wait_send()


class Reduce:
    def __init__(self, parts, other, sums, inbox, z, h, sems):
        self.parts, self.other, self.sums, self.inbox, self.z, self.h = parts, other, sums, inbox, z, h
        self.ss, self.rs, self.sz, self.rz = sems
        self.sent = []
        self.core = {}
        self.ring = {}

    def give(self, k, value):
        chunk = lax.rem(self.z + k, 4)
        self.parts[chunk] = value.astype(BF).reshape(2, HALF, D)
        self.offer(k)

    def offer(self, k):
        chunk = lax.rem(self.z + k, 4)
        copy = rcopy(
            self.parts.at[chunk, 1 - self.h],
            self.other.at[chunk],
            self.ss.at[k],
            self.rs.at[k],
            {"head": 1 - self.h},
        )
        copy.start()
        self.core[k] = copy
        self.sent.append(copy)

    def pass_on(self, k):
        chunk = lax.rem(self.z + k, 4)
        self.core[k].wait_recv()
        both = self.parts[chunk, self.h].astype(F32) + self.other[chunk].astype(F32)
        self.sums[chunk] = both.astype(BF)
        copy = rcopy(
            self.sums.at[chunk],
            self.inbox.at[self.z],
            self.sz.at[k],
            self.rz.at[k],
            ring_peer(self.z, k),
        )
        copy.start()
        self.ring[k] = copy
        self.sent.append(copy)

    def total(self):
        self.core[0].wait_recv()
        result = self.parts[self.z, self.h].astype(F32) + self.other[self.z].astype(F32)
        for k in RING:
            self.ring[k].wait_recv()
            result += self.inbox[lax.rem(self.z + 4 - k, 4)].astype(F32)
        return result

    def finish(self):
        for copy in self.sent:
            copy.wait_send()


def reduce_scratch(parts=True):
    return [pltpu.VMEM((4, 2, HALF, D), BF)] * parts + [
        pltpu.VMEM((4, HALF, D), BF),
        pltpu.VMEM((4, HALF, D), BF),
        pltpu.VMEM((4, HALF, D), BF),
    ] + [pltpu.SemaphoreType.DMA((4,))] * 4


def gather_scratch():
    return [pltpu.SemaphoreType.DMA((4,))] * 4


def columns(source, width, peer):
    return source.at[:, pl.ds(pl.multiple_of(peer * width, 128), width)]


def swap_columns(source, width, ring, first, z, send, recv):
    slot = ring.at[z, :, pl.ds(first, width)]
    copies = []
    for k in RING:
        peer = lax.rem(z + k, 4)
        copy = rcopy(columns(source, width, peer), slot, send.at[k], recv.at[k], ring_peer(z, k))
        copy.start()
        copies.append(copy)
    keep = pltpu.make_async_copy(columns(source, width, z), slot, send.at[0])
    keep.start()
    return copies, keep


def swap_ring(source, ring, z, send, recv):
    copies = []
    for k in RING:
        copy = rcopy(source.at[lax.rem(z + k, 4)], ring.at[z], send.at[k], recv.at[k], ring_peer(z, k))
        copy.start()
        copies.append(copy)
    return copies


TURNS = (1, 3, 2)


def beside(x, y):
    along = [{"ctx_2": lax.rem(y + dy, 4)} for dy in TURNS]
    return along, {"ctx_1": 1 - x}, {"ctx_1": 1 - x, "rep": 1 - lax.axis_index("rep")}


def plane_neighbours(x, y):
    along, near, far = beside(x, y)
    return along + [near, far]


class PlaneGather:
    def __init__(self, source, buf, x, y, send, recv):
        self.buf, self.x, self.y, self.send, self.recv = buf, x, y, send, recv
        along, self.near, self.far = beside(x, y)
        self.down = []
        self.over = []
        slot = buf.at[:, x * 4 + y]
        for j in range(3):
            copy = rcopy(source, slot, send.at[j], recv.at[j], along[j])
            copy.start()
            self.down.append(copy)
        self.across(0, source, slot)

    def across(self, j, source, slot):
        for a, device in ((0, self.near), (1, self.far)):
            part = pl.ds(2 * a, 2)
            n = 3 + 2 * j + a
            copy = rcopy(source.at[part], slot.at[part], self.send.at[n], self.recv.at[n], device)
            copy.start()
            self.over.append(copy)

    def relay(self):
        for j, dy in enumerate(TURNS):
            self.down[j].wait_recv()
            slot = self.buf.at[:, self.x * 4 + lax.rem(self.y + 4 - dy, 4)]
            self.across(j + 1, slot, slot)

    def arrived(self):
        for copy in self.over:
            copy.wait_recv()

    def finish(self):
        for copy in self.down + self.over:
            copy.wait_send()


class PlaneReduce:
    def __init__(self, parts, inx, col, iny, x, y, send, recv):
        self.parts, self.inx, self.col, self.iny = parts, inx, col, iny
        self.x, self.y, self.send, self.recv = x, y, send, recv
        self.along, near, far = beside(x, y)
        self.over = []
        self.down = []
        for j, dy in enumerate(TURNS + (0,)):
            row = lax.rem(y + dy, 4)
            for a, device in ((0, near), (1, far)):
                part = pl.ds(2 * a, 2)
                copy = rcopy(
                    parts.at[part, (1 - x) * 4 + row],
                    inx.at[part, row],
                    send.at[2 * j + a],
                    recv.at[2 * j + a],
                    device,
                )
                copy.start()
                self.over.append(copy)

    def joined(self, j, row):
        self.over[2 * j].wait_recv()
        self.over[2 * j + 1].wait_recv()
        return self.parts[:, self.x * 4 + row].astype(F32) + self.inx[:, row].astype(F32)

    def relay(self):
        for j, dy in enumerate(TURNS):
            row = lax.rem(self.y + dy, 4)
            self.col[:, row] = self.joined(j, row).astype(BF)
            copy = rcopy(
                self.col.at[:, row], self.iny.at[j], self.send.at[8 + j], self.recv.at[8 + j], self.along[j]
            )
            copy.start()
            self.down.append(copy)

    def total(self):
        result = self.joined(3, self.y)
        for j in range(3):
            self.down[j].wait_recv()
            result += self.iny[j].astype(F32)
        return result

    def finish(self):
        for copy in self.down + self.over:
            copy.wait_send()


def plane_scratch(width):
    return [
        pltpu.VMEM((4, 4, 32, width), BF),
        pltpu.VMEM((4, 4, 32, width), BF),
        pltpu.VMEM((3, 4, 32, width), BF),
    ]


def turn(u, cosine, sine):
    return u * cosine + pltpu.roll(u, HD // 2, 1) * sine


def joined_gain(gains, first):
    return jnp.concatenate(
        [gains[c // 8, c % 8, 0:1, first : first + 32] for c in range(32)], axis=1
    )


def rms_rate(v):
    return lax.rsqrt(jnp.mean(v * v, axis=-1, keepdims=True) + EPSILON)


def make_heads(tok_all, w1, gain, qgain, kgain, cosine, sine, q, kv, pre, normed):
    for chunk in range(4):
        span = slice(chunk * CH, (chunk + 1) * CH)
        v = tok_all[chunk].reshape(CH, D).astype(F32)
        n = (v * rms_rate(v) * gain).astype(BF)
        normed[span] = n
        out = nn(n, w1[...].reshape(D, W1C))
        pre[span] = out[:, :384]
        c, s = cosine[span], sine[span]
        for i in range(3):
            u = out[:, i * HD : (i + 1) * HD]
            u = turn(u * rms_rate(u) * (qgain if i < 2 else kgain)[...], c, s).astype(BF)
            if i < 2:
                q[chunk, i * CH : (i + 1) * CH, :] = u
            else:
                kv[chunk, :, :HD] = u
        kv[chunk, :, HD:] = out[:, 384:].astype(BF)


def query_index(chunk):
    lane = lax.broadcasted_iota(jnp.int32, (1, 2 * CH), 1)
    return chunk * CH + jnp.where(lane < CH, lane, lane - CH)


def first_allowed(index, start):
    return jnp.where(index < start, 0, jnp.where(index < start + MIDDLE, start, start + MIDDLE))


def key_index(chunk):
    return chunk * CH + lax.broadcasted_iota(jnp.int32, (CH, 1), 0)


def row_sums(p):
    return jnp.sum(p.reshape(p.shape[0] // 8, 8, p.shape[1]), axis=0)


def spread_part(
    tok, wq, wk, wv, ga, gm, seg, pos, inverse, tok_all, w1_all, gains_all, start_out, cosine, sine,
    gains, w1_ring, gains_ring, local, ring_send, ring_recv, plane_send, plane_recv, *sems
):
    z, x, y, h = place()
    t = x * 4 + y
    gains[...] = jnp.zeros_like(gains)
    gains[0:1, 0:32] = ga[...].astype(F32)
    gains[0:1, 32:64] = gm[...].astype(F32)
    keep = [
        pltpu.make_async_copy(gains, gains_ring.at[z], local.at[1]),
        pltpu.make_async_copy(tok, tok_all.at[z], local.at[2]),
    ]
    for copy in keep:
        copy.start()
    ring = []
    for n, (source, width, first) in enumerate(((wq, 256, 0), (wk, 128, 256), (wv, 128, 384))):
        copies, own = swap_columns(source, width, w1_ring, first, z, ring_send.at[n], ring_recv.at[n])
        ring += copies
        keep.append(own)
    for k in RING:
        copy = rcopy(gains, gains_ring.at[z], ring_send.at[3, k], ring_recv.at[3, k], ring_peer(z, k))
        copy.start()
        ring.append(copy)
    tokens_out = Gather(tok.at[h], tok_all, z, h, sems)
    for copy in keep:
        copy.wait()
    for copy in ring:
        copy.wait_recv()
    plane = [
        PlaneGather(w1_ring, w1_all, x, y, plane_send.at[0], plane_recv.at[0]),
        PlaneGather(gains_ring, gains_all, x, y, plane_send.at[1], plane_recv.at[1]),
    ]
    keep = [
        pltpu.make_async_copy(w1_ring, w1_all.at[:, t], local.at[3]),
        pltpu.make_async_copy(gains_ring, gains_all.at[:, t], local.at[4]),
    ]
    for copy in keep:
        copy.start()
    own_index = (z * 8 + t) * CH + lax.broadcasted_iota(jnp.int32, (1, CH), 1)
    known = jnp.where(seg[...] == 1, own_index - pos[...], 0)
    start = jnp.max(known.astype(F32), axis=1, keepdims=True).astype(jnp.int32)
    start_out[...] = start
    for c in range(4):
        index = (c * 8 + t) * CH + lax.broadcasted_iota(jnp.int32, (CH, 1), 0)
        angle = (index - first_allowed(index, start)).astype(F32) * inverse[...]
        co, si = jnp.cos(angle), jnp.sin(angle)
        cosine[c * CH : (c + 1) * CH, :] = co
        sine[c * CH : (c + 1) * CH, :] = jnp.where(
            lax.broadcasted_iota(jnp.int32, (1, HD), 1) < HD // 2, -si, si
        )
    for item in plane:
        item.relay()
    for k in RING:
        tokens_out.forward(k)
    for k in RING:
        tokens_out.arrived(k)
    for copy in ring:
        copy.wait_send()
    for item in plane:
        item.arrived()
        item.finish()
    tokens_out.finish()
    for copy in keep:
        copy.wait()
    return start


def attend_part(
    tok_all, w1, gains, qgain, kgain, cosine, sine, cot, wo, wgate, wup, wd, start,
    q, pre, normed, att, out_t, logs, kv_all, cot_all, wo_all, wg_ring, wd_ring,
    kv, acc, den, own_acc, own_den, wo_ring, wo_send, wo_recv, local, kv_send, kv_recv, ring_send, ring_recv, *sems
):
    z, x, y, h = place()
    t = x * 4 + y
    along, near, _ = beside(x, y)

    def send(n, source, slot, device):
        copy = rcopy(source, slot, kv_send.at[n], kv_recv.at[n], device)
        copy.start()
        return copy

    cot_out = Gather(cot.at[h], cot_all, z, h, sems)
    weights = []
    keep = [pltpu.make_async_copy(cot, cot_all.at[z], local.at[3])]
    keep[0].start()
    for n, (source, width, ring, first) in enumerate(
        ((wo, 256, wo_ring, 0), (wgate, 384, wg_ring, 0), (wup, 384, wg_ring, 384), (wd, 384, wd_ring, 0))
    ):
        moved, own = swap_columns(source, width, ring, first, z, ring_send.at[n], ring_recv.at[n])
        weights += moved
        keep.append(own)
    make_heads(tok_all, w1, joined_gain(gains, 0), qgain, kgain, cosine, sine, q, kv, pre, normed)
    copies = [send(n, kv, kv_all.at[t], device) for n, device in enumerate(along + [near])]
    kv_all[t] = kv[...]
    acc[...] = jnp.zeros_like(acc)
    den[...] = jnp.zeros_like(den)

    def block(other, first, keys, at, count):
        k = kv_all[other, first : first + keys, :, :HD].reshape(keys * CH, HD)
        v = kv_all[other, first : first + keys, :, HD:].reshape(keys * CH, HD)
        p = jnp.exp2(nt(k, q[at : at + count].reshape(count * 2 * CH, HD)) * SCALE2)
        if first == 0:
            row = lax.broadcasted_iota(jnp.int32, (keys * CH, 1), 0)
            p = jnp.where((row >= CH) | (row + other * CH >= start), p, 0.0)
        lanes = slice(at * 2 * CH, (at + count) * 2 * CH)
        den[:, lanes] += row_sums(p)
        acc[:, lanes] += tn(v, p.astype(BF))

    def visit(other, own=False):
        block(other, 0, 2, 2, 2)

        def later():
            block(other, 2, 1, 3, 1)
            block(other, 0, 1, 1, 1)

        def earlier():
            block(other, 2, 1, 2, 2)
            block(other, 3, 1, 3, 1)
            block(other, 0, 1, 0, 2)
            block(other, 1, 1, 1, 1)

        if own:
            later()
        else:
            pl.when(other < t)(earlier)
            pl.when(other > t)(later)

    for c in range(4):
        mine = c * 8 + t
        index = query_index(mine)
        last = key_index(mine)
        p = jnp.exp2(nt(kv[c, :, :HD], q[c]) * SCALE2)
        p = jnp.where((last <= index) & (last >= first_allowed(index, start)), p, 0.0)
        own_acc[:, c * 2 * CH : (c + 1) * 2 * CH] = tn(kv[c, :, HD:], p.astype(BF))
        own_den[:, c * 2 * CH : (c + 1) * 2 * CH] = row_sums(p)
    visit(t, True)
    rows = [lax.rem(y + 4 - dy, 4) for dy in TURNS]
    halves = (pl.ds(0, 2), pl.ds(2, 2))

    def over(j):
        copies[j].wait_recv()
        slot = kv_all.at[x * 4 + rows[j], halves[0]]
        copies.append(send(4 + j, slot, slot, near))

    over(0)
    over(1)
    copies[3].wait_recv()
    across = (1 - x) * 4 + y
    slot = kv_all.at[across, halves[1]]
    for j in range(3):
        copies.append(send(7 + j, slot, slot, along[j]))
    for copy in weights[:3]:
        copy.wait_recv()
    keep[1].wait()
    wo_in = PlaneGather(wo_ring, wo_all, x, y, wo_send, wo_recv)
    visit(x * 4 + rows[0])
    visit(x * 4 + rows[1])
    over(2)
    visit(across)
    visit(x * 4 + rows[2])
    wo_in.relay()
    wo_all[:, t] = wo_ring[...]
    relayed = {0: (4, 6), 1: (5, 7), 2: (9, 8)}
    for k in RING:
        cot_out.forward(k)
    for j in range(3):
        for n in relayed[j]:
            copies[n].wait_recv()
        visit((1 - x) * 4 + rows[j])
    for c in range(4):
        inside = (query_index(c * 8 + t) < start + MIDDLE).astype(F32)
        lanes = slice(c * 2 * CH, (c + 1) * 2 * CH)
        denominator = jnp.sum(den[:, lanes] * inside + own_den[:, lanes], axis=0, keepdims=True)
        total = (acc[:, lanes] * inside + own_acc[:, lanes]) / denominator
        out_t[c] = total
        logs[c] = jnp.log2(denominator)
        full = total.T.astype(BF)
        att[c, :, :HD] = full[:CH]
        att[c, :, HD:] = full[CH:]
    for copy in copies:
        copy.wait_send()
    for k in RING:
        cot_out.arrived(k)
    cot_out.finish()
    wo_in.arrived()
    wo_in.finish()
    for copy in weights[:3]:
        copy.wait_send()
    for copy in weights[3:] + keep[:1] + keep[2:]:
        copy.wait()


def forward_kernel(*refs):
    z, x, y, h = place()
    greet(group_devices(z, h) + plane_neighbours(x, y))
    tok_all = refs[32]
    count = 33 + len(spread_scratch())
    start = spread_part(*refs[:9], tok_all, *refs[16:21], *refs[33:count])
    attend_part(
        tok_all, refs[16], refs[17], *refs[9:11], refs[19], refs[20], *refs[11:16], start,
        *refs[21:32], *refs[count:],
    )


def spread_scratch():
    return (
        [
            pltpu.VMEM((8, 128), F32),
            pltpu.VMEM((4, 32, W1C), BF),
            pltpu.VMEM((4, 8, 128), F32),
            pltpu.SemaphoreType.DMA((5,)),
            pltpu.SemaphoreType.DMA((4, 4)),
            pltpu.SemaphoreType.DMA((4, 4)),
            pltpu.SemaphoreType.DMA((2, 11)),
            pltpu.SemaphoreType.DMA((2, 11)),
        ]
        + gather_scratch()
    )


def attend_scratch():
    return (
        [
            pltpu.VMEM((4, CH, 2 * HD), BF),
            pltpu.VMEM((HD, 8 * CH), F32),
            pltpu.VMEM((8, 8 * CH), F32),
            pltpu.VMEM((HD, 8 * CH), F32),
            pltpu.VMEM((8, 8 * CH), F32),
            pltpu.VMEM((4, 32, 256), BF),
            pltpu.SemaphoreType.DMA((11,)),
            pltpu.SemaphoreType.DMA((11,)),
            pltpu.SemaphoreType.DMA((4,)),
            pltpu.SemaphoreType.DMA((10,)),
            pltpu.SemaphoreType.DMA((10,)),
            pltpu.SemaphoreType.DMA((4, 4)),
            pltpu.SemaphoreType.DMA((4, 4)),
        ]
        + gather_scratch()
    )


def forward(*arrays):
    any_ = pl.BlockSpec(memory_space=pl.ANY)
    vmem = pl.BlockSpec(memory_space=pltpu.VMEM)
    return pl.pallas_call(
        forward_kernel,
        out_shape=(
            jax.ShapeDtypeStruct((4, 8, 32, W1C), BF),
            jax.ShapeDtypeStruct((4, 8, 8, 128), F32),
            jax.ShapeDtypeStruct((1, 1), jnp.int32),
            jax.ShapeDtypeStruct((4 * CH, HD), F32),
            jax.ShapeDtypeStruct((4 * CH, HD), F32),
            jax.ShapeDtypeStruct((4, 2 * CH, HD), BF),
            jax.ShapeDtypeStruct((4 * CH, 384), F32),
            jax.ShapeDtypeStruct((4 * CH, D), BF),
            jax.ShapeDtypeStruct((4, CH, 2 * HD), BF),
            jax.ShapeDtypeStruct((4, HD, 2 * CH), F32),
            jax.ShapeDtypeStruct((4, 1, 2 * CH), F32),
            jax.ShapeDtypeStruct((8, 4, CH, 2 * HD), BF),
            jax.ShapeDtypeStruct((4, 2, HALF, D), BF),
            jax.ShapeDtypeStruct((4, 8, 32, 256), BF),
            jax.ShapeDtypeStruct((4, 32, 768), BF),
            jax.ShapeDtypeStruct((4, 32, 384), BF),
        ),
        in_specs=[any_] * 4 + [vmem] * 7 + [any_] * 5,
        out_specs=(vmem,) * 12 + (any_, vmem, any_, any_),
        scratch_shapes=[
            pltpu.VMEM((4, 2, HALF, D), BF),
        ]
        + spread_scratch()
        + attend_scratch(),
        compiler_params=pltpu.CompilerParams(
            collective_id=0, has_side_effects=True, vmem_limit_bytes=VMEM_LIMIT
        ),
        name="forward",
    )(*arrays)


def middle_kernel(
    att, wo_all, wg_ring, wd_ring, gains, tok, cot_all,
    hidden, down_parts, grad_hidden, grad_att, dwo, dwg_sum, dwd, gain_term,
    n2, gh, act, ggu, wg_all, wd_all, dwg, *scratch,
):
    first = scratch[0:8]
    back = scratch[8:16]
    fwd_sems = scratch[16:20]
    bwd_sems = scratch[20:24]
    dwg_buf = scratch[24:27]
    w_send, w_recv = scratch[27:29]
    z, x, y, h = place()
    t = x * 4 + y
    greet(group_devices(z, h) + plane_neighbours(x, y))
    wg_all[:, t] = wg_ring[...]
    wd_all[:, t] = wd_ring[...]
    wg_in = PlaneGather(wg_ring, wg_all, x, y, w_send.at[1], w_recv.at[1])
    wd_in = PlaneGather(wd_ring, wd_all, x, y, w_send.at[2], w_recv.at[2])
    out_sum = Reduce(*first[:4], z, h, first[4:])
    for k in (1, 3, 2, 0):
        out_sum.give(k, nt(att[lax.rem(z + k, 4)], wo_all[...].reshape(D, 256)))
    for k in RING:
        out_sum.pass_on(k)
    wg_in.relay()
    v = tok[h].astype(F32) + out_sum.total()
    hidden[...] = v
    g = joined_gain(gains, 32)
    rate = rms_rate(v)
    n2[z, h] = (v * rate * g).astype(BF)
    n2_out = Gather(n2.at[z, h], n2, z, h, fwd_sems)
    n2_out.to_core(0)
    wd_in.relay()
    back_sum = Reduce(*back[:4], z, h, back[4:])

    def feed(k):
        chunk = lax.rem(z + 4 - k, 4)
        back_k = (4 - k) % 4
        rows = n2[chunk].reshape(CH, D)
        gu = nn(rows, wg_all[...].reshape(D, 768))
        if k == 0:
            wd_in.arrived()
        ga = nn(cot_all[chunk].reshape(CH, D), wd_all[...].reshape(D, 384))
        gate, up = gu[:, :384], gu[:, 384:]
        s = 1.0 / (1.0 + jnp.exp(-gate))
        silu = gate * s
        a = (silu * up).astype(BF)
        act[chunk] = a
        gg = (ga * up * s * (1.0 + gate * (1.0 - s))).astype(BF)
        gp = (ga * silu).astype(BF)
        ggu[chunk, :, :384] = gg
        ggu[chunk, :, 384:] = gp
        back_sum.give(back_k, nt(ggu[chunk], wg_all[...].reshape(D, 768)))
        down_parts[chunk] = nt(a, wd_all[...].reshape(D, 384)).astype(BF).reshape(2, HALF, D)

    n2_out.arrived(0)
    wg_in.arrived()
    feed(0)
    n2_out.forward(1)
    n2_out.forward(3)
    n2_out.arrived(1)
    feed(1)
    n2_out.forward(2)
    n2_out.arrived(3)
    back_sum.pass_on(3)
    feed(3)
    back_sum.pass_on(1)
    n2_out.arrived(2)
    feed(2)
    back_sum.pass_on(2)
    dwg[...] = (
        tn(n2[...].reshape(4 * CH, D), ggu[...].reshape(4 * CH, 768)).astype(BF).reshape(4, 8, 32, 768)
    )
    dwg_out = PlaneReduce(dwg, *dwg_buf, x, y, w_send.at[3], w_recv.at[3])
    gy = back_sum.total()
    v = hidden[...]
    rate = rms_rate(v)
    vr = v * rate
    gain_term[...] = jnp.sum(gy * vr, axis=0, keepdims=True)
    gg = gy * g
    gv = rate * (gg - vr * jnp.mean(gg * vr, axis=-1, keepdims=True))
    grad = cot_all[z, h].astype(F32) + gv
    grad_hidden[...] = grad
    gh[z, h] = grad.astype(BF)
    gh_out = Gather(gh.at[z, h], gh, z, h, bwd_sems)
    gh_out.to_core(0)
    dwd[...] = (
        tn(cot_all[...].reshape(4 * CH, D), act[...].reshape(4 * CH, 384)).astype(BF).reshape(4, 8, 32, 384)
    )
    for k in RING:
        gh_out.forward(k)
    dwg_out.relay()
    for k in range(4):
        gh_out.arrived(k)
    full = gh[...].reshape(4 * CH, D)
    ga = nn(full, wo_all[...].reshape(D, 256)).astype(BF)
    for c in range(4):
        for i in range(2):
            grad_att[c, i * CH : (i + 1) * CH, :] = ga[c * CH : (c + 1) * CH, i * HD : (i + 1) * HD]
    dwo[...] = tn(full, att[...].reshape(4 * CH, 256)).astype(BF)
    dwg_sum[...] = dwg_out.total().astype(BF)
    for item in (out_sum, back_sum, n2_out, gh_out, wg_in, wd_in, dwg_out):
        item.finish()


def middle(att, wo, wg, wd, gains, tok, cot_all):
    vmem = pl.BlockSpec(memory_space=pltpu.VMEM)
    return pl.pallas_call(
        middle_kernel,
        out_shape=(
            jax.ShapeDtypeStruct((HALF, D), F32),
            jax.ShapeDtypeStruct((4, 2, HALF, D), BF),
            jax.ShapeDtypeStruct((HALF, D), F32),
            jax.ShapeDtypeStruct((4, 2 * CH, HD), BF),
            jax.ShapeDtypeStruct((D, 256), BF),
            jax.ShapeDtypeStruct((4, 32, 768), BF),
            jax.ShapeDtypeStruct((4, 8, 32, 384), BF),
            jax.ShapeDtypeStruct((1, D), F32),
        ),
        in_specs=[vmem] * 7,
        out_specs=(vmem,) * 8,
        scratch_shapes=[
            pltpu.VMEM((4, 2, HALF, D), BF),
            pltpu.VMEM((4, 2, HALF, D), BF),
            pltpu.VMEM((4, CH, 384), BF),
            pltpu.VMEM((4, CH, 768), BF),
            pltpu.VMEM((4, 8, 32, 768), BF),
            pltpu.VMEM((4, 8, 32, 384), BF),
            pltpu.VMEM((4, 8, 32, 768), BF),
        ]
        + reduce_scratch() * 2
        + gather_scratch() * 2
        + plane_scratch(768)
        + [pltpu.SemaphoreType.DMA((4, 11))] * 2,
        compiler_params=pltpu.CompilerParams(
            collective_id=2, has_side_effects=True, vmem_limit_bytes=VMEM_LIMIT
        ),
        name="middle",
    )(att, wo, wg, wd, gains, tok, cot_all)


def attend_back_part(
    q, kv_all, go, out_t, logs, dwo, dwg, dwd, hidden, down_parts, start_ref,
    dq, dkv, dwo_ring, dwg_ring, dwd_ring, res,
    dq_t, delta, far, acc, give_b, take_b, give_a, take_a, give_c, take_c, give_d, take_d, dwo_sum, dwd_sum, *scratch,
):
    dwo_buf = scratch[:3]
    dwd_buf = scratch[3:6]
    down = scratch[6:13]
    kv_send, kv_recv, w_send, w_recv, r_send, r_recv, res_send, res_recv = scratch[13:]
    z, x, y, h = place()
    t = x * 4 + y
    along, near, _ = beside(x, y)
    down_sum = Reduce(down_parts, *down[:3], z, h, down[3:])
    for k in (1, 3, 2, 0):
        down_sum.offer(k)
    dwo_out = PlaneReduce(dwo, *dwo_buf, x, y, w_send.at[0], w_recv.at[0])
    dwd_out = PlaneReduce(dwd, *dwd_buf, x, y, w_send.at[1], w_recv.at[1])
    rings = swap_ring(dwg, dwg_ring, z, r_send.at[1], r_recv.at[1])
    dwg_ring[z] = dwg[z]
    start = start_ref[0, 0]
    dq_t[...] = jnp.zeros_like(dq_t)
    for c in range(4):
        delta[c] = jnp.sum(out_t[c] * go[c].astype(F32).T, axis=0, keepdims=True)
        far[c] = jnp.where(query_index(c * 8 + t) < start + MIDDLE, logs[c], 1e30)

    def pair(c, k, v, log, keep):
        qc, g = q[c], go[c]
        p = jnp.exp2(nt(k, qc) * SCALE2 - log)
        if keep is not None:
            p = jnp.where(keep, p, 0.0)
        ds = (p * (nt(v, g) - delta[c])).astype(BF)
        dq_t[c] += tn(k, ds)
        return nn(ds, qc), nn(p.astype(BF), g)

    def keys_of(other, chunks, own=False):
        result = []
        for c in chunks:
            both = kv_all[other, c]
            k, v = both[:, :HD], both[:, HD:]
            index = key_index(c * 8 + other)
            late = index >= start if c == 0 else None
            if own:
                mine = query_index(c * 8 + t)
                keep = (index <= mine) & (index >= first_allowed(mine, start))
                dk, dv = pair(c, k, v, logs[c], keep)
                acc[:, :HD] = dk
                acc[:, HD:] = dv
            else:
                acc[...] = jnp.zeros_like(acc)

                @pl.when(other < t)
                def _():
                    dk, dv = pair(c, k, v, far[c], late)
                    acc[:, :HD] = dk
                    acc[:, HD:] = dv

            dk, dv = acc[:, :HD], acc[:, HD:]
            for later in range(c + 1, 4):
                a, b = pair(later, k, v, far[later], late)
                dk += a
                dv += b
            result.append((dk * SCALE, dv))
        return result

    sent = []

    def send(n, source, slot, device):
        copy = rcopy(source, slot, kv_send.at[n], kv_recv.at[n], device)
        copy.start()
        sent.append(copy)

    def put(ref, values):
        for i, (dk, dv) in enumerate(values):
            ref[i, :, :HD] = dk.astype(BF)
            ref[i, :, HD:] = dv.astype(BF)

    rows = [lax.rem(y + dy, 4) for dy in TURNS]
    for j in range(3):
        for i, column in enumerate((x, 1 - x)):
            put(give_b.at[j, i], keys_of(column * 4 + rows[j], (2, 3)))
        send(j, give_b.at[j], take_b.at[j], along[j])
    for k in RING:
        down_sum.pass_on(k)
    for j, row in enumerate(rows + [y]):
        put(give_a.at[j], keys_of((1 - x) * 4 + row, (0, 1)))
        send(3 + j, give_a.at[j], take_a.at[j], near)
    dwo_out.relay()
    dwd_out.relay()
    res[h] = (hidden[...] + down_sum.total()).astype(BF)
    res_out = rcopy(res.at[h], res.at[h], res_send.at[0], res_recv.at[0], {"head": 1 - h})
    res_out.start()
    dwo_sum[...] = dwo_out.total().astype(BF)
    rings += swap_ring(dwo_sum, dwo_ring, z, r_send.at[0], r_recv.at[0])
    dwo_ring[z] = dwo_sum[z]
    dwd_sum[...] = dwd_out.total().astype(BF)
    rings += swap_ring(dwd_sum, dwd_ring, z, r_send.at[2], r_recv.at[2])
    dwd_ring[z] = dwd_sum[z]

    def add(values, *others):
        result = []
        for i, (dk, dv) in enumerate(values):
            for other in others:
                both = other[i].astype(F32)
                dk += both[:, :HD]
                dv += both[:, HD:]
            result.append((dk, dv))
        return result

    for j in range(3):
        values = keys_of(x * 4 + rows[j], (0, 1))
        sent[3 + j].wait_recv()
        put(give_c.at[j], add(values, take_a.at[j]))
        send(7 + j, give_c.at[j], take_c.at[j], along[j])
    values = keys_of((1 - x) * 4 + y, (2, 3))
    for j in range(3):
        sent[j].wait_recv()
    put(give_d, add(values, *(take_b.at[j, 1] for j in range(3))))
    send(10, give_d, take_d, near)
    low = keys_of(t, (0, 1), True)
    high = keys_of(t, (2, 3), True)
    for c in range(4):
        dq[c] = (dq_t[c] * SCALE).T
    sent[6].wait_recv()
    low = add(low, take_a.at[3])
    high = add(high, *(take_b.at[j, 0] for j in range(3)))
    for j in range(3):
        sent[7 + j].wait_recv()
    sent[10].wait_recv()
    low = add(low, *(take_c.at[j] for j in range(3)))
    high = add(high, take_d)
    for c, (dk, dv) in enumerate(low + high):
        dkv[c, :, :HD] = dk
        dkv[c, :, HD:] = dv
    for copy in rings:
        copy.wait()
    res_out.wait()
    for copy in sent:
        copy.wait_send()
    dwo_out.finish()
    dwd_out.finish()
    down_sum.finish()


def finish_part(
    dq, dkv, pre, normed, w1, gains, qgain, kgain, cosine, sine, tok, grad_hidden, dwo, dwg, dwd,
    gain_two, ig, ring1, twin1, two, twg, twd, terms_out,
    dpre, dw1, dw1_sum, term, term_plane, term_ring, *scratch,
):
    sums = scratch[0:8]
    dw1_buf = scratch[8:11]
    plane_send, plane_recv, ring_send, ring_recv, twin_send, twin_recv, ig_send, ig_recv, term_send, term_recv = scratch[11:]
    z, x, y, h = place()
    t = x * 4 + y
    twin = {"rep": 1 - lax.axis_index("rep")}
    others = [{"head": h_, **device} for device in plane_devices(x, y) for h_ in (h, 1 - h)]
    rings = [{**ring_peer(z, k), **r} for k in RING for r in ({}, twin)]

    twins = []
    for i, (source, other) in enumerate(((dwo, two), (dwg, twg), (dwd, twd))):
        copy = rcopy(source, other, twin_send.at[i], twin_recv.at[i], twin)
        copy.start()
        twins.append(copy)
    c_, s_ = cosine[...], sine[...]
    heads = []
    for i in range(2):
        heads.append(jnp.concatenate([dq[c, i * CH : (i + 1) * CH, :] for c in range(4)], axis=0))
    heads.append(dkv[...].reshape(4 * CH, 2 * HD)[:, :HD])
    terms = []
    for i, dy in enumerate(heads):
        gy = turn(dy, c_, -s_)
        v = pre[:, i * HD : (i + 1) * HD]
        rate = rms_rate(v)
        vr = v * rate
        terms.append(jnp.sum(gy * vr, axis=0, keepdims=True))
        gg = gy * (qgain if i < 2 else kgain)[...]
        out = rate * (gg - vr * jnp.mean(gg * vr, axis=-1, keepdims=True))
        dpre[:, i * HD : (i + 1) * HD] = out.astype(BF)
    dpre[:, 3 * HD :] = dkv[...].reshape(4 * CH, 2 * HD)[:, HD:].astype(BF)
    term[...] = jnp.zeros_like(term)
    term[16:17] = terms[0] + terms[1]
    term[17:18] = terms[2]
    dw1[...] = tn(normed[...], dpre[...]).astype(BF).reshape(4, 8, 32, W1C)
    dw1_out = PlaneReduce(dw1, *dw1_buf, x, y, plane_send, plane_recv)
    norm_sum = Reduce(*sums[:4], z, h, sums[4:])
    for k in (1, 3, 2, 0):
        chunk = lax.rem(z + k, 4)
        norm_sum.give(k, nt(dpre[pl.ds(pl.multiple_of(chunk * CH, CH), CH), :], w1[...]))
    for k in RING:
        norm_sum.pass_on(k)
    dw1_out.relay()
    gy = norm_sum.total()
    v = tok[h].astype(F32)
    rate = rms_rate(v)
    vr = v * rate
    own_term = jnp.sum(gy * vr, axis=0, keepdims=True)
    for i in range(8):
        term[i : i + 1] = own_term[:, i * HD : (i + 1) * HD]
        term[8 + i : 9 + i] = gain_two[:, i * HD : (i + 1) * HD]
    term_copies = []
    for n, device in enumerate(group_devices(z, h)[:1] + others):
        copy = rcopy(term, term_plane.at[n], term_send.at[n], term_recv.at[n], device)
        copy.start()
        term_copies.append(copy)
    gg = gy * joined_gain(gains, 0)
    gv = rate * (gg - vr * jnp.mean(gg * vr, axis=-1, keepdims=True))
    ig[h] = (grad_hidden[...] + gv).astype(BF)
    ig_out = rcopy(ig.at[h], ig.at[h], ig_send.at[0], ig_recv.at[0], {"head": 1 - h})
    ig_out.start()
    dw1_sum[...] = dw1_out.total().astype(BF)
    copies1 = swap_ring(dw1_sum, ring1, z, ring_send, ring_recv)
    for k in range(4):
        copy = rcopy(
            dw1_sum.at[lax.rem(z + k, 4)],
            twin1.at[z],
            twin_send.at[3 + k],
            twin_recv.at[3 + k],
            {**ring_peer(z, k), **twin},
        )
        copy.start()
        copies1.append(copy)
    ring1[z] = dw1_sum[z]
    for copy in term_copies:
        copy.wait()
    for n in range(15):
        term[...] += term_plane[n]
    term_copies = []
    for n, device in enumerate(rings + [twin]):
        copy = rcopy(term, term_ring.at[n], term_send.at[15 + n], term_recv.at[15 + n], device)
        copy.start()
        term_copies.append(copy)
    for copy in twins:
        copy.wait()
    for copy in term_copies:
        copy.wait()
    own_term = term[...]
    for n in range(7):
        own_term += term_ring[n]
    terms_out[...] = own_term
    for copy in copies1:
        copy.wait()
    ig_out.wait()
    dw1_out.finish()
    norm_sum.finish()


def backward_kernel(*refs):
    z, x, y, h = place()
    twin = {"rep": 1 - lax.axis_index("rep")}
    others = [{"head": h_, **device} for device in plane_devices(x, y) for h_ in (h, 1 - h)]
    rings = [{**ring_peer(z, k), **r} for k in RING for r in ({}, twin)]
    greet(group_devices(z, h)[:1] + others + rings + [twin, beside(x, y)[2]])
    dq, dkv = refs[33:35]
    count = 35 + len(back_scratch())
    attend_back_part(*refs[:11], dq, dkv, *refs[22:26], *refs[35:count])
    finish_part(dq, dkv, *refs[11:21], *refs[22:25], refs[21], *refs[26:33], *refs[count:])


def back_scratch():
    return (
        [
            pltpu.VMEM((4, HD, 2 * CH), F32),
            pltpu.VMEM((4, 1, 2 * CH), F32),
            pltpu.VMEM((4, 1, 2 * CH), F32),
            pltpu.VMEM((CH, 2 * HD), F32),
            pltpu.VMEM((3, 2, 2, CH, 2 * HD), BF),
            pltpu.VMEM((3, 2, 2, CH, 2 * HD), BF),
            pltpu.VMEM((4, 2, CH, 2 * HD), BF),
            pltpu.VMEM((4, 2, CH, 2 * HD), BF),
            pltpu.VMEM((3, 2, CH, 2 * HD), BF),
            pltpu.VMEM((3, 2, CH, 2 * HD), BF),
            pltpu.VMEM((2, CH, 2 * HD), BF),
            pltpu.VMEM((2, CH, 2 * HD), BF),
            pltpu.VMEM((4, 32, 256), BF),
            pltpu.VMEM((4, 32, 384), BF),
        ]
        + plane_scratch(256)
        + plane_scratch(384)
        + reduce_scratch(False)
        + [
            pltpu.SemaphoreType.DMA((11,)),
            pltpu.SemaphoreType.DMA((11,)),
            pltpu.SemaphoreType.DMA((2, 11)),
            pltpu.SemaphoreType.DMA((2, 11)),
            pltpu.SemaphoreType.DMA((3, 4)),
            pltpu.SemaphoreType.DMA((3, 4)),
            pltpu.SemaphoreType.DMA((1,)),
            pltpu.SemaphoreType.DMA((1,)),
        ]
    )


def finish_scratch():
    return (
        [
            pltpu.VMEM((4 * CH, W1C), BF),
            pltpu.VMEM((4, 8, 32, W1C), BF),
            pltpu.VMEM((4, 32, W1C), BF),
            pltpu.VMEM((24, HD), F32),
            pltpu.VMEM((15, 24, HD), F32),
            pltpu.VMEM((7, 24, HD), F32),
        ]
        + reduce_scratch()
        + plane_scratch(W1C)
        + [
            pltpu.SemaphoreType.DMA((11,)),
            pltpu.SemaphoreType.DMA((11,)),
            pltpu.SemaphoreType.DMA((4,)),
            pltpu.SemaphoreType.DMA((4,)),
            pltpu.SemaphoreType.DMA((7,)),
            pltpu.SemaphoreType.DMA((7,)),
            pltpu.SemaphoreType.DMA((1,)),
            pltpu.SemaphoreType.DMA((1,)),
            pltpu.SemaphoreType.DMA((22,)),
            pltpu.SemaphoreType.DMA((22,)),
        ]
    )


def backward(*arrays):
    vmem = pl.BlockSpec(memory_space=pltpu.VMEM)
    smem = pl.BlockSpec(memory_space=pltpu.SMEM)
    return pl.pallas_call(
        backward_kernel,
        out_shape=(
            jax.ShapeDtypeStruct((4, 32, 256), BF),
            jax.ShapeDtypeStruct((4, 32, 768), BF),
            jax.ShapeDtypeStruct((4, 32, 384), BF),
            jax.ShapeDtypeStruct((2, HALF, D), BF),
            jax.ShapeDtypeStruct((2, HALF, D), BF),
            jax.ShapeDtypeStruct((4, 32, W1C), BF),
            jax.ShapeDtypeStruct((4, 32, W1C), BF),
            jax.ShapeDtypeStruct((4, 32, 256), BF),
            jax.ShapeDtypeStruct((4, 32, 768), BF),
            jax.ShapeDtypeStruct((4, 32, 384), BF),
            jax.ShapeDtypeStruct((24, HD), F32),
        ),
        in_specs=[vmem] * 10 + [smem] + [vmem] * 11,
        out_specs=(vmem,) * 11,
        scratch_shapes=[
            pltpu.VMEM((4, 2 * CH, HD), F32),
            pltpu.VMEM((4, CH, 2 * HD), F32),
        ]
        + back_scratch()
        + finish_scratch(),
        compiler_params=pltpu.CompilerParams(
            collective_id=3, has_side_effects=True, vmem_limit_bytes=VMEM_LIMIT
        ),
        name="backward",
    )(*arrays)


def arrange_kernel(
    res, ig, ring1, twin1, dwo, two, dwg, twg, dwd, twd, terms,
    res_out, ig_out, gq, gk, gv, g_out, g_gate, g_up, g_down, g_attn, g_mlp, g_qgain, g_kgain,
):
    z, x, y, _ = place()
    c = z * 8 + x * 4 + y
    res_out[...] = res[...]
    ig_out[...] = ig[...]
    for i in range(4):
        both = ring1[i].astype(F32) + twin1[i].astype(F32)
        gq[:, i * 256 : (i + 1) * 256] = both[:, :256]
        gk[:, i * 128 : (i + 1) * 128] = both[:, 256:384]
        gv[:, i * 128 : (i + 1) * 128] = both[:, 384:]
        both = dwg[i].astype(F32) + twg[i].astype(F32)
        g_gate[:, i * 384 : (i + 1) * 384] = both[:, :384]
        g_up[:, i * 384 : (i + 1) * 384] = both[:, 384:]
        g_out[:, i * 256 : (i + 1) * 256] = dwo[i].astype(F32) + two[i].astype(F32)
        g_down[:, i * 384 : (i + 1) * 384] = dwd[i].astype(F32) + twd[i].astype(F32)
    g_qgain[...] = terms[16:17]
    g_kgain[...] = terms[17:18]
    for out, first in ((g_attn, 0), (g_mlp, 8)):
        value = jnp.zeros((1, 32), F32)
        for n in range(32):
            piece = terms[first + n // 4 : first + n // 4 + 1, (n % 4) * 32 : (n % 4 + 1) * 32]
            value += jnp.where(c == n, piece, 0.0)
        out[...] = value


def arrange(*arrays):
    vmem = pl.BlockSpec(memory_space=pltpu.VMEM)
    return pl.pallas_call(
        arrange_kernel,
        out_shape=(
            jax.ShapeDtypeStruct((2, HALF, D), BF),
            jax.ShapeDtypeStruct((2, HALF, D), BF),
            jax.ShapeDtypeStruct((32, 1024), F32),
            jax.ShapeDtypeStruct((32, 512), F32),
            jax.ShapeDtypeStruct((32, 512), F32),
            jax.ShapeDtypeStruct((32, 1024), F32),
            jax.ShapeDtypeStruct((32, 1536), F32),
            jax.ShapeDtypeStruct((32, 1536), F32),
            jax.ShapeDtypeStruct((32, 1536), F32),
            jax.ShapeDtypeStruct((1, 32), F32),
            jax.ShapeDtypeStruct((1, 32), F32),
            jax.ShapeDtypeStruct((1, HD), F32),
            jax.ShapeDtypeStruct((1, HD), F32),
        ),
        in_specs=[vmem] * 11,
        out_specs=(vmem,) * 13,
        compiler_params=pltpu.CompilerParams(vmem_limit_bytes=VMEM_LIMIT),
        name="arrange",
    )(*arrays)


def on_device(
    tokens, segments, positions, cotangent, query_weight, key_weight, value_weight, out_weight,
    attn_gain, query_gain, key_gain, gate_weight, up_weight, down_weight, mlp_gain,
):
    half = HD // 2
    inverse = ROPE_BASE ** (-np.arange(half) / half)
    inverse = jnp.asarray(np.concatenate([inverse, inverse])[None], F32)
    tok = tokens.reshape(2, HALF, D)
    qgain, kgain = query_gain[None], key_gain[None]
    (
        w1_all, gains_all, start, cosine, sine, q, pre, normed, att, out_t, logs, kv_all, cot_all, wo, wg, wd,
    ) = forward(
        tok, query_weight, key_weight, value_weight, attn_gain[None], mlp_gain[None], segments, positions, inverse,
        qgain, kgain, cotangent.reshape(2, HALF, D), out_weight.T, gate_weight, up_weight, down_weight.T,
    )
    w1_all = w1_all.reshape(D, W1C)
    hidden, down_parts, grad_hidden, grad_att, dwo, dwg, dwd, gain_two_term = middle(
        att, wo, wg, wd, gains_all, tok, cot_all
    )
    dwo, dwg, dwd, result, input_grad, ring1, twin1, two, twg, twd, terms = backward(
        q, kv_all, grad_att, out_t, logs, dwo.reshape(4, 8, 32, 256), dwg, dwd, hidden, down_parts, start,
        pre, normed, w1_all, gains_all, qgain, kgain, cosine, sine, tok, grad_hidden, gain_two_term,
    )
    result, input_grad, gq, gk, gv, g_out, g_gate, g_up, g_down, g_attn, g_mlp, g_qgain, g_kgain = arrange(
        result, input_grad, ring1, twin1, dwo, two, dwg, twg, dwd, twd, terms
    )
    return (
        result.reshape(1, CH, D),
        input_grad.reshape(1, CH, D),
        gq,
        gk,
        gv,
        g_out.T,
        g_attn[0],
        g_qgain[0],
        g_kgain[0],
        g_gate,
        g_up,
        g_down.T,
        g_mlp[0],
    )


def solution(mesh):
    torus = Mesh(
        mesh.devices.reshape(mesh.shape["rep"], 4, 2, 4, mesh.shape["head"]),
        ("rep", "ctx_0", "ctx_1", "ctx_2", "head"),
    )
    return jax.shard_map(
        on_device,
        mesh=torus,
        in_specs=(
            P("rep", CTX, None),
            P("rep", CTX),
            P("rep", CTX),
            P("rep", CTX, None),
            P(CTX, "head"),
            P(CTX, "head"),
            P(CTX, "head"),
            P("head", CTX),
            P(CTX),
            P(),
            P(),
            P(CTX, "head"),
            P(CTX, "head"),
            P("head", CTX),
            P(CTX),
        ),
        out_specs=(
            P("rep", CTX, None),
            P("rep", CTX, None),
            P(CTX, "head"),
            P(CTX, "head"),
            P(CTX, "head"),
            P("head", CTX),
            P(CTX),
            P(),
            P(),
            P(CTX, "head"),
            P(CTX, "head"),
            P("head", CTX),
            P(CTX),
        ),
        check_vma=False,
    )
```
